32 devices in a mesh: grp: 2 (over x), cross: 16 (over z, y, core).
Axes of the slice: x: 2, y: 2, z: 4, core: 2. Of those that a mesh axis runs over, the one named last changes fastest.
Arguments:
- state: float32 [3, 512, 2048], P(None, 'grp', 'cross'), parts along dimension 1, may hold values from -4 to 4, as said below
- log_mu: float32 [512, 2048], P('grp', 'cross'), parts along dimension 0, may hold values from -2.3 to -0.7
- log_xi: float32 [512, 2048], P('grp', 'cross'), parts along dimension 0, may hold values from 0 to 1.6
- dir_mu: float32 [512, 2048], P('grp', 'cross'), parts along dimension 0, may hold values from -4 to 4
- dir_xi: float32 [512, 2048], P('grp', 'cross'), parts along dimension 0, may hold values from -4 to 4
- wet: int32 [512, 2048], P('grp', 'cross'), parts along dimension 0, may hold values from 0 to 1, as said below
- observed: int32 [512, 2048], P('grp', 'cross'), parts along dimension 0, may hold values from 0 to 1, as said below
- terrain: int32 [512, 2048], P('grp', 'cross'), parts along dimension 0, may hold values from 0 to 7
- class_weight: float32 [8], replicated, may hold values from 0.01 to 0.1
Outputs:
- hvp_mu: float32 [512, 2048], P('grp', 'cross'), parts along dimension 0
- hvp_xi: float32 [512, 2048], P('grp', 'cross'), parts along dimension 0
The draws below stay inside these ranges and needn't reach their ends.
There are 2 independent parts, one for each index of `grp`. The reference program is written for one: setup_inputs(seed, part) draws one part's arguments, and reference() takes and returns one part's arrays. A program takes and returns all parts, laid end to end along the dimension named above; an argument that names none is the same for every part. Nothing has to cross between parts.
Inputs may be any that keep to these rules, and one draw needn't show every extreme that they name: state[0] holds heights, never negative; state[1] and state[2] hold discharges. 1 marks a cell that was wet in the checkpoint. 1 marks a pixel with an observed deposit depth.
All inputs are finite; a program needn't handle non-finite values.
Results may differ from the reference program's by a relative error of at most 0.00002.
Values sent between devices are 32-bit elements; how exact they have to be, the bound alone decides.
No kernel may reach another device: no remote copies, remote signals or barrier semaphores. Data moves between devices by JAX's collectives and lax.ppermute only.
A program may use at most 64 MiB of HBM per device.

```python
import math
import jax
import jax.numpy as jnp

ROWS = 256
CLASSES = 8
NC = 2048


def wet_cells(key):
    chance = jax.random.randint(jax.random.fold_in(key, 101), (ROWS, NC), 0, 100)
    return (chance < 88).astype(jnp.int32)


def draw_wet(key, part):
    return wet_cells(key)


def draw_state(key, part):
    wet_mask = wet_cells(key).astype(jnp.float32)
    key = jax.random.fold_in(key, 7)
    subkeys = jax.random.split(key, 6)
    column = jnp.arange(NC, dtype=jnp.float32)
    center = jax.random.randint(subkeys[5], (), 0, NC).astype(jnp.float32)
    reach = max(NC / 8.0, 2.0)
    column_ramp = 1.0 + 2.0 * jnp.maximum(0.0, 1.0 - jnp.abs(column - center) / reach)
    wet_height = jnp.exp(jax.random.uniform(subkeys[0], (ROWS, NC), minval=-1.386, maxval=-0.288)) * column_ramp[None, :]
    dry_height = jax.random.uniform(subkeys[1], (ROWS, NC), minval=0.0, maxval=0.08)
    vel_down = 0.5 * jax.random.truncated_normal(subkeys[2], -3.0, 3.0, (ROWS, NC))
    vel_across = 0.3 * jax.random.truncated_normal(subkeys[3], -3.0, 3.0, (ROWS, NC))
    height = wet_mask * wet_height + (1.0 - wet_mask) * dry_height
    return jnp.stack([height, height * vel_down, height * vel_across]).astype(jnp.float32)


def draw_observed(key, part):
    key = jax.random.fold_in(key, 11)
    column = jnp.arange(NC, dtype=jnp.int32)
    cutoff = 20 + 50 * column // max(NC - 1, 1)
    chance = jax.random.randint(key, (ROWS, NC), 0, 100)
    return (chance < cutoff[None, :]).astype(jnp.int32)


def with_ends(array, key, least, high):
    longest = array.shape.index(max(array.shape))
    spots = []
    for shift in (0, 1):
        where = [jax.random.randint(jax.random.fold_in(key, axis), (), 0, length) for axis, length in enumerate(array.shape)]
        where[longest] = (where[longest] + shift) % array.shape[longest]
        spots.append(tuple(where))
    return array.at[spots[0]].set(least).at[spots[1]].set(high)


def block_levels(key, extent, shards, low, largest):
    def one(dim, shards_of):
        draws = jax.random.uniform(jax.random.fold_in(jax.random.fold_in(key, 6), dim), (shards_of,), jnp.float32, low / len(shards), largest / len(shards))
        return jnp.repeat(jnp.exp(draws), extent[dim] // shards_of).reshape((-1,) + (1,) * (len(extent) - dim - 1))

    gain = one(*shards[0])
    for cut in shards[1:]:
        gain = gain * one(*cut)
    return gain


def noise(own_key, shape, width, most, cuts=(), held_as=jnp.bfloat16):
    factor_of = block_levels(own_key, shape, cuts, -0.22, 0.18) if cuts else 1.0
    entries = jax.random.normal(own_key, shape, jnp.float32) * width * factor_of
    return jnp.minimum(jnp.maximum(entries, -most), most).astype(held_as)


def setup_inputs(seed: int = 0, part: int = 0) -> dict:
    keys = jax.random.split(jax.random.key(seed), 10)
    part_keys = jax.random.split(jax.random.fold_in(keys[9], part), 10)
    return {
        "state": draw_state(jax.random.fold_in(jax.random.fold_in(keys[9], part), 71), part),
        "log_mu": jnp.clip(-2.3 + 1.59999996 * jax.random.uniform(part_keys[1], (ROWS, NC), jnp.float32) ** block_levels(part_keys[1], (ROWS, NC), ((1, 16),), -0.2, 0.2), -2.3, -0.7),
        "log_xi": jnp.clip(1.6 * jax.random.uniform(part_keys[2], (ROWS, NC), jnp.float32) ** block_levels(part_keys[2], (ROWS, NC), ((1, 16),), -0.2, 0.2), 0.0, 1.6),
        "dir_mu": noise(part_keys[3], (ROWS, NC), 1.0, 4.0, ((1, 16),), jnp.float32),
        "dir_xi": noise(part_keys[4], (ROWS, NC), 1.0, 4.0, ((1, 16),), jnp.float32),
        "wet": draw_wet(jax.random.fold_in(jax.random.fold_in(keys[9], part), 71), part),
        "observed": draw_observed(jax.random.fold_in(jax.random.fold_in(keys[9], part), 71), part),
        "terrain": with_ends(jax.random.randint(part_keys[7], (ROWS, NC), 0, CLASSES), jax.random.fold_in(part_keys[7], 1), 0, CLASSES - 1).astype(jnp.int32),
        "class_weight": jnp.clip(jnp.exp(jax.random.uniform(keys[8], (CLASSES,), jnp.float32, math.log(0.01), math.log(0.1))), 0.01, 0.1),
    }


COS_SLOPE = 0.8
SIN_SLOPE = 0.6
DEPTH_FLOOR = 0.05
SPEED_EPS = 0.01
COURANT = 0.2
DATA_WEIGHT = 100000.0

def section_rate(padded, log_mu, log_xi, wet_frac, wave_speed):
    full_rows = jnp.pad(padded, ((0, 0), (1, 1), (0, 0)))
    height = full_rows[0]
    flow_down = full_rows[1]
    flow_across = full_rows[2]
    safe_height = jnp.maximum(height, DEPTH_FLOOR)
    vel_down = flow_down / safe_height
    vel_across = flow_across / safe_height
    pressure = 0.5 * COS_SLOPE * height * height
    flux_x = jnp.stack([flow_down, flow_down * vel_down + pressure, flow_down * vel_across])
    flux_y = jnp.stack([flow_across, flow_across * vel_down, flow_across * vel_across + pressure])
    face_down = 0.5 * (flux_x[:, :-1, 1:-1] + flux_x[:, 1:, 1:-1]) - 0.5 * wave_speed * (full_rows[:, 1:, 1:-1] - full_rows[:, :-1, 1:-1])
    face_across = 0.5 * (flux_y[:, 1:-1, :-1] + flux_y[:, 1:-1, 1:]) - 0.5 * wave_speed * (full_rows[:, 1:-1, 1:] - full_rows[:, 1:-1, :-1])
    diverge = face_down[:, 1:] - face_down[:, :-1] + face_across[:, :, 1:] - face_across[:, :, :-1]
    inner_height = height[1:-1, 1:-1]
    inner_down = vel_down[1:-1, 1:-1]
    inner_across = vel_across[1:-1, 1:-1]
    speed_norm = jnp.sqrt(inner_down * inner_down + inner_across * inner_across + SPEED_EPS)
    resistance = wet_frac * (jnp.exp(log_mu) * COS_SLOPE * inner_height + speed_norm * speed_norm * jnp.exp(-log_xi)) / speed_norm
    source_term = jnp.stack([jnp.zeros_like(inner_height), SIN_SLOPE * inner_height - resistance * inner_down, -resistance * inner_across])
    return source_term - diverge

def pad_columns(field):
    return jnp.pad(field, ((0, 0), (0, 0), (1, 1)))

def heun_step(state, log_mu, log_xi, wet_frac, wave_speed, time_step):
    first_section = state + time_step * section_rate(pad_columns(state), log_mu, log_xi, wet_frac, wave_speed)
    return 0.5 * (state + first_section + time_step * section_rate(pad_columns(first_section), log_mu, log_xi, wet_frac, wave_speed))

def fastest(state):
    safe_height = jnp.maximum(state[0], DEPTH_FLOOR)
    vel_down = state[1] / safe_height
    vel_across = state[2] / safe_height
    return jnp.max(jnp.sqrt(vel_down * vel_down + vel_across * vel_across) + jnp.sqrt(COS_SLOPE * jnp.maximum(state[0], 0.0)))

def laplace(field):
    padded = jnp.pad(field, ((1, 1), (1, 1)))
    return 4.0 * field - padded[:-2, 1:-1] - padded[2:, 1:-1] - padded[1:-1, :-2] - padded[1:-1, 2:]

def reference(state, log_mu, log_xi, dir_mu, dir_xi, wet, observed, terrain, class_weight):
    wet_frac = wet.astype(jnp.float32)
    speed_start = fastest(state)
    step_start = COURANT / speed_start

    def first_map(state_in, mu_in, xi_in):
        return heun_step(state_in, mu_in, xi_in, wet_frac, speed_start, step_start)
    state_mid, tangent_mid = jax.jvp(first_map, (state, log_mu, log_xi), (jnp.zeros_like(state), dir_mu, dir_xi))
    speed_next = fastest(state_mid)
    step_next = COURANT / speed_next

    def second_map(state_in, mu_in, xi_in):
        return heun_step(state_in, mu_in, xi_in, wet_frac, speed_next, step_next)
    state_end, tangent_end = jax.jvp(second_map, (state_mid, log_mu, log_xi), (tangent_mid, dir_mu, dir_xi))
    observed_count = jnp.sum(observed).astype(jnp.float32)
    weight = DATA_WEIGHT * (ROWS * NC) / observed_count
    blank = jnp.zeros_like(tangent_end[0])
    seed_cot = jnp.stack([weight * observed.astype(jnp.float32) * tangent_end[0], blank, blank])
    unused_end, pull_second = jax.vjp(second_map, state_mid, log_mu, log_xi)
    cot_mid, mu_late, xi_late = pull_second(seed_cot)

    def params_only(mu_in, xi_in):
        return first_map(state, mu_in, xi_in)
    unused_mid, pull_first = jax.vjp(params_only, log_mu, log_xi)
    mu_early, xi_early = pull_first(cot_mid)
    reg_weight = jnp.zeros_like(dir_mu)
    for class_id in range(CLASSES):
        reg_weight = reg_weight + jnp.where(terrain == class_id, class_weight[class_id], 0.0)
    reg_mu = laplace(reg_weight * laplace(dir_mu))
    reg_xi = laplace(reg_weight * laplace(dir_xi))
    return (mu_early + mu_late + reg_mu, xi_early + xi_late + reg_xi)
```

```python
import jax
import jax.numpy as jnp
from jax import lax
from jax.sharding import PartitionSpec as P

COS_SLOPE = 0.8
SIN_SLOPE = 0.6
DEPTH_FLOOR = 0.05
SPEED_EPS = 0.01
COURANT = 0.2
DATA_WEIGHT = 100000.0


def padded_2(cells, sides, width):
    for axis, dim in sides:
        count = lax.axis_size(axis)
        ends = count - 1
        head = lax.slice_in_dim(cells, 0, width, axis=dim)
        tail = lax.slice_in_dim(cells, cells.shape[dim] - width, cells.shape[dim], axis=dim)
        cells = jnp.concatenate(
            [
                lax.ppermute(tail, axis, [(i, (i + 1) % count) for i in range(ends)]),
                cells,
                lax.ppermute(head, axis, [((i + 1) % count, i) for i in range(ends)]),
            ],
            axis=dim,
        )
    return cells


def over_cross(value, combine):
    count = lax.axis_size("cross")
    step = 1
    while step < count:
        other = lax.ppermute(value, "cross", [(i, i ^ step) for i in range(count)])
        value = combine(value, other)
        step *= 2
    return value


def max_and_sum(a, b):
    return jnp.stack([jnp.maximum(a[0], b[0]), a[1] + b[1]])


def shifted(shard, axis, by):
    count = lax.axis_size(axis)
    pairs = [(i, i + by) for i in range(count) if 0 <= i + by < count]
    return lax.ppermute(shard, axis, pairs)


def section_rate(padded, log_mu, log_xi, wet_frac, wave_speed):
    full_rows = jnp.pad(padded, ((0, 0), (1, 1), (0, 0)))
    height = full_rows[0]
    flow_down = full_rows[1]
    flow_across = full_rows[2]
    safe_height = jnp.maximum(height, DEPTH_FLOOR)
    vel_down = flow_down / safe_height
    vel_across = flow_across / safe_height
    pressure = 0.5 * COS_SLOPE * height * height
    flux_x = jnp.stack([flow_down, flow_down * vel_down + pressure, flow_down * vel_across])
    flux_y = jnp.stack([flow_across, flow_across * vel_down, flow_across * vel_across + pressure])
    face_down = 0.5 * (flux_x[:, :-1, 1:-1] + flux_x[:, 1:, 1:-1]) - 0.5 * wave_speed * (
        full_rows[:, 1:, 1:-1] - full_rows[:, :-1, 1:-1]
    )
    face_across = 0.5 * (flux_y[:, 1:-1, :-1] + flux_y[:, 1:-1, 1:]) - 0.5 * wave_speed * (
        full_rows[:, 1:-1, 1:] - full_rows[:, 1:-1, :-1]
    )
    diverge = face_down[:, 1:] - face_down[:, :-1] + face_across[:, :, 1:] - face_across[:, :, :-1]
    inner_height = height[1:-1, 1:-1]
    inner_down = vel_down[1:-1, 1:-1]
    inner_across = vel_across[1:-1, 1:-1]
    speed_norm = jnp.sqrt(inner_down * inner_down + inner_across * inner_across + SPEED_EPS)
    resistance = (
        wet_frac
        * (jnp.exp(log_mu) * COS_SLOPE * inner_height + speed_norm * speed_norm * jnp.exp(-log_xi))
        / speed_norm
    )
    source_term = jnp.stack(
        [
            jnp.zeros_like(inner_height),
            SIN_SLOPE * inner_height - resistance * inner_down,
            -resistance * inner_across,
        ]
    )
    return source_term - diverge


def fastest_local(state):
    safe_height = jnp.maximum(state[0], DEPTH_FLOOR)
    vel_down = state[1] / safe_height
    vel_across = state[2] / safe_height
    return jnp.max(
        jnp.sqrt(vel_down * vel_down + vel_across * vel_across)
        + jnp.sqrt(COS_SLOPE * jnp.maximum(state[0], 0.0))
    )


def laplace_cols(padded):
    full_rows = jnp.pad(padded, ((0, 0), (1, 1), (0, 0)))
    center = full_rows[:, 1:-1, 1:-1]
    return (
        4.0 * center
        - full_rows[:, :-2, 1:-1]
        - full_rows[:, 2:, 1:-1]
        - full_rows[:, 1:-1, :-2]
        - full_rows[:, 1:-1, 2:]
    )


def pair_halo(primal, tangent):
    both_rims = padded_2(jnp.concatenate([primal, tangent]), (("cross", 2),), 1)
    return (both_rims[:3], both_rims[3:])


def return_ghosts(cot_padded):
    from_left = shifted(cot_padded[:, :, -1], "cross", 1)
    from_right = shifted(cot_padded[:, :, 0], "cross", -1)
    interior = cot_padded[:, :, 1:-1]
    interior = interior.at[:, :, 0].add(from_left)
    interior = interior.at[:, :, -1].add(from_right)
    return interior


def local(state, log_mu, log_xi, dir_mu, dir_xi, wet, observed, terrain, class_weight):
    wet_frac = wet.astype(jnp.float32)
    row_count = state.shape[1]
    col_count = state.shape[2]
    devices = lax.axis_size("cross")
    local_fast = fastest_local(state)
    local_count = jnp.sum(observed).astype(jnp.float32)
    both = over_cross(jnp.stack([jnp.full((128,), local_fast), jnp.full((128,), local_count)]), max_and_sum)
    speed_start = both[0, 0]
    observed_count = both[1, 0]
    step_start = COURANT / speed_start

    def advance(state_now, tangent_now, wave, time_step, opening):
        if opening:
            pad_first = padded_2(state_now, (("cross", 2),), 1)
            tangent_first = jnp.zeros_like(pad_first)
        else:
            pad_first, tangent_first = pair_halo(state_now, tangent_now)

        def rate_here(padded, mu_in, xi_in):
            return section_rate(padded, mu_in, xi_in, wet_frac, wave)

        rate_first, slope_first = jax.jvp(
            rate_here, (pad_first, log_mu, log_xi), (tangent_first, dir_mu, dir_xi)
        )
        first_section = state_now + time_step * rate_first
        first_tangent = tangent_now + time_step * slope_first
        pad_second, tangent_second = pair_halo(first_section, first_tangent)
        rate_second, slope_second = jax.jvp(
            rate_here, (pad_second, log_mu, log_xi), (tangent_second, dir_mu, dir_xi)
        )
        next_state = 0.5 * (state_now + first_section + time_step * rate_second)
        next_tangent = 0.5 * (tangent_now + first_tangent + time_step * slope_second)
        return (next_state, next_tangent, pad_first, pad_second)

    state_mid, tangent_mid, early_first, early_second = advance(
        state, jnp.zeros_like(state), speed_start, step_start, True
    )
    speed_next = over_cross(jnp.full((1, 128), fastest_local(state_mid)), jnp.maximum)[0, 0]
    step_next = COURANT / speed_next
    state_end, tangent_end, late_first, late_second = advance(
        state_mid, tangent_mid, speed_next, step_next, False
    )

    def step_back(cotangent, pad_first, pad_second, wave, time_step, carry_state):

        def rate_here(padded, mu_in, xi_in):
            return section_rate(padded, mu_in, xi_in, wet_frac, wave)

        unused_rate, pull_second = jax.vjp(rate_here, pad_second, log_mu, log_xi)
        cot_second, grad_mu, grad_xi = pull_second(0.5 * time_step * cotangent)
        cot_first = 0.5 * cotangent + return_ghosts(cot_second)
        if carry_state:
            unused_first, pull_first = jax.vjp(rate_here, pad_first, log_mu, log_xi)
            cot_pad, more_mu, more_xi = pull_first(time_step * cot_first)
            cot_state = 0.5 * cotangent + cot_first + return_ghosts(cot_pad)
        else:

            def params_only(mu_in, xi_in):
                return rate_here(pad_first, mu_in, xi_in)

            unused_first, pull_first = jax.vjp(params_only, log_mu, log_xi)
            more_mu, more_xi = pull_first(time_step * cot_first)
            cot_state = cot_first
        return (cot_state, grad_mu + more_mu, grad_xi + more_xi)

    weight = DATA_WEIGHT * (row_count * col_count * devices) / observed_count
    blank = jnp.zeros_like(tangent_end[0])
    seed_cot = jnp.stack([weight * observed.astype(jnp.float32) * tangent_end[0], blank, blank])
    cot_mid, mu_late, xi_late = step_back(
        seed_cot, late_first, late_second, speed_next, step_next, True
    )
    unused_cot, mu_early, xi_early = step_back(
        cot_mid, early_first, early_second, speed_start, step_start, False
    )
    reg_weight = jnp.zeros_like(dir_mu)
    for class_id in range(class_weight.shape[0]):
        reg_weight = reg_weight + jnp.where(terrain == class_id, class_weight[class_id], 0.0)
    dir_rim = padded_2(jnp.stack([dir_mu, dir_xi]), (("cross", 2),), 1)
    bent_field = laplace_cols(dir_rim) * reg_weight
    smoothed = laplace_cols(padded_2(bent_field, (("cross", 2),), 1))
    return (mu_early + mu_late + smoothed[0], xi_early + xi_late + smoothed[1])


def solution(mesh):
    return jax.shard_map(
        local,
        mesh=mesh,
        in_specs=(
            P(None, "grp", "cross"),
            P("grp", "cross"),
            P("grp", "cross"),
            P("grp", "cross"),
            P("grp", "cross"),
            P("grp", "cross"),
            P("grp", "cross"),
            P("grp", "cross"),
            P(),
        ),
        out_specs=(P("grp", "cross"), P("grp", "cross")),
        check_vma=False,
    )
```

```python
import jax
import jax.numpy as jnp
from jax import lax
from jax.sharding import PartitionSpec as P

COS_SLOPE = 0.8
SIN_SLOPE = 0.6
DEPTH_FLOOR = 0.05
SPEED_EPS = 0.01
COURANT = 0.2
DATA_WEIGHT = 100000.0


def padded_2(cells, sides, width):
    for axis, dim in sides:
        count = lax.axis_size(axis)
        ends = count - 1
        head = lax.slice_in_dim(cells, 0, width, axis=dim)
        tail = lax.slice_in_dim(cells, cells.shape[dim] - width, cells.shape[dim], axis=dim)
        cells = jnp.concatenate(
            [
                lax.ppermute(tail, axis, [(i, (i + 1) % count) for i in range(ends)]),
                cells,
                lax.ppermute(head, axis, [((i + 1) % count, i) for i in range(ends)]),
            ],
            axis=dim,
        )
    return cells


def over_cross(value):
    return lax.all_gather(value, "cross")


def shifted(shard, axis, by):
    count = lax.axis_size(axis)
    pairs = [(i, i + by) for i in range(count) if 0 <= i + by < count]
    return lax.ppermute(shard, axis, pairs)


def section_rate(padded, log_mu, log_xi, wet_frac, wave_speed):
    full_rows = jnp.pad(padded, ((0, 0), (1, 1), (0, 0)))
    height = full_rows[0]
    flow_down = full_rows[1]
    flow_across = full_rows[2]
    safe_height = jnp.maximum(height, DEPTH_FLOOR)
    vel_down = flow_down / safe_height
    vel_across = flow_across / safe_height
    pressure = 0.5 * COS_SLOPE * height * height
    flux_x = jnp.stack([flow_down, flow_down * vel_down + pressure, flow_down * vel_across])
    flux_y = jnp.stack([flow_across, flow_across * vel_down, flow_across * vel_across + pressure])
    face_down = 0.5 * (flux_x[:, :-1, 1:-1] + flux_x[:, 1:, 1:-1]) - 0.5 * wave_speed * (
        full_rows[:, 1:, 1:-1] - full_rows[:, :-1, 1:-1]
    )
    face_across = 0.5 * (flux_y[:, 1:-1, :-1] + flux_y[:, 1:-1, 1:]) - 0.5 * wave_speed * (
        full_rows[:, 1:-1, 1:] - full_rows[:, 1:-1, :-1]
    )
    diverge = face_down[:, 1:] - face_down[:, :-1] + face_across[:, :, 1:] - face_across[:, :, :-1]
    inner_height = height[1:-1, 1:-1]
    inner_down = vel_down[1:-1, 1:-1]
    inner_across = vel_across[1:-1, 1:-1]
    speed_norm = jnp.sqrt(inner_down * inner_down + inner_across * inner_across + SPEED_EPS)
    resistance = (
        wet_frac
        * (jnp.exp(log_mu) * COS_SLOPE * inner_height + speed_norm * speed_norm * jnp.exp(-log_xi))
        / speed_norm
    )
    source_term = jnp.stack(
        [
            jnp.zeros_like(inner_height),
            SIN_SLOPE * inner_height - resistance * inner_down,
            -resistance * inner_across,
        ]
    )
    return source_term - diverge


def fastest_local(state):
    safe_height = jnp.maximum(state[0], DEPTH_FLOOR)
    vel_down = state[1] / safe_height
    vel_across = state[2] / safe_height
    return jnp.max(
        jnp.sqrt(vel_down * vel_down + vel_across * vel_across)
        + jnp.sqrt(COS_SLOPE * jnp.maximum(state[0], 0.0))
    )


def laplace_cols(padded):
    full_rows = jnp.pad(padded, ((0, 0), (1, 1), (0, 0)))
    center = full_rows[:, 1:-1, 1:-1]
    return (
        4.0 * center
        - full_rows[:, :-2, 1:-1]
        - full_rows[:, 2:, 1:-1]
        - full_rows[:, 1:-1, :-2]
        - full_rows[:, 1:-1, 2:]
    )


def pair_halo(primal, tangent):
    both_rims = padded_2(jnp.concatenate([primal, tangent]), (("cross", 2),), 1)
    return (both_rims[:3], both_rims[3:])


def return_ghosts(cot_padded):
    from_left = shifted(cot_padded[:, :, -1], "cross", 1)
    from_right = shifted(cot_padded[:, :, 0], "cross", -1)
    interior = cot_padded[:, :, 1:-1]
    interior = interior.at[:, :, 0].add(from_left)
    interior = interior.at[:, :, -1].add(from_right)
    return interior


def local(state, log_mu, log_xi, dir_mu, dir_xi, wet, observed, terrain, class_weight):
    wet_frac = wet.astype(jnp.float32)
    row_count = state.shape[1]
    col_count = state.shape[2]
    devices = lax.axis_size("cross")
    local_fast = fastest_local(state)
    local_count = jnp.sum(observed).astype(jnp.float32)
    both = over_cross(jnp.stack([jnp.full((128,), local_fast), jnp.full((128,), local_count)]))
    speed_start = jnp.max(both[:, 0, 0])
    observed_count = jnp.sum(both[:, 1, 0])
    step_start = COURANT / speed_start

    def advance(state_now, tangent_now, wave, time_step, opening):
        if opening:
            pad_first = padded_2(state_now, (("cross", 2),), 1)
            tangent_first = jnp.zeros_like(pad_first)
        else:
            pad_first, tangent_first = pair_halo(state_now, tangent_now)

        def rate_here(padded, mu_in, xi_in):
            return section_rate(padded, mu_in, xi_in, wet_frac, wave)

        rate_first, slope_first = jax.jvp(
            rate_here, (pad_first, log_mu, log_xi), (tangent_first, dir_mu, dir_xi)
        )
        first_section = state_now + time_step * rate_first
        first_tangent = tangent_now + time_step * slope_first
        pad_second, tangent_second = pair_halo(first_section, first_tangent)
        rate_second, slope_second = jax.jvp(
            rate_here, (pad_second, log_mu, log_xi), (tangent_second, dir_mu, dir_xi)
        )
        next_state = 0.5 * (state_now + first_section + time_step * rate_second)
        next_tangent = 0.5 * (tangent_now + first_tangent + time_step * slope_second)
        return (next_state, next_tangent, pad_first, pad_second)

    state_mid, tangent_mid, early_first, early_second = advance(
        state, jnp.zeros_like(state), speed_start, step_start, True
    )
    speed_next = jnp.max(over_cross(jnp.full((1, 128), fastest_local(state_mid))))
    step_next = COURANT / speed_next
    state_end, tangent_end, late_first, late_second = advance(
        state_mid, tangent_mid, speed_next, step_next, False
    )

    def step_back(cotangent, pad_first, pad_second, wave, time_step, carry_state):

        def rate_here(padded, mu_in, xi_in):
            return section_rate(padded, mu_in, xi_in, wet_frac, wave)

        unused_rate, pull_second = jax.vjp(rate_here, pad_second, log_mu, log_xi)
        cot_second, grad_mu, grad_xi = pull_second(0.5 * time_step * cotangent)
        cot_first = 0.5 * cotangent + return_ghosts(cot_second)
        if carry_state:
            unused_first, pull_first = jax.vjp(rate_here, pad_first, log_mu, log_xi)
            cot_pad, more_mu, more_xi = pull_first(time_step * cot_first)
            cot_state = 0.5 * cotangent + cot_first + return_ghosts(cot_pad)
        else:

            def params_only(mu_in, xi_in):
                return rate_here(pad_first, mu_in, xi_in)

            unused_first, pull_first = jax.vjp(params_only, log_mu, log_xi)
            more_mu, more_xi = pull_first(time_step * cot_first)
            cot_state = cot_first
        return (cot_state, grad_mu + more_mu, grad_xi + more_xi)

    weight = DATA_WEIGHT * (row_count * col_count * devices) / observed_count
    blank = jnp.zeros_like(tangent_end[0])
    seed_cot = jnp.stack([weight * observed.astype(jnp.float32) * tangent_end[0], blank, blank])
    cot_mid, mu_late, xi_late = step_back(
        seed_cot, late_first, late_second, speed_next, step_next, True
    )
    unused_cot, mu_early, xi_early = step_back(
        cot_mid, early_first, early_second, speed_start, step_start, False
    )
    reg_weight = jnp.zeros_like(dir_mu)
    for class_id in range(class_weight.shape[0]):
        reg_weight = reg_weight + jnp.where(terrain == class_id, class_weight[class_id], 0.0)
    dir_rim = padded_2(jnp.stack([dir_mu, dir_xi]), (("cross", 2),), 1)
    bent_field = laplace_cols(dir_rim) * reg_weight
    smoothed = laplace_cols(padded_2(bent_field, (("cross", 2),), 1))
    return (mu_early + mu_late + smoothed[0], xi_early + xi_late + smoothed[1])


def solution(mesh):
    return jax.shard_map(
        local,
        mesh=mesh,
        in_specs=(
            P(None, "grp", "cross"),
            P("grp", "cross"),
            P("grp", "cross"),
            P("grp", "cross"),
            P("grp", "cross"),
            P("grp", "cross"),
            P("grp", "cross"),
            P("grp", "cross"),
            P(),
        ),
        out_specs=(P("grp", "cross"), P("grp", "cross")),
        check_vma=False,
    )
```

```python
import jax
import jax.numpy as jnp
from jax import lax
from jax.sharding import PartitionSpec as P

COS_SLOPE = 0.8
SIN_SLOPE = 0.6
DEPTH_FLOOR = 0.05
SPEED_EPS = 0.01
COURANT = 0.2
DATA_WEIGHT = 100000.0


def padded_2(cells, sides, width):
    for axis, dim in sides:
        count = lax.axis_size(axis)
        ends = count - 1
        head = lax.slice_in_dim(cells, 0, width, axis=dim)
        tail = lax.slice_in_dim(cells, cells.shape[dim] - width, cells.shape[dim], axis=dim)
        cells = jnp.concatenate(
            [
                lax.ppermute(tail, axis, [(i, (i + 1) % count) for i in range(ends)]),
                cells,
                lax.ppermute(head, axis, [((i + 1) % count, i) for i in range(ends)]),
            ],
            axis=dim,
        )
    return cells


def over_cross(value):
    count = lax.axis_size("cross")
    copies = jnp.broadcast_to(value[None], (count,) + value.shape)
    return lax.all_to_all(copies, "cross", 0, 0)


def shifted(shard, axis, by):
    count = lax.axis_size(axis)
    pairs = [(i, i + by) for i in range(count) if 0 <= i + by < count]
    return lax.ppermute(shard, axis, pairs)


def section_rate(padded, log_mu, log_xi, wet_frac, wave_speed):
    full_rows = jnp.pad(padded, ((0, 0), (1, 1), (0, 0)))
    height = full_rows[0]
    flow_down = full_rows[1]
    flow_across = full_rows[2]
    safe_height = jnp.maximum(height, DEPTH_FLOOR)
    vel_down = flow_down / safe_height
    vel_across = flow_across / safe_height
    pressure = 0.5 * COS_SLOPE * height * height
    flux_x = jnp.stack([flow_down, flow_down * vel_down + pressure, flow_down * vel_across])
    flux_y = jnp.stack([flow_across, flow_across * vel_down, flow_across * vel_across + pressure])
    face_down = 0.5 * (flux_x[:, :-1, 1:-1] + flux_x[:, 1:, 1:-1]) - 0.5 * wave_speed * (
        full_rows[:, 1:, 1:-1] - full_rows[:, :-1, 1:-1]
    )
    face_across = 0.5 * (flux_y[:, 1:-1, :-1] + flux_y[:, 1:-1, 1:]) - 0.5 * wave_speed * (
        full_rows[:, 1:-1, 1:] - full_rows[:, 1:-1, :-1]
    )
    diverge = face_down[:, 1:] - face_down[:, :-1] + face_across[:, :, 1:] - face_across[:, :, :-1]
    inner_height = height[1:-1, 1:-1]
    inner_down = vel_down[1:-1, 1:-1]
    inner_across = vel_across[1:-1, 1:-1]
    speed_norm = jnp.sqrt(inner_down * inner_down + inner_across * inner_across + SPEED_EPS)
    resistance = (
        wet_frac
        * (jnp.exp(log_mu) * COS_SLOPE * inner_height + speed_norm * speed_norm * jnp.exp(-log_xi))
        / speed_norm
    )
    source_term = jnp.stack(
        [
            jnp.zeros_like(inner_height),
            SIN_SLOPE * inner_height - resistance * inner_down,
            -resistance * inner_across,
        ]
    )
    return source_term - diverge


def fastest_local(state):
    safe_height = jnp.maximum(state[0], DEPTH_FLOOR)
    vel_down = state[1] / safe_height
    vel_across = state[2] / safe_height
    return jnp.max(
        jnp.sqrt(vel_down * vel_down + vel_across * vel_across)
        + jnp.sqrt(COS_SLOPE * jnp.maximum(state[0], 0.0))
    )


def laplace_cols(padded):
    full_rows = jnp.pad(padded, ((0, 0), (1, 1), (0, 0)))
    center = full_rows[:, 1:-1, 1:-1]
    return (
        4.0 * center
        - full_rows[:, :-2, 1:-1]
        - full_rows[:, 2:, 1:-1]
        - full_rows[:, 1:-1, :-2]
        - full_rows[:, 1:-1, 2:]
    )


def pair_halo(primal, tangent):
    both_rims = padded_2(jnp.concatenate([primal, tangent]), (("cross", 2),), 1)
    return (both_rims[:3], both_rims[3:])


def return_ghosts(cot_padded):
    from_left = shifted(cot_padded[:, :, -1], "cross", 1)
    from_right = shifted(cot_padded[:, :, 0], "cross", -1)
    interior = cot_padded[:, :, 1:-1]
    interior = interior.at[:, :, 0].add(from_left)
    interior = interior.at[:, :, -1].add(from_right)
    return interior


def local(state, log_mu, log_xi, dir_mu, dir_xi, wet, observed, terrain, class_weight):
    wet_frac = wet.astype(jnp.float32)
    row_count = state.shape[1]
    col_count = state.shape[2]
    devices = lax.axis_size("cross")
    local_fast = fastest_local(state)
    local_count = jnp.sum(observed).astype(jnp.float32)
    both = over_cross(jnp.stack([jnp.full((128,), local_fast), jnp.full((128,), local_count)]))
    speed_start = jnp.max(both[:, 0, 0])
    observed_count = jnp.sum(both[:, 1, 0])
    step_start = COURANT / speed_start

    def advance(state_now, tangent_now, wave, time_step, opening):
        if opening:
            pad_first = padded_2(state_now, (("cross", 2),), 1)
            tangent_first = jnp.zeros_like(pad_first)
        else:
            pad_first, tangent_first = pair_halo(state_now, tangent_now)

        def rate_here(padded, mu_in, xi_in):
            return section_rate(padded, mu_in, xi_in, wet_frac, wave)

        rate_first, slope_first = jax.jvp(
            rate_here, (pad_first, log_mu, log_xi), (tangent_first, dir_mu, dir_xi)
        )
        first_section = state_now + time_step * rate_first
        first_tangent = tangent_now + time_step * slope_first
        pad_second, tangent_second = pair_halo(first_section, first_tangent)
        rate_second, slope_second = jax.jvp(
            rate_here, (pad_second, log_mu, log_xi), (tangent_second, dir_mu, dir_xi)
        )
        next_state = 0.5 * (state_now + first_section + time_step * rate_second)
        next_tangent = 0.5 * (tangent_now + first_tangent + time_step * slope_second)
        return (next_state, next_tangent, pad_first, pad_second)

    state_mid, tangent_mid, early_first, early_second = advance(
        state, jnp.zeros_like(state), speed_start, step_start, True
    )
    speed_next = jnp.max(over_cross(jnp.full((1, 128), fastest_local(state_mid))))
    step_next = COURANT / speed_next
    state_end, tangent_end, late_first, late_second = advance(
        state_mid, tangent_mid, speed_next, step_next, False
    )

    def step_back(cotangent, pad_first, pad_second, wave, time_step, carry_state):

        def rate_here(padded, mu_in, xi_in):
            return section_rate(padded, mu_in, xi_in, wet_frac, wave)

        unused_rate, pull_second = jax.vjp(rate_here, pad_second, log_mu, log_xi)
        cot_second, grad_mu, grad_xi = pull_second(0.5 * time_step * cotangent)
        cot_first = 0.5 * cotangent + return_ghosts(cot_second)
        if carry_state:
            unused_first, pull_first = jax.vjp(rate_here, pad_first, log_mu, log_xi)
            cot_pad, more_mu, more_xi = pull_first(time_step * cot_first)
            cot_state = 0.5 * cotangent + cot_first + return_ghosts(cot_pad)
        else:

            def params_only(mu_in, xi_in):
                return rate_here(pad_first, mu_in, xi_in)

            unused_first, pull_first = jax.vjp(params_only, log_mu, log_xi)
            more_mu, more_xi = pull_first(time_step * cot_first)
            cot_state = cot_first
        return (cot_state, grad_mu + more_mu, grad_xi + more_xi)

    weight = DATA_WEIGHT * (row_count * col_count * devices) / observed_count
    blank = jnp.zeros_like(tangent_end[0])
    seed_cot = jnp.stack([weight * observed.astype(jnp.float32) * tangent_end[0], blank, blank])
    cot_mid, mu_late, xi_late = step_back(
        seed_cot, late_first, late_second, speed_next, step_next, True
    )
    unused_cot, mu_early, xi_early = step_back(
        cot_mid, early_first, early_second, speed_start, step_start, False
    )
    reg_weight = jnp.zeros_like(dir_mu)
    for class_id in range(class_weight.shape[0]):
        reg_weight = reg_weight + jnp.where(terrain == class_id, class_weight[class_id], 0.0)
    dir_rim = padded_2(jnp.stack([dir_mu, dir_xi]), (("cross", 2),), 1)
    bent_field = laplace_cols(dir_rim) * reg_weight
    smoothed = laplace_cols(padded_2(bent_field, (("cross", 2),), 1))
    return (mu_early + mu_late + smoothed[0], xi_early + xi_late + smoothed[1])


def solution(mesh):
    return jax.shard_map(
        local,
        mesh=mesh,
        in_specs=(
            P(None, "grp", "cross"),
            P("grp", "cross"),
            P("grp", "cross"),
            P("grp", "cross"),
            P("grp", "cross"),
            P("grp", "cross"),
            P("grp", "cross"),
            P("grp", "cross"),
            P(),
        ),
        out_specs=(P("grp", "cross"), P("grp", "cross")),
        check_vma=False,
    )
```

```python
import functools

import jax
import jax.numpy as jnp
from jax import lax
from jax.experimental import pallas as pl
from jax.experimental.pallas import tpu as pltpu
from jax.sharding import PartitionSpec as P

COS_SLOPE = 0.8
SIN_SLOPE = 0.6
DEPTH_FLOOR = 0.05
SPEED_EPS = 0.01
COURANT = 0.2
DATA_WEIGHT = 100000.0

LANES = 128
TILE = 8
H, Q1, Q2, FA, FB, DA, DB, DM, DX, WR, OB = range(11)
FIELDS = 11
UNROLL = 2


def load(ref, k, col, groups):
    return jnp.concatenate([ref[k, g, pl.ds(col, TILE), :] for g in range(groups)], axis=0)


def store(ref, k, col, value, groups):
    for g in range(groups):
        ref[k, g, pl.ds(col, TILE), :] = value[g * TILE : (g + 1) * TILE]


class Grid:
    def __init__(self, groups, cols):
        self.groups = groups
        self.cols = cols
        self.tiles = cols // TILE + 2
        self.lane = lax.broadcasted_iota(jnp.int32, (groups * TILE, LANES), 1)
        self.blank = jnp.zeros((TILE, LANES), jnp.float32)

    def rows_next(self, v):
        turned = pltpu.roll(v, LANES - 1, 1)
        after = jnp.concatenate([turned[TILE:], self.blank], axis=0)
        return jnp.where(self.lane == LANES - 1, after, turned)

    def rows_prev(self, v):
        turned = pltpu.roll(v, 1, 1)
        before = jnp.concatenate([self.blank, turned[: -TILE]], axis=0)
        return jnp.where(self.lane == 0, before, turned)

    def both_rows(self, v):
        return self.rows_next(v), self.rows_prev(v)

    def get(self, ref, k, col):
        return load(ref, k, col, self.groups)

    def put(self, ref, k, col, v):
        store(ref, k, col, v, self.groups)

    def both_cols(self, ref, k, col):
        return load(ref, k, col + 1, self.groups), load(ref, k, col - 1, self.groups)

    def sweep(self, body, first=0, last=None, carry=None):
        last = self.tiles if last is None else last
        steps, rest = divmod(last - first, UNROLL)

        def visit(t, col, carry):
            return body(t, col) if carry is None else body(t, col, carry)

        def step(i, carry):
            for u in range(UNROLL):
                t = first + i * UNROLL + u
                carry = visit(t, pl.multiple_of((t + 1) * TILE, TILE), carry)
            return carry

        carry = lax.fori_loop(0, steps, step, carry)
        for t in range(last - rest, last):
            carry = visit(t, (t + 1) * TILE, carry)
        return carry

    def inside(self, t, ends):
        return jnp.logical_not(((t == 0) & ends[0]) | ((t == self.tiles - 1) & ends[1]))


def end_flags():
    me = lax.axis_index("cross")
    return me == 0, me == lax.axis_size("cross") - 1


def speed_of(height, down, across):
    inv = 1.0 / jnp.maximum(height, DEPTH_FLOOR)
    vel_down = down * inv
    vel_across = across * inv
    return jnp.sqrt(vel_down * vel_down + vel_across * vel_across) + jnp.sqrt(COS_SLOPE * jnp.maximum(height, 0.0))


def velocities(height, down, across):
    inv = 1.0 / jnp.maximum(height, DEPTH_FLOOR)
    return inv, down * inv, across * inv


def friction(height, vel_down, vel_across, dry, turbulent):
    squared = vel_down * vel_down + vel_across * vel_across + SPEED_EPS
    inv_speed = lax.rsqrt(squared)
    speed = squared * inv_speed
    return inv_speed, speed, dry * height * inv_speed, turbulent * speed


def splat_max(rows, shape):
    return jnp.broadcast_to(jnp.max(rows, axis=0, keepdims=True), shape)


def prepare(state, log_mu, log_xi, dir_mu, dir_xi, wet, observed, terrain, class_weight,
            own, edge_a, edge_b, row, count_row, code, turned):
    rows, cols = log_mu.shape
    groups = rows // LANES
    step_rows = 16

    def scan(i, carry):
        top, seen = carry
        at = pl.ds(pl.multiple_of(i * step_rows, step_rows), step_rows)
        seen_here = observed[at, :]
        code[at, :] = (wet[at, :] + 2 * seen_here + 4 * terrain[at, :]).astype(jnp.float32)
        here = speed_of(state[0, at, :], state[1, at, :], state[2, at, :])
        return jnp.maximum(top, here), seen + seen_here.astype(jnp.float32)

    zero = jnp.zeros((step_rows, cols), jnp.float32)
    top, seen = lax.fori_loop(0, rows // step_rows, scan, (zero, zero))
    row[...] = jnp.full(row.shape, jnp.max(top), jnp.float32)
    count_row[...] = jnp.full(count_row.shape, jnp.sum(seen), jnp.float32)

    for g in range(groups):
        at = pl.ds(g * LANES, LANES)
        for k in range(3):
            own[k, g] = state[k, at, :].T
        own[DM, g] = dir_mu[at, :].T
        own[DX, g] = dir_xi[at, :].T
        turned[0, g] = log_mu[at, :].T
        turned[1, g] = log_xi[at, :].T
        turned[2, g] = code[at, :].T

    def derive(i, carry):
        for g in range(groups):
            at = pl.ds(pl.multiple_of(i * TILE, TILE), TILE)
            bits = turned[2, g, at, :].astype(jnp.int32)
            wet_here = (bits & 1).astype(jnp.float32)
            kind = bits >> 2
            dry = wet_here * jnp.exp(turned[0, g, at, :]) * COS_SLOPE
            turbulent = wet_here * jnp.exp(-turned[1, g, at, :])
            own[FA, g, at, :] = dry
            own[FB, g, at, :] = turbulent
            own[DA, g, at, :] = dry * own[DM, g, at, :]
            own[DB, g, at, :] = -turbulent * own[DX, g, at, :]
            own[OB, g, at, :] = ((bits >> 1) & 1).astype(jnp.float32)
            weight = jnp.zeros((TILE, LANES), jnp.float32)
            for c in range(class_weight.shape[0]):
                weight = jnp.where(kind == c, class_weight[c], weight)
            own[WR, g, at, :] = weight
        return carry

    lax.fori_loop(0, cols // TILE, derive, 0)
    even = lax.rem(lax.axis_index("cross"), 2) == 0
    for k in range(FIELDS):
        for g in range(groups):
            left = own[k, g, :TILE, :]
            right = own[k, g, cols - TILE :, :]
            edge_a[k, g] = jnp.where(even, right, left)
            edge_b[k, g] = jnp.where(even, left, right)


def open_step(own, edge_a, edge_b, ext, xy, base):
    groups, cols = own.shape[1], own.shape[2]
    grid = Grid(groups, cols)
    even = lax.rem(lax.axis_index("cross"), 2) == 0
    for k in range(FIELDS):
        for g in range(groups):
            ext[k, g, TILE : 2 * TILE, :] = jnp.where(even, edge_b[k, g], edge_a[k, g])
            ext[k, g, 2 * TILE + cols : 3 * TILE + cols, :] = jnp.where(even, edge_a[k, g], edge_b[k, g])
            ext[k, g, 2 * TILE : 2 * TILE + cols, :] = own[k, g]

    def first(t, col):
        height, down, across = (grid.get(ext, k, col) for k in (H, Q1, Q2))
        _, u, v = velocities(height, down, across)
        inv_speed, speed, dry, turb = friction(height, u, v, grid.get(ext, FA, col), grid.get(ext, FB, col))
        change = grid.get(ext, DA, col) * height * inv_speed + grid.get(ext, DB, col) * speed
        grid.put(xy, 6, col, -u * change)
        grid.put(xy, 7, col, -v * change)
        for k, value in enumerate((u, v, dry, turb)):
            grid.put(base, k, col, value)
        drag = dry + turb
        pressure = 0.5 * COS_SLOPE * height * height
        mixed = down * v
        hn, hp = grid.both_rows(height)
        pn, pp = grid.both_rows(down)
        qn, qp = grid.both_rows(across)
        fn, fp = grid.both_rows(down * u + pressure)
        gn, gp = grid.both_rows(mixed)
        grid.put(base, 4, col, mixed)
        grid.put(base, 5, col, across * v + pressure)
        grid.put(xy, 0, col, 0.6 * height + 0.1 * (hn + hp))
        grid.put(xy, 1, col, 0.6 * down + 0.1 * (pn + pp))
        grid.put(xy, 2, col, 0.6 * across + 0.1 * (qn + qp))
        grid.put(xy, 3, col, -0.5 * (pn - pp))
        grid.put(xy, 4, col, SIN_SLOPE * height - drag * u - 0.5 * (fn - fp))
        grid.put(xy, 5, col, -drag * v - 0.5 * (gn - gp))

    grid.sweep(first)

    def second(t, col):
        hn, hp = grid.both_cols(ext, H, col)
        pn, pp = grid.both_cols(ext, Q1, col)
        qn, qp = grid.both_cols(ext, Q2, col)
        gn, gp = grid.both_cols(base, 4, col)
        fn, fp = grid.both_cols(base, 5, col)
        for k, (n, p) in enumerate(((hn, hp), (pn, pp), (qn, qp))):
            grid.put(xy, k, col, grid.get(xy, k, col) + 0.1 * (n + p))
        for k, (n, p) in enumerate(((qn, qp), (gn, gp), (fn, fp))):
            grid.put(xy, 3 + k, col, grid.get(xy, 3 + k, col) - 0.5 * (n - p))

    grid.sweep(second)


CU, CV, CZ, CW, CE, CB, CD = range(7)
MU, MV, MZ, MW, ME, MB, MM, MH, MY = range(9)


def middle(ends_of, top_rows, ext, xy, count_row, at_one, mid, row, work):
    groups, cols = ext.shape[1], ext.shape[2] - 4 * TILE
    grid = Grid(groups, cols)
    ends = ends_of()
    dt = COURANT / splat_max(top_rows[...], grid.lane.shape)
    half = 0.5 * dt

    def first(t, col):
        keep = grid.inside(t, ends)
        height, down, across = (
            jnp.where(keep, grid.get(xy, k, col) + dt * grid.get(xy, 3 + k, col), 0.0) for k in range(3)
        )
        inv, u, v = velocities(height, down, across)
        inv_speed, speed, dry, turb = friction(height, u, v, grid.get(ext, FA, col), grid.get(ext, FB, col))
        drag = dry + turb
        grid.put(at_one, CU, col, u)
        grid.put(at_one, CV, col, v)
        grid.put(at_one, CZ, col, (grid.get(ext, FB, col) - dry * inv_speed) * inv_speed * inv)
        grid.put(at_one, CW, col, drag * inv)
        grid.put(at_one, CE, col, dry)
        grid.put(at_one, CB, col, turb)
        grid.put(at_one, CD, col, grid.get(ext, DA, col) * height * inv_speed + grid.get(ext, DB, col) * speed)
        pressure = 0.5 * COS_SLOPE * height * height
        mixed = down * v
        for k, value in enumerate((height, down, across, mixed, across * v + pressure)):
            grid.put(work, k, col, value)
        sources = (0.0, dt * (SIN_SLOPE * height - drag * u), -dt * drag * v)
        for k, (value, flux) in enumerate(((height, down), (down, down * u + pressure), (across, mixed))):
            tenth, moved = 0.1 * value, half * flux
            total = grid.get(ext, k, col) + 0.6 * value + sources[k]
            total += grid.rows_next(tenth - moved) + grid.rows_prev(tenth + moved)
            grid.put(mid, k, col, total)

    grid.sweep(first)

    def second(t, col, top):
        keep = grid.inside(t, ends)
        found = []
        for k, (value, flux) in enumerate(((0, 2), (1, 3), (2, 4))):
            vn, vp = grid.both_cols(work, value, col)
            fn, fp = grid.both_cols(work, flux, col)
            total = grid.get(mid, k, col) + 0.1 * (vn + vp) - half * (fn - fp)
            found.append(jnp.where(keep, 0.5 * total, 0.0))
            grid.put(mid, k, col, found[k])
        own = (t > 0) & (t < grid.tiles - 1)
        return jnp.maximum(top, jnp.where(own, speed_of(*found), 0.0))

    top = grid.sweep(second, carry=jnp.zeros(grid.lane.shape, jnp.float32))
    lane = lax.broadcasted_iota(jnp.int32, row.shape, 1)
    count = jnp.broadcast_to(count_row[:1, :], row.shape)
    row[...] = jnp.where(lane < LANES // 2, jnp.full(row.shape, jnp.max(top), jnp.float32), count)


def tangents(ends_of, top_rows, ext, xy, at_one, mid, tan, at_mid, smooth, work):
    groups, cols = ext.shape[1], ext.shape[2] - 4 * TILE
    grid = Grid(groups, cols)
    ends = ends_of()
    dt = COURANT / splat_max(top_rows[...], grid.lane.shape)
    half = 0.5 * dt

    def first(t, col):
        tp, tq = dt * grid.get(xy, 6, col), dt * grid.get(xy, 7, col)
        u, v = grid.get(at_one, CU, col), grid.get(at_one, CV, col)
        w = grid.get(at_one, CW, col)
        along = grid.get(at_one, CZ, col) * (u * tp + v * tq) + grid.get(at_one, CD, col)
        mixed = v * tp + u * tq
        for k, value in enumerate((tp, tq, mixed, 2.0 * v * tq)):
            grid.put(work, k, col, value)
        moved = half * tp
        grid.put(tan, 0, col, grid.rows_prev(moved) - grid.rows_next(moved))
        sources = (-dt * (u * along + w * tp), -dt * (v * along + w * tq))
        for k, (value, flux) in enumerate(((tp, 2.0 * u * tp), (tq, mixed))):
            tenth, moved = 0.1 * value, half * flux
            total = 0.6 * value + sources[k]
            total += grid.rows_next(tenth - moved) + grid.rows_prev(tenth + moved)
            grid.put(tan, 1 + k, col, total)

    grid.sweep(first)

    def second(t, col):
        keep = grid.inside(t, ends)
        qn, qp = grid.both_cols(work, 1, col)
        pn, pp = grid.both_cols(work, 0, col)
        gn, gp = grid.both_cols(work, 2, col)
        fn, fp = grid.both_cols(work, 3, col)
        th = grid.get(tan, 0, col) - half * (qn - qp)
        tp = grid.get(tan, 1, col) + 0.1 * (pn + pp) - half * (gn - gp)
        tq = grid.get(tan, 2, col) + 0.1 * (qn + qp) - half * (fn - fp)
        th, tp, tq = (jnp.where(keep, 0.5 * x, 0.0) for x in (th, tp, tq))
        height, down, across = (grid.get(mid, k, col) for k in range(3))
        inv, u, v = velocities(height, down, across)
        above = jnp.where(height > DEPTH_FLOOR, 1.0, jnp.where(height == DEPTH_FLOOR, 0.5, 0.0))
        turb_of = grid.get(ext, FB, col)
        dry_of = grid.get(ext, FA, col)
        inv_speed, speed, dry, turb = friction(height, u, v, dry_of, turb_of)
        z = (turb_of - dry * inv_speed) * inv_speed * inv
        w = (dry + turb) * inv
        y = dry_of * inv_speed - above * (z * (u * u + v * v) + w)
        eight = COS_SLOPE * height
        for k, value in ((MU, u), (MV, v), (MZ, z), (MW, w), (ME, dry), (MB, turb), (MM, above), (MH, eight), (MY, y)):
            grid.put(at_mid, k, col, value)
        change = grid.get(ext, DA, col) * height * inv_speed + grid.get(ext, DB, col) * speed
        along = z * (u * tp + v * tq) + y * th + change
        lift = above * th
        flux_down = 2.0 * u * tp + eight * th - u * u * lift
        mixed = v * tp + u * tq - u * v * lift
        for k, value in enumerate((th, tp, tq, mixed, 2.0 * v * tq + eight * th - v * v * lift)):
            grid.put(work, 4 + k, col, value)
        hn, hp = grid.both_rows(th)
        pn, pp = grid.both_rows(tp)
        qn, qp = grid.both_rows(tq)
        fn, fp = grid.both_rows(flux_down)
        gn, gp = grid.both_rows(mixed)
        grid.put(tan, 0, col, th)
        grid.put(tan, 1, col, 0.6 * th + 0.1 * (hn + hp))
        grid.put(tan, 2, col, 0.6 * tp + 0.1 * (pn + pp))
        grid.put(tan, 3, col, 0.6 * tq + 0.1 * (qn + qp))
        grid.put(tan, 4, col, -0.5 * (pn - pp))
        grid.put(tan, 5, col, SIN_SLOPE * th - u * along - w * tp - 0.5 * (fn - fp))
        grid.put(tan, 6, col, -v * along - w * tq - 0.5 * (gn - gp))

    grid.sweep(second)

    def third(t, col):
        keep = grid.inside(t, ends)
        hn, hp = grid.both_cols(work, 4, col)
        pn, pp = grid.both_cols(work, 5, col)
        qn, qp = grid.both_cols(work, 6, col)
        gn, gp = grid.both_cols(work, 7, col)
        fn, fp = grid.both_cols(work, 8, col)
        for k, (n, p) in enumerate(((hn, hp), (pn, pp), (qn, qp))):
            grid.put(tan, 1 + k, col, jnp.where(keep, grid.get(tan, 1 + k, col) + 0.1 * (n + p), 0.0))
        for k, (n, p) in enumerate(((qn, qp), (gn, gp), (fn, fp))):
            grid.put(tan, 4 + k, col, jnp.where(keep, grid.get(tan, 4 + k, col) - 0.5 * (n - p), 0.0))

    grid.sweep(third)

    def laplace(ref, k, col):
        value = grid.get(ref, k, col)
        rn, rp = grid.both_rows(value)
        cn, cp = grid.both_cols(ref, k, col)
        return 4.0 * value - rn - rp - cn - cp

    def bend(t, col):
        weight = grid.get(ext, WR, col)
        for k, field in enumerate((DM, DX)):
            grid.put(work, k, col, weight * laplace(ext, field, col))

    grid.sweep(bend)

    def bend_again(t, col):
        for k in range(2):
            grid.put(smooth, k, col, laplace(work, k, col))

    grid.sweep(bend_again, 1, grid.tiles - 1)


def finish(ends_of, cells, top_rows, next_rows, ext, base, at_one, tan, at_mid, smooth, out_mu, out_xi, work, total):
    groups, cols = ext.shape[1], ext.shape[2] - 4 * TILE
    grid = Grid(groups, cols)
    ends = ends_of()
    shape = grid.lane.shape
    dt0 = COURANT / splat_max(top_rows[...], shape)
    rows = next_rows[...]
    lane = lax.broadcasted_iota(jnp.int32, (1, LANES), 1)
    most = jnp.max(rows, axis=0, keepdims=True)
    added = jnp.sum(rows, axis=0, keepdims=True)
    dt1 = COURANT / jnp.broadcast_to(jnp.where(lane < LANES // 2, most, pltpu.roll(most, LANES // 2, 1)), shape)
    count = jnp.where(lane < LANES // 2, pltpu.roll(added, LANES // 2, 1), added)
    weight = jnp.broadcast_to((DATA_WEIGHT * cells) / count, shape)
    half1 = 0.5 * dt1
    half0 = 0.5 * dt0

    def end(t, col):
        def section(k, off):
            return grid.get(tan, 1 + k, col + off) + dt1 * grid.get(tan, 4 + k, col + off)

        th, tp = section(0, 0), section(1, 0)
        tenth, moved = 0.1 * th, half1 * tp
        value = grid.get(tan, 0, col) + 0.6 * th + grid.rows_next(tenth - moved) + grid.rows_prev(tenth + moved)
        value += 0.1 * (section(0, 1) + section(0, -1)) - half1 * (section(2, 1) - section(2, -1))
        grid.put(work, 0, col, weight * grid.get(ext, OB, col) * (0.5 * value))

    grid.sweep(end)

    def back_second(t, col):
        keep = grid.inside(t, ends)
        seed = grid.get(work, 0, col)
        rn, rp = grid.both_rows(seed)
        cn, cp = grid.both_cols(work, 0, col)
        zero = jnp.zeros_like(seed)
        grid.put(work, 1, col, jnp.where(keep, 0.3 * seed + 0.05 * (rn + rp + cn + cp), zero))
        grid.put(work, 2, col, jnp.where(keep, 0.5 * half1 * (rn - rp), zero))
        grid.put(work, 3, col, jnp.where(keep, 0.5 * half1 * (cn - cp), zero))

    grid.sweep(back_second)

    def back_first(t, col):
        keep = grid.inside(t, ends)
        g0, g1, g2 = (grid.get(work, 1 + k, col) for k in range(3))
        r0n, r0p = grid.both_rows(g0)
        r1n, r1p = grid.both_rows(g1)
        r2n, r2p = grid.both_rows(g2)
        c0n, c0p = grid.both_cols(work, 1, col)
        c1n, c1p = grid.both_cols(work, 2, col)
        c2n, c2p = grid.both_cols(work, 3, col)
        u, v = grid.get(at_mid, MU, col), grid.get(at_mid, MV, col)
        z, w = grid.get(at_mid, MZ, col), grid.get(at_mid, MW, col)
        down = half1 * (r1n - r1p)
        cross = half1 * ((r2n - r2p) + (c1n - c1p))
        side = half1 * (c2n - c2p)
        h1, h2 = dt1 * g1, dt1 * g2
        along = u * h1 + v * h2
        grid.put(total, 0, col, grid.get(smooth, 0, col) - grid.get(at_mid, ME, col) * along)
        grid.put(total, 1, col, grid.get(smooth, 1, col) + grid.get(at_mid, MB, col) * along)
        pull = z * along
        part_u = u * down + v * cross
        part_v = v * side
        m0 = 0.5 * grid.get(work, 0, col) + 0.6 * g0 + 0.1 * (r0n + r0p + c0n + c0p)
        m0 += SIN_SLOPE * h1 - grid.get(at_mid, MY, col) * along + grid.get(at_mid, MH, col) * (down + side)
        m0 -= grid.get(at_mid, MM, col) * (u * part_u + v * part_v)
        m1 = 0.6 * g1 + 0.1 * (r1n + r1p + c1n + c1p)
        m1 += half1 * (r0n - r0p) + 2.0 * u * down + v * cross - u * pull - w * h1
        m2 = 0.6 * g2 + 0.1 * (r2n + r2p + c2n + c2p)
        m2 += half1 * (c0n - c0p) + u * cross + 2.0 * v * side - v * pull - w * h2
        for k, value in enumerate((m0, m1, m2)):
            grid.put(work, 4 + k, col, jnp.where(keep, value, 0.0))

    grid.sweep(back_first)

    def early(t, col):
        m0, m1, m2 = (grid.get(work, 4 + k, col) for k in range(3))
        r0n, r0p = grid.both_rows(m0)
        r1n, r1p = grid.both_rows(m1)
        r2n, r2p = grid.both_rows(m2)
        c0n, c0p = grid.both_cols(work, 4, col)
        c1n, c1p = grid.both_cols(work, 5, col)
        c2n, c2p = grid.both_cols(work, 6, col)
        u, v = grid.get(at_one, CU, col), grid.get(at_one, CV, col)
        z, w = grid.get(at_one, CZ, col), grid.get(at_one, CW, col)
        quarter = 0.5 * half0
        down = quarter * (r1n - r1p)
        cross = quarter * ((r2n - r2p) + (c1n - c1p))
        side = quarter * (c2n - c2p)
        p1, p2 = half0 * m1, half0 * m2
        along = u * p1 + v * p2
        pull = z * along
        f1 = 0.3 * m1 + 0.05 * (r1n + r1p + c1n + c1p)
        f1 += quarter * (r0n - r0p) + 2.0 * u * down + v * cross - u * pull - w * p1
        f2 = 0.3 * m2 + 0.05 * (r2n + r2p + c2n + c2p)
        f2 += quarter * (c0n - c0p) + u * cross + 2.0 * v * side - v * pull - w * p2
        start = dt0 * (grid.get(base, 0, col) * f1 + grid.get(base, 1, col) * f2)
        mu = grid.get(total, 0, col) - grid.get(at_one, CE, col) * along - grid.get(base, 2, col) * start
        xi = grid.get(total, 1, col) + grid.get(at_one, CB, col) * along + grid.get(base, 3, col) * start
        grid.put(total, 0, col, mu)
        grid.put(total, 1, col, xi)

    grid.sweep(early, 1, grid.tiles - 1)

    for g in range(groups):
        at = pl.ds(g * LANES, LANES)
        out_mu[at, :] = total[0, g, 2 * TILE : 2 * TILE + cols, :].T
        out_xi[at, :] = total[1, g, 2 * TILE : 2 * TILE + cols, :].T


VMEM = pl.BlockSpec(memory_space=pltpu.VMEM)
SMEM = pl.BlockSpec(memory_space=pltpu.SMEM)


def call(body, name, operands, outs, scratch, flops, small=()):
    outs = [jax.ShapeDtypeStruct(shape, jnp.float32) for shape in outs]
    moved = 4 * sum(x.size for x in operands) + 4 * sum(x.size for x in outs)
    return pl.pallas_call(
        body,
        name=name,
        out_shape=outs,
        in_specs=[SMEM if i in small else VMEM for i in range(len(operands))],
        out_specs=[VMEM] * len(outs),
        scratch_shapes=[pltpu.VMEM(shape, jnp.float32) for shape in scratch],
        compiler_params=pltpu.CompilerParams(vmem_limit_bytes=24 * 1024 * 1024),
        cost_estimate=pl.CostEstimate(flops=flops, bytes_accessed=moved, transcendentals=0),
    )(*operands)


def swap_edges(edge_a, edge_b, count):
    pairs_a = [(i, i ^ 1) for i in range(count)]
    pairs_b = [(i, i - 1 if i % 2 == 0 else i + 1) for i in range(1, count - 1)]
    return lax.ppermute(edge_a, "cross", pairs_a), lax.ppermute(edge_b, "cross", pairs_b)


def share(row):
    return lax.all_to_all(row, "cross", 0, 0, tiled=True)


def local(state, log_mu, log_xi, dir_mu, dir_xi, wet, observed, terrain, class_weight):
    rows, cols = log_mu.shape
    groups = rows // LANES
    count = lax.axis_size("cross")
    cells = rows * cols * count
    wide = (groups, cols + 4 * TILE, LANES)
    edge = (FIELDS, groups, TILE, LANES)
    work = rows * cols

    own, edge_a, edge_b, row, count_row = call(
        prepare,
        "prepare",
        (state, log_mu, log_xi, dir_mu, dir_xi, wet, observed, terrain, class_weight),
        [(FIELDS, groups, cols, LANES), edge, edge, (count, LANES), (TILE, LANES)],
        [(rows, cols), (3, groups, cols, LANES)],
        100 * work,
        small=(8,),
    )
    edge_a, edge_b = swap_edges(edge_a, edge_b, count)
    top_rows = share(row)
    ext, xy, base = call(
        open_step, "open_step", (own, edge_a, edge_b), [(FIELDS,) + wide, (8,) + wide, (6,) + wide], [], 100 * work
    )
    at_one, mid, next_row = call(
        functools.partial(middle, end_flags),
        "middle",
        (top_rows, ext, xy, count_row),
        [(7,) + wide, (3,) + wide, (count, LANES)],
        [(5,) + wide],
        120 * work,
    )
    next_rows = share(next_row)
    tan, at_mid, smooth = call(
        functools.partial(tangents, end_flags),
        "tangents",
        (top_rows, ext, xy, at_one, mid),
        [(7,) + wide, (9,) + wide, (2,) + wide],
        [(9,) + wide],
        200 * work,
    )
    out_mu, out_xi = call(
        functools.partial(finish, end_flags, float(cells)),
        "finish",
        (top_rows, next_rows, ext, base, at_one, tan, at_mid, smooth),
        [(rows, cols), (rows, cols)],
        [(7,) + wide, (2,) + wide],
        200 * work,
    )
    return out_mu, out_xi


def solution(mesh):
    return jax.shard_map(
        local,
        mesh=mesh,
        in_specs=(
            P(None, "grp", "cross"),
            P("grp", "cross"),
            P("grp", "cross"),
            P("grp", "cross"),
            P("grp", "cross"),
            P("grp", "cross"),
            P("grp", "cross"),
            P("grp", "cross"),
            P(),
        ),
        out_specs=(P("grp", "cross"), P("grp", "cross")),
        check_vma=False,
    )
```

```python
import functools

import jax
import jax.numpy as jnp
from jax import lax
from jax.experimental import pallas as pl
from jax.experimental.pallas import tpu as pltpu
from jax.sharding import PartitionSpec as P

COS_SLOPE = 0.8
SIN_SLOPE = 0.6
DEPTH_FLOOR = 0.05
SPEED_EPS = 0.01
COURANT = 0.2
DATA_WEIGHT = 100000.0

LANES = 128
TILE = 8
H, Q1, Q2, FA, FB, DA, DB, DM, DX, WR, OB = range(11)
FIELDS = 11
UNROLL = 6


def load(ref, k, col, groups):
    return jnp.concatenate([ref[k, g, pl.ds(col, TILE), :] for g in range(groups)], axis=0)


def store(ref, k, col, value, groups):
    for g in range(groups):
        ref[k, g, pl.ds(col, TILE), :] = value[g * TILE : (g + 1) * TILE]


class Grid:
    def __init__(self, groups, cols):
        self.groups = groups
        self.cols = cols
        self.tiles = cols // TILE + 2
        self.lane = lax.broadcasted_iota(jnp.int32, (groups * TILE, LANES), 1)
        self.blank = jnp.zeros((TILE, LANES), jnp.float32)

    def rows_next(self, v):
        turned = pltpu.roll(v, LANES - 1, 1)
        after = jnp.concatenate([turned[TILE:], self.blank], axis=0)
        return jnp.where(self.lane == LANES - 1, after, turned)

    def rows_prev(self, v):
        turned = pltpu.roll(v, 1, 1)
        before = jnp.concatenate([self.blank, turned[: -TILE]], axis=0)
        return jnp.where(self.lane == 0, before, turned)

    def both_rows(self, v):
        return self.rows_next(v), self.rows_prev(v)

    def get(self, ref, k, col):
        return load(ref, k, col, self.groups)

    def put(self, ref, k, col, v):
        store(ref, k, col, v, self.groups)

    def both_cols(self, ref, k, col):
        return load(ref, k, col + 1, self.groups), load(ref, k, col - 1, self.groups)

    def sweep(self, body, first=0, last=None, carry=None):
        last = self.tiles if last is None else last
        steps, rest = divmod(last - first, UNROLL)

        def visit(t, col, carry):
            return body(t, col) if carry is None else body(t, col, carry)

        def step(i, carry):
            for u in range(UNROLL):
                t = first + i * UNROLL + u
                carry = visit(t, pl.multiple_of((t + 1) * TILE, TILE), carry)
            return carry

        carry = lax.fori_loop(0, steps, step, carry)
        for t in range(last - rest, last):
            carry = visit(t, (t + 1) * TILE, carry)
        return carry

    def inside(self, t, ends):
        return jnp.logical_not(((t == 0) & ends[0]) | ((t == self.tiles - 1) & ends[1]))


def end_flags():
    me = lax.axis_index("cross")
    return me == 0, me == lax.axis_size("cross") - 1


def speed_of(height, down, across):
    inv = 1.0 / jnp.maximum(height, DEPTH_FLOOR)
    vel_down = down * inv
    vel_across = across * inv
    return jnp.sqrt(vel_down * vel_down + vel_across * vel_across) + jnp.sqrt(COS_SLOPE * jnp.maximum(height, 0.0))


def velocities(height, down, across):
    inv = 1.0 / jnp.maximum(height, DEPTH_FLOOR)
    return inv, down * inv, across * inv


def friction(height, vel_down, vel_across, dry, turbulent):
    squared = vel_down * vel_down + vel_across * vel_across + SPEED_EPS
    inv_speed = lax.rsqrt(squared)
    speed = squared * inv_speed
    return inv_speed, speed, dry * height * inv_speed, turbulent * speed


def first_speed(state, row, held, arrived):
    rows, cols = state.shape[1:]
    parts = held.shape[0]
    size = rows // parts
    copies = []
    for i in range(parts):
        copies.append(pltpu.make_async_copy(state.at[:, pl.ds(i * size, size), :], held.at[i], arrived.at[i]))
        copies[i].start()
    top = jnp.zeros((16, cols), jnp.float32)
    for i in range(parts):
        copies[i].wait()
        for j in range(0, size, 16):
            top = jnp.maximum(top, speed_of(*(held[i, k, j : j + 16, :] for k in range(3))))
    row[...] = jnp.full(row.shape, jnp.max(top), jnp.float32)


def prepare(*refs):
    sources, rest = refs[:9], refs[10:]
    own, edge_a, edge_b, count_row, code, turned = rest[:6]
    held, arrived = rest[6:15], rest[15]
    copies = [pltpu.make_async_copy(src, dst, arrived.at[i]) for i, (src, dst) in enumerate(zip(sources, held))]
    order = (6, 5, 7, 0, 3, 4, 1, 2, 8)
    for i in order:
        copies[i].start()
    state, log_mu, log_xi, dir_mu, dir_xi, wet, observed, terrain, class_weight = held
    rows, cols = log_mu.shape
    groups = rows // LANES
    for i in (5, 6, 7):
        copies[i].wait()
    seen = jnp.zeros((16, cols), jnp.float32)
    for i in range(0, rows, 16):
        seen_here = observed[i : i + 16, :]
        code[i : i + 16, :] = (wet[i : i + 16, :] + 2 * seen_here + 4 * terrain[i : i + 16, :]).astype(jnp.float32)
        seen += seen_here.astype(jnp.float32)
    count_row[...] = jnp.full(count_row.shape, jnp.sum(seen), jnp.float32)

    copies[0].wait()
    for g in range(groups):
        at = pl.ds(g * LANES, LANES)
        for k in range(3):
            own[k, g] = state[k, at, :].T
        turned[2, g] = code[at, :].T
    for i in (1, 2, 3, 4, 8):
        copies[i].wait()
    for g in range(groups):
        at = pl.ds(g * LANES, LANES)
        own[DM, g] = dir_mu[at, :].T
        own[DX, g] = dir_xi[at, :].T
        turned[0, g] = log_mu[at, :].T
        turned[1, g] = log_xi[at, :].T

    def derive(i, carry):
        for g, half in ((g, half) for g in range(groups) for half in range(2)):
            at = pl.ds(pl.multiple_of((2 * i + half) * TILE, TILE), TILE)
            bits = turned[2, g, at, :].astype(jnp.int32)
            wet_here = (bits & 1).astype(jnp.float32)
            kind = bits >> 2
            dry = wet_here * jnp.exp(turned[0, g, at, :]) * COS_SLOPE
            turbulent = wet_here * jnp.exp(-turned[1, g, at, :])
            own[FA, g, at, :] = dry
            own[FB, g, at, :] = turbulent
            own[DA, g, at, :] = dry * own[DM, g, at, :]
            own[DB, g, at, :] = -turbulent * own[DX, g, at, :]
            own[OB, g, at, :] = ((bits >> 1) & 1).astype(jnp.float32)
            weight = jnp.zeros((TILE, LANES), jnp.float32)
            for c in range(class_weight.shape[0]):
                weight = jnp.where(kind == c, class_weight[c], weight)
            own[WR, g, at, :] = weight
        return carry

    lax.fori_loop(0, cols // (2 * TILE), derive, 0)
    even = lax.rem(lax.axis_index("cross"), 2) == 0
    for k in range(FIELDS):
        for g in range(groups):
            left = own[k, g, :TILE, :]
            right = own[k, g, cols - TILE :, :]
            edge_a[k, g] = jnp.where(even, right, left)
            edge_b[k, g] = jnp.where(even, left, right)


def open_step(own, edge_a, edge_b, ext, xy, base):
    groups, cols = own.shape[1], own.shape[2]
    grid = Grid(groups, cols)
    even = lax.rem(lax.axis_index("cross"), 2) == 0
    for k in range(FIELDS):
        for g in range(groups):
            ext[k, g, TILE : 2 * TILE, :] = jnp.where(even, edge_b[k, g], edge_a[k, g])
            ext[k, g, 2 * TILE + cols : 3 * TILE + cols, :] = jnp.where(even, edge_a[k, g], edge_b[k, g])
            ext[k, g, 2 * TILE : 2 * TILE + cols, :] = own[k, g]

    def first(t, col):
        height, down, across = (grid.get(ext, k, col) for k in (H, Q1, Q2))
        _, u, v = velocities(height, down, across)
        inv_speed, speed, dry, turb = friction(height, u, v, grid.get(ext, FA, col), grid.get(ext, FB, col))
        change = grid.get(ext, DA, col) * height * inv_speed + grid.get(ext, DB, col) * speed
        grid.put(xy, 6, col, -u * change)
        grid.put(xy, 7, col, -v * change)
        for k, value in enumerate((u, v, dry, turb)):
            grid.put(base, k, col, value)
        drag = dry + turb
        pressure = 0.5 * COS_SLOPE * height * height
        mixed = down * v
        hn, hp = grid.both_rows(height)
        pn, pp = grid.both_rows(down)
        qn, qp = grid.both_rows(across)
        fn, fp = grid.both_rows(down * u + pressure)
        gn, gp = grid.both_rows(mixed)
        grid.put(base, 4, col, mixed)
        grid.put(base, 5, col, across * v + pressure)
        grid.put(xy, 0, col, 0.6 * height + 0.1 * (hn + hp))
        grid.put(xy, 1, col, 0.6 * down + 0.1 * (pn + pp))
        grid.put(xy, 2, col, 0.6 * across + 0.1 * (qn + qp))
        grid.put(xy, 3, col, -0.5 * (pn - pp))
        grid.put(xy, 4, col, SIN_SLOPE * height - drag * u - 0.5 * (fn - fp))
        grid.put(xy, 5, col, -drag * v - 0.5 * (gn - gp))

    grid.sweep(first)

    def second(t, col):
        hn, hp = grid.both_cols(ext, H, col)
        pn, pp = grid.both_cols(ext, Q1, col)
        qn, qp = grid.both_cols(ext, Q2, col)
        gn, gp = grid.both_cols(base, 4, col)
        fn, fp = grid.both_cols(base, 5, col)
        for k, (n, p) in enumerate(((hn, hp), (pn, pp), (qn, qp))):
            grid.put(xy, k, col, grid.get(xy, k, col) + 0.1 * (n + p))
        for k, (n, p) in enumerate(((qn, qp), (gn, gp), (fn, fp))):
            grid.put(xy, 3 + k, col, grid.get(xy, 3 + k, col) - 0.5 * (n - p))

    grid.sweep(second)


CU, CV, CZ, CW, CE, CB, CD = range(7)
MU, MV, MZ, MW, ME, MB, MM, MH, MY = range(9)


def middle(ends_of, top, top_last, ext, xy, count_row, at_one, mid, row, work):
    groups, cols = ext.shape[1], ext.shape[2] - 4 * TILE
    grid = Grid(groups, cols)
    ends = ends_of()
    dt = COURANT / jnp.broadcast_to(jnp.maximum(top[...], top_last[...]), grid.lane.shape)
    half = 0.5 * dt

    def first(t, col):
        keep = grid.inside(t, ends)
        height, down, across = (
            jnp.where(keep, grid.get(xy, k, col) + dt * grid.get(xy, 3 + k, col), 0.0) for k in range(3)
        )
        inv, u, v = velocities(height, down, across)
        inv_speed, speed, dry, turb = friction(height, u, v, grid.get(ext, FA, col), grid.get(ext, FB, col))
        drag = dry + turb
        grid.put(at_one, CU, col, u)
        grid.put(at_one, CV, col, v)
        grid.put(at_one, CZ, col, (grid.get(ext, FB, col) - dry * inv_speed) * inv_speed * inv)
        grid.put(at_one, CW, col, drag * inv)
        grid.put(at_one, CE, col, dry)
        grid.put(at_one, CB, col, turb)
        grid.put(at_one, CD, col, grid.get(ext, DA, col) * height * inv_speed + grid.get(ext, DB, col) * speed)
        pressure = 0.5 * COS_SLOPE * height * height
        mixed = down * v
        for k, value in enumerate((height, down, across, mixed, across * v + pressure)):
            grid.put(work, k, col, value)
        sources = (0.0, dt * (SIN_SLOPE * height - drag * u), -dt * drag * v)
        for k, (value, flux) in enumerate(((height, down), (down, down * u + pressure), (across, mixed))):
            tenth, moved = 0.1 * value, half * flux
            total = grid.get(ext, k, col) + 0.6 * value + sources[k]
            total += grid.rows_next(tenth - moved) + grid.rows_prev(tenth + moved)
            grid.put(mid, k, col, total)

    grid.sweep(first)

    def second(t, col, most):
        keep = grid.inside(t, ends)
        found = []
        for k, (value, flux) in enumerate(((0, 2), (1, 3), (2, 4))):
            vn, vp = grid.both_cols(work, value, col)
            fn, fp = grid.both_cols(work, flux, col)
            total = grid.get(mid, k, col) + 0.1 * (vn + vp) - half * (fn - fp)
            found.append(jnp.where(keep, 0.5 * total, 0.0))
            grid.put(mid, k, col, found[k])
        own = (t > 0) & (t < grid.tiles - 1)
        return jnp.maximum(most, jnp.where(own, speed_of(*found), 0.0))

    fastest = grid.sweep(second, carry=jnp.zeros(grid.lane.shape, jnp.float32))
    row[0:1, :] = jnp.full((1, LANES), jnp.max(fastest), jnp.float32)
    row[1:2, :] = count_row[...]


def tangent_one(top, top_last, xy, at_one, one):
    groups, cols = xy.shape[1], xy.shape[2] - 4 * TILE
    grid = Grid(groups, cols)
    dt = COURANT / jnp.broadcast_to(jnp.maximum(top[...], top_last[...]), grid.lane.shape)
    half = 0.5 * dt

    def first(t, col):
        tp, tq = dt * grid.get(xy, 6, col), dt * grid.get(xy, 7, col)
        u, v = grid.get(at_one, CU, col), grid.get(at_one, CV, col)
        w = grid.get(at_one, CW, col)
        along = grid.get(at_one, CZ, col) * (u * tp + v * tq) + grid.get(at_one, CD, col)
        mixed = v * tp + u * tq
        for k, value in enumerate((tp, tq, mixed, 2.0 * v * tq)):
            grid.put(one, k, col, value)
        moved = half * tp
        grid.put(one, 4, col, grid.rows_prev(moved) - grid.rows_next(moved))
        sources = (-dt * (u * along + w * tp), -dt * (v * along + w * tq))
        for k, (value, flux) in enumerate(((tp, 2.0 * u * tp), (tq, mixed))):
            tenth, moved = 0.1 * value, half * flux
            total = 0.6 * value + sources[k]
            total += grid.rows_next(tenth - moved) + grid.rows_prev(tenth + moved)
            grid.put(one, 5 + k, col, total)

    grid.sweep(first)

def tangent_mid(ends_of, top, top_last, ext, one, mid, part, at_mid, work):
    groups, cols = ext.shape[1], ext.shape[2] - 4 * TILE
    grid = Grid(groups, cols)
    ends = ends_of()
    dt = COURANT / jnp.broadcast_to(jnp.maximum(top[...], top_last[...]), grid.lane.shape)
    half = 0.5 * dt

    def second(t, col):
        keep = grid.inside(t, ends)
        qn, qp = grid.both_cols(one, 1, col)
        pn, pp = grid.both_cols(one, 0, col)
        gn, gp = grid.both_cols(one, 2, col)
        fn, fp = grid.both_cols(one, 3, col)
        th = grid.get(one, 4, col) - half * (qn - qp)
        tp = grid.get(one, 5, col) + 0.1 * (pn + pp) - half * (gn - gp)
        tq = grid.get(one, 6, col) + 0.1 * (qn + qp) - half * (fn - fp)
        th, tp, tq = (jnp.where(keep, 0.5 * x, 0.0) for x in (th, tp, tq))
        height, down, across = (grid.get(mid, k, col) for k in range(3))
        inv, u, v = velocities(height, down, across)
        above = jnp.where(height > DEPTH_FLOOR, 1.0, jnp.where(height == DEPTH_FLOOR, 0.5, 0.0))
        turb_of = grid.get(ext, FB, col)
        dry_of = grid.get(ext, FA, col)
        inv_speed, speed, dry, turb = friction(height, u, v, dry_of, turb_of)
        z = (turb_of - dry * inv_speed) * inv_speed * inv
        w = (dry + turb) * inv
        y = dry_of * inv_speed - above * (z * (u * u + v * v) + w)
        eight = COS_SLOPE * height
        for k, value in ((MU, u), (MV, v), (MZ, z), (MW, w), (ME, dry), (MB, turb), (MM, above), (MH, eight), (MY, y)):
            grid.put(at_mid, k, col, value)
        change = grid.get(ext, DA, col) * height * inv_speed + grid.get(ext, DB, col) * speed
        along = z * (u * tp + v * tq) + y * th + change
        lift = above * th
        flux_down = 2.0 * u * tp + eight * th - u * u * lift
        mixed = v * tp + u * tq - u * v * lift
        for k, value in enumerate((th, tp, tq, mixed, 2.0 * v * tq + eight * th - v * v * lift)):
            grid.put(work, k, col, value)
        hn, hp = grid.both_rows(th)
        pn, pp = grid.both_rows(tp)
        qn, qp = grid.both_rows(tq)
        fn, fp = grid.both_rows(flux_down)
        gn, gp = grid.both_rows(mixed)
        grid.put(part, 0, col, th)
        grid.put(part, 1, col, 0.6 * th + 0.1 * (hn + hp))
        grid.put(part, 2, col, 0.6 * tp + 0.1 * (pn + pp))
        grid.put(part, 3, col, 0.6 * tq + 0.1 * (qn + qp))
        grid.put(part, 4, col, -0.5 * (pn - pp))
        grid.put(part, 5, col, SIN_SLOPE * th - u * along - w * tp - 0.5 * (fn - fp))
        grid.put(part, 6, col, -v * along - w * tq - 0.5 * (gn - gp))

    grid.sweep(second)

def tangent_end(ends_of, part, work, tan):
    groups, cols = part.shape[1], part.shape[2] - 4 * TILE
    grid = Grid(groups, cols)
    ends = ends_of()

    def third(t, col):
        keep = grid.inside(t, ends)
        hn, hp = grid.both_cols(work, 0, col)
        pn, pp = grid.both_cols(work, 1, col)
        qn, qp = grid.both_cols(work, 2, col)
        gn, gp = grid.both_cols(work, 3, col)
        fn, fp = grid.both_cols(work, 4, col)
        grid.put(tan, 0, col, grid.get(part, 0, col))
        for k, (n, p) in enumerate(((hn, hp), (pn, pp), (qn, qp))):
            grid.put(tan, 1 + k, col, jnp.where(keep, grid.get(part, 1 + k, col) + 0.1 * (n + p), 0.0))
        for k, (n, p) in enumerate(((qn, qp), (gn, gp), (fn, fp))):
            grid.put(tan, 4 + k, col, jnp.where(keep, grid.get(part, 4 + k, col) - 0.5 * (n - p), 0.0))

    grid.sweep(third)

def regularize(ext, smooth, work):
    groups, cols = ext.shape[1], ext.shape[2] - 4 * TILE
    grid = Grid(groups, cols)

    def laplace(ref, k, col):
        value = grid.get(ref, k, col)
        rn, rp = grid.both_rows(value)
        cn, cp = grid.both_cols(ref, k, col)
        return 4.0 * value - rn - rp - cn - cp

    def bend(t, col):
        weight = grid.get(ext, WR, col)
        for k, field in enumerate((DM, DX)):
            grid.put(work, k, col, weight * laplace(ext, field, col))

    grid.sweep(bend)

    def bend_again(t, col):
        for k in range(2):
            grid.put(smooth, k, col, laplace(work, k, col))

    grid.sweep(bend_again, 1, grid.tiles - 1)


def finish(ends_of, cells, top, top_last, fast, fast_last, ext, base, at_one, tan, at_mid, smooth, out_mu, out_xi, work, total):
    groups, cols = ext.shape[1], ext.shape[2] - 4 * TILE
    grid = Grid(groups, cols)
    ends = ends_of()
    shape = grid.lane.shape
    dt0 = COURANT / jnp.broadcast_to(jnp.maximum(top[...], top_last[...]), shape)
    dt1 = COURANT / jnp.broadcast_to(jnp.maximum(fast[0:1, :], fast_last[0:1, :]), shape)
    weight = jnp.broadcast_to((DATA_WEIGHT * cells) / (fast[1:2, :] + fast_last[1:2, :]), shape)
    half1 = 0.5 * dt1
    half0 = 0.5 * dt0

    def end(t, col):
        def section(k, off):
            return grid.get(tan, 1 + k, col + off) + dt1 * grid.get(tan, 4 + k, col + off)

        th, tp = section(0, 0), section(1, 0)
        tenth, moved = 0.1 * th, half1 * tp
        value = grid.get(tan, 0, col) + 0.6 * th + grid.rows_next(tenth - moved) + grid.rows_prev(tenth + moved)
        value += 0.1 * (section(0, 1) + section(0, -1)) - half1 * (section(2, 1) - section(2, -1))
        grid.put(work, 0, col, weight * grid.get(ext, OB, col) * (0.5 * value))

    grid.sweep(end)

    def back_second(t, col):
        keep = grid.inside(t, ends)
        seed = grid.get(work, 0, col)
        rn, rp = grid.both_rows(seed)
        cn, cp = grid.both_cols(work, 0, col)
        zero = jnp.zeros_like(seed)
        grid.put(work, 1, col, jnp.where(keep, 0.3 * seed + 0.05 * (rn + rp + cn + cp), zero))
        grid.put(work, 2, col, jnp.where(keep, 0.5 * half1 * (rn - rp), zero))
        grid.put(work, 3, col, jnp.where(keep, 0.5 * half1 * (cn - cp), zero))

    grid.sweep(back_second)

    def back_first(t, col):
        keep = grid.inside(t, ends)
        g0, g1, g2 = (grid.get(work, 1 + k, col) for k in range(3))
        r0n, r0p = grid.both_rows(g0)
        r1n, r1p = grid.both_rows(g1)
        r2n, r2p = grid.both_rows(g2)
        c0n, c0p = grid.both_cols(work, 1, col)
        c1n, c1p = grid.both_cols(work, 2, col)
        c2n, c2p = grid.both_cols(work, 3, col)
        u, v = grid.get(at_mid, MU, col), grid.get(at_mid, MV, col)
        z, w = grid.get(at_mid, MZ, col), grid.get(at_mid, MW, col)
        down = half1 * (r1n - r1p)
        cross = half1 * ((r2n - r2p) + (c1n - c1p))
        side = half1 * (c2n - c2p)
        h1, h2 = dt1 * g1, dt1 * g2
        along = u * h1 + v * h2
        grid.put(total, 0, col, grid.get(smooth, 0, col) - grid.get(at_mid, ME, col) * along)
        grid.put(total, 1, col, grid.get(smooth, 1, col) + grid.get(at_mid, MB, col) * along)
        pull = z * along
        part_u = u * down + v * cross
        part_v = v * side
        m0 = 0.5 * grid.get(work, 0, col) + 0.6 * g0 + 0.1 * (r0n + r0p + c0n + c0p)
        m0 += SIN_SLOPE * h1 - grid.get(at_mid, MY, col) * along + grid.get(at_mid, MH, col) * (down + side)
        m0 -= grid.get(at_mid, MM, col) * (u * part_u + v * part_v)
        m1 = 0.6 * g1 + 0.1 * (r1n + r1p + c1n + c1p)
        m1 += half1 * (r0n - r0p) + 2.0 * u * down + v * cross - u * pull - w * h1
        m2 = 0.6 * g2 + 0.1 * (r2n + r2p + c2n + c2p)
        m2 += half1 * (c0n - c0p) + u * cross + 2.0 * v * side - v * pull - w * h2
        for k, value in enumerate((m0, m1, m2)):
            grid.put(work, 4 + k, col, jnp.where(keep, value, 0.0))

    grid.sweep(back_first)

    def early(t, col):
        m0, m1, m2 = (grid.get(work, 4 + k, col) for k in range(3))
        r0n, r0p = grid.both_rows(m0)
        r1n, r1p = grid.both_rows(m1)
        r2n, r2p = grid.both_rows(m2)
        c0n, c0p = grid.both_cols(work, 4, col)
        c1n, c1p = grid.both_cols(work, 5, col)
        c2n, c2p = grid.both_cols(work, 6, col)
        u, v = grid.get(at_one, CU, col), grid.get(at_one, CV, col)
        z, w = grid.get(at_one, CZ, col), grid.get(at_one, CW, col)
        quarter = 0.5 * half0
        down = quarter * (r1n - r1p)
        cross = quarter * ((r2n - r2p) + (c1n - c1p))
        side = quarter * (c2n - c2p)
        p1, p2 = half0 * m1, half0 * m2
        along = u * p1 + v * p2
        pull = z * along
        f1 = 0.3 * m1 + 0.05 * (r1n + r1p + c1n + c1p)
        f1 += quarter * (r0n - r0p) + 2.0 * u * down + v * cross - u * pull - w * p1
        f2 = 0.3 * m2 + 0.05 * (r2n + r2p + c2n + c2p)
        f2 += quarter * (c0n - c0p) + u * cross + 2.0 * v * side - v * pull - w * p2
        start = dt0 * (grid.get(base, 0, col) * f1 + grid.get(base, 1, col) * f2)
        mu = grid.get(total, 0, col) - grid.get(at_one, CE, col) * along - grid.get(base, 2, col) * start
        xi = grid.get(total, 1, col) + grid.get(at_one, CB, col) * along + grid.get(base, 3, col) * start
        grid.put(total, 0, col, mu)
        grid.put(total, 1, col, xi)

    grid.sweep(early, 1, grid.tiles - 1)

    for g in range(groups):
        at = pl.ds(g * LANES, LANES)
        out_mu[at, :] = total[0, g, 2 * TILE : 2 * TILE + cols, :].T
        out_xi[at, :] = total[1, g, 2 * TILE : 2 * TILE + cols, :].T


VMEM = pl.BlockSpec(memory_space=pltpu.VMEM)
ANY = pl.BlockSpec(memory_space=pltpu.HBM)


def call(body, name, operands, outs, scratch, flops, spaces=None):
    outs = [jax.ShapeDtypeStruct(shape, jnp.float32) for shape in outs]
    moved = 4 * sum(x.size for x in operands) + 4 * sum(x.size for x in outs)
    return pl.pallas_call(
        body,
        name=name,
        out_shape=outs,
        in_specs=spaces or [VMEM] * len(operands),
        out_specs=[VMEM] * len(outs),
        scratch_shapes=[pltpu.VMEM(x, jnp.float32) if isinstance(x, tuple) else x for x in scratch],
        compiler_params=pltpu.CompilerParams(vmem_limit_bytes=24 * 1024 * 1024),
        cost_estimate=pl.CostEstimate(flops=flops, bytes_accessed=moved, transcendentals=0),
    )(*operands)


def swap_edges(edge_a, edge_b, count):
    pairs_a = [(i, i ^ 1) for i in range(count)]
    pairs_b = [(i, i - 1 if i % 2 == 0 else i + 1) for i in range(1, count - 1)]
    return lax.ppermute(edge_a, "cross", pairs_a), lax.ppermute(edge_b, "cross", pairs_b)


def exchange(row, step):
    return lax.ppermute(row, "cross", [(i, i ^ step) for i in range(lax.axis_size("cross"))])


def share(row, combine, first=1):
    step = first
    while 2 * step < lax.axis_size("cross"):
        row = combine(row, exchange(row, step))
        step *= 2
    return row, exchange(row, step)


def round_beside(row, step, result):
    arrived, result = lax.optimization_barrier((exchange(row, step), result))
    return max_and_sum(row, arrived), result


def max_and_sum(a, b):
    return jnp.where(lax.broadcasted_iota(jnp.int32, a.shape, 0) == 0, jnp.maximum(a, b), a + b)


def local(state, log_mu, log_xi, dir_mu, dir_xi, wet, observed, terrain, class_weight):
    rows, cols = log_mu.shape
    groups = rows // LANES
    count = lax.axis_size("cross")
    cells = rows * cols * count
    wide = (groups, cols + 4 * TILE, LANES)
    edge = (FIELDS, groups, TILE, LANES)
    work = rows * cols

    inputs = (state, log_mu, log_xi, dir_mu, dir_xi, wet, observed, terrain, class_weight)
    inputs = tuple(pltpu.with_memory_space_constraint(x, pltpu.HBM) for x in inputs)
    (row,) = call(
        first_speed,
        "first_speed",
        inputs[:1],
        [(1, LANES)],
        [pltpu.VMEM((4, 3, rows // 4, cols), jnp.float32), pltpu.SemaphoreType.DMA((4,))],
        20 * work,
        spaces=(ANY,),
    )
    row = jnp.maximum(row, exchange(row, 1))
    own, edge_a, edge_b, count_row = call(
        prepare,
        "prepare",
        inputs + (row,),
        [(FIELDS, groups, cols, LANES), edge, edge, (1, LANES)],
        [(rows, cols), (3, groups, cols, LANES)]
        + [pltpu.VMEM(x.shape, x.dtype) for x in inputs[:-1]]
        + [pltpu.SMEM(class_weight.shape, jnp.float32), pltpu.SemaphoreType.DMA((len(inputs),))],
        100 * work,
        spaces=(ANY,) * 9 + (VMEM,),
    )
    row = jnp.maximum(row, exchange(row, 2))
    row, edge_a, edge_b = lax.optimization_barrier((row, edge_a, edge_b))
    edge_a, edge_b = swap_edges(edge_a, edge_b, count)
    top, top_last = share(row, jnp.maximum, 4)
    ext, xy, base = call(
        open_step, "open_step", (own, edge_a, edge_b), [(FIELDS,) + wide, (8,) + wide, (6,) + wide], [], 100 * work
    )
    at_one, mid, next_row = call(
        functools.partial(middle, end_flags),
        "middle",
        (top, top_last, ext, xy, count_row),
        [(7,) + wide, (3,) + wide, (2, LANES)],
        [(5,) + wide],
        120 * work,
    )
    (smooth,) = call(regularize, "regularize", (ext,), [(2,) + wide], [(2,) + wide], 30 * work)
    fast, smooth = round_beside(next_row, 1, smooth)
    (one,) = call(tangent_one, "tangent_one", (top, top_last, xy, at_one), [(7,) + wide], [], 60 * work)
    fast, one = round_beside(fast, 2, one)
    part, at_mid, between = call(
        functools.partial(tangent_mid, end_flags),
        "tangent_mid",
        (top, top_last, ext, one, mid),
        [(7,) + wide, (9,) + wide, (5,) + wide],
        [],
        120 * work,
    )
    fast, part = round_beside(fast, 4, part)
    (tan,) = call(
        functools.partial(tangent_end, end_flags), "tangent_end", (part, between), [(7,) + wide], [], 30 * work
    )
    fast, fast_last = share(fast, max_and_sum, 8)
    out_mu, out_xi = call(
        functools.partial(finish, end_flags, float(cells)),
        "finish",
        (top, top_last, fast, fast_last, ext, base, at_one, tan, at_mid, smooth),
        [(rows, cols), (rows, cols)],
        [(7,) + wide, (2,) + wide],
        200 * work,
    )
    return out_mu, out_xi


def solution(mesh):
    return jax.shard_map(
        local,
        mesh=mesh,
        in_specs=(
            P(None, "grp", "cross"),
            P("grp", "cross"),
            P("grp", "cross"),
            P("grp", "cross"),
            P("grp", "cross"),
            P("grp", "cross"),
            P("grp", "cross"),
            P("grp", "cross"),
            P(),
        ),
        out_specs=(P("grp", "cross"), P("grp", "cross")),
        check_vma=False,
    )
```

```python
import functools

import jax
import jax.numpy as jnp
from jax import lax
from jax.experimental import pallas as pl
from jax.experimental.pallas import tpu as pltpu
from jax.sharding import PartitionSpec as P

COS_SLOPE = 0.8
SIN_SLOPE = 0.6
DEPTH_FLOOR = 0.05
SPEED_EPS = 0.01
COURANT = 0.2
DATA_WEIGHT = 100000.0

LANES = 128
TILE = 8
H, Q1, Q2, FA, FB, DM, DX, OB, WR = range(9)
KEPT = 8
SHARED = 9
UNROLL = 6


class Grid:
    def __init__(self, groups, wide):
        self.groups = groups
        self.tiles = wide // TILE
        self.lane = lax.broadcasted_iota(jnp.int32, (groups * TILE, LANES), 1)
        self.blank = jnp.zeros((TILE, LANES), jnp.float32)
        me = lax.axis_index("cross")
        self.ends = (me == 0, me == lax.axis_size("cross") - 1)

    def rows_next(self, v):
        turned = pltpu.roll(v, LANES - 1, 1)
        after = jnp.concatenate([turned[TILE:], self.blank], axis=0)
        return jnp.where(self.lane == LANES - 1, after, turned)

    def rows_prev(self, v):
        turned = pltpu.roll(v, 1, 1)
        before = jnp.concatenate([self.blank, turned[:-TILE]], axis=0)
        return jnp.where(self.lane == 0, before, turned)

    def both_rows(self, v):
        return self.rows_next(v), self.rows_prev(v)

    def get(self, ref, k, col):
        return jnp.concatenate([ref[k, g, pl.ds(col, TILE), :] for g in range(self.groups)], axis=0)

    def put(self, ref, k, col, value):
        for g in range(self.groups):
            ref[k, g, pl.ds(col, TILE), :] = value[g * TILE : (g + 1) * TILE]

    def spare_get(self, ref, k, col, off=0):
        return self.get(ref, k, col + TILE + off)

    def spare_put(self, ref, k, col, value):
        self.put(ref, k, col + TILE, value)

    def both_cols(self, ref, k, col):
        return self.spare_get(ref, k, col, 1), self.spare_get(ref, k, col, -1)

    def sweep(self, body, first=0, last=None, carry=None):
        last = self.tiles if last is None else last
        steps, rest = divmod(last - first, UNROLL)

        def visit(t, col, carry):
            return body(t, col) if carry is None else body(t, col, carry)

        def step(i, carry):
            for u in range(UNROLL):
                t = first + i * UNROLL + u
                carry = visit(t, pl.multiple_of(t * TILE, TILE), carry)
            return carry

        carry = lax.fori_loop(0, steps, step, carry)
        for t in range(last - rest, last):
            carry = visit(t, t * TILE, carry)
        return carry

    def sweep_own(self, body):
        self.sweep(body, 1, self.tiles - 1)

    def inside(self, t):
        return jnp.logical_not(((t == 0) & self.ends[0]) | ((t == self.tiles - 1) & self.ends[1]))


def speed_of(height, down, across):
    inv = 1.0 / jnp.maximum(height, DEPTH_FLOOR)
    vel_down = down * inv
    vel_across = across * inv
    return jnp.sqrt(vel_down * vel_down + vel_across * vel_across) + jnp.sqrt(COS_SLOPE * jnp.maximum(height, 0.0))


def velocities(height, down, across):
    inv = 1.0 / jnp.maximum(height, DEPTH_FLOOR)
    return inv, down * inv, across * inv


def friction(height, vel_down, vel_across, dry, turbulent):
    squared = vel_down * vel_down + vel_across * vel_across + SPEED_EPS
    inv_speed = lax.rsqrt(squared)
    return inv_speed, dry * height * inv_speed, turbulent * (squared * inv_speed)


def step_length(rows, shape):
    return COURANT / jnp.broadcast_to(jnp.max(rows[...], axis=0, keepdims=True), shape)


def prepare(*refs):
    sources = refs[:9]
    kept, weights, edge_a, edge_b, row, count_row, code, turned = refs[9:17]
    held, arrived = refs[17:26], refs[26]
    copies = [pltpu.make_async_copy(src, dst, arrived.at[i]) for i, (src, dst) in enumerate(zip(sources, held))]
    for i in (0, 6, 5, 7, 3, 4, 1, 2, 8):
        copies[i].start()
    state, log_mu, log_xi, dir_mu, dir_xi, wet, observed, terrain, class_weight = held
    rows, cols = log_mu.shape
    groups = rows // LANES
    own = pl.ds(TILE, cols)

    copies[0].wait()
    top = jnp.zeros((16, cols), jnp.float32)
    for i in range(0, rows, 16):
        top = jnp.maximum(top, speed_of(*(state[k, i : i + 16, :] for k in range(3))))
    row[...] = jnp.full(row.shape, jnp.max(top), jnp.float32)
    for g in range(groups):
        for k in range(3):
            kept[k, g, own, :] = state[k, pl.ds(g * LANES, LANES), :].T

    for i in (6, 5, 7):
        copies[i].wait()
    seen = jnp.zeros((16, cols), jnp.float32)
    for i in range(0, rows, 16):
        seen_here = observed[i : i + 16, :]
        code[i : i + 16, :] = (wet[i : i + 16, :] + 2 * seen_here + 4 * terrain[i : i + 16, :]).astype(jnp.float32)
        seen += seen_here.astype(jnp.float32)
    count_row[...] = jnp.full(count_row.shape, jnp.sum(seen), jnp.float32)

    for i in (3, 4, 1, 2, 8):
        copies[i].wait()
    for g in range(groups):
        at = pl.ds(g * LANES, LANES)
        turned[2, g] = code[at, :].T
        kept[DM, g, own, :] = dir_mu[at, :].T
        kept[DX, g, own, :] = dir_xi[at, :].T
        turned[0, g] = log_mu[at, :].T
        turned[1, g] = log_xi[at, :].T

    def derive(i, carry):
        for g, half in ((g, half) for g in range(groups) for half in range(2)):
            at = pl.ds(pl.multiple_of((2 * i + half) * TILE, TILE), TILE)
            to = pl.ds(pl.multiple_of((2 * i + half + 1) * TILE, TILE), TILE)
            bits = turned[2, g, at, :].astype(jnp.int32)
            wet_here = (bits & 1).astype(jnp.float32)
            kind = bits >> 2
            kept[FA, g, to, :] = wet_here * jnp.exp(turned[0, g, at, :]) * COS_SLOPE
            kept[FB, g, to, :] = wet_here * jnp.exp(-turned[1, g, at, :])
            kept[OB, g, to, :] = ((bits >> 1) & 1).astype(jnp.float32)
            weight = jnp.zeros((TILE, LANES), jnp.float32)
            for c in range(class_weight.shape[0]):
                weight = jnp.where(kind == c, class_weight[c], weight)
            weights[0, g, to, :] = weight
        return carry

    lax.fori_loop(0, cols // (2 * TILE), derive, 0)
    even = lax.rem(lax.axis_index("cross"), 2) == 0
    for k in range(SHARED):
        ref, j = (kept, k) if k < KEPT else (weights, 0)
        for g in range(groups):
            left = ref[j, g, TILE : 2 * TILE, :]
            right = ref[j, g, cols : cols + TILE, :]
            edge_a[k, g] = jnp.where(even, right, left)
            edge_b[k, g] = jnp.where(even, left, right)


def fill_halo(source, ref, j, k, edge_a, edge_b):
    even = lax.rem(lax.axis_index("cross"), 2) == 0
    wide = ref.shape[2]
    for g in range(ref.shape[1]):
        ref[j, g, TILE : wide - TILE, :] = source[j, g, TILE : wide - TILE, :]
        ref[j, g, :TILE, :] = jnp.where(even, edge_b[k, g], edge_a[k, g])
        ref[j, g, wide - TILE :, :] = jnp.where(even, edge_a[k, g], edge_b[k, g])


def open_step(kept_in, weights_in, edge_a, edge_b, kept, weights, xy, change, work):
    grid = Grid(kept.shape[1], kept.shape[2])
    for k in range(KEPT):
        fill_halo(kept_in, kept, k, k, edge_a, edge_b)
    fill_halo(weights_in, weights, 0, WR, edge_a, edge_b)

    def first(t, col):
        height, down, across = (grid.get(kept, k, col) for k in (H, Q1, Q2))
        _, u, v = velocities(height, down, across)
        _, dry, turb = friction(height, u, v, grid.get(kept, FA, col), grid.get(kept, FB, col))
        moved = dry * grid.get(kept, DM, col) - turb * grid.get(kept, DX, col)
        grid.put(change, 0, col, -u * moved)
        grid.put(change, 1, col, -v * moved)
        drag = dry + turb
        pressure = 0.5 * COS_SLOPE * height * height
        mixed = down * v
        for k, value in enumerate((height, down, across, mixed, across * v + pressure)):
            grid.spare_put(work, k, col, value)
        hn, hp = grid.both_rows(height)
        pn, pp = grid.both_rows(down)
        qn, qp = grid.both_rows(across)
        fn, fp = grid.both_rows(down * u + pressure)
        gn, gp = grid.both_rows(mixed)
        grid.put(xy, 0, col, 0.6 * height + 0.1 * (hn + hp))
        grid.put(xy, 1, col, 0.6 * down + 0.1 * (pn + pp))
        grid.put(xy, 2, col, 0.6 * across + 0.1 * (qn + qp))
        grid.put(xy, 3, col, -0.5 * (pn - pp))
        grid.put(xy, 4, col, SIN_SLOPE * height - drag * u - 0.5 * (fn - fp))
        grid.put(xy, 5, col, -drag * v - 0.5 * (gn - gp))

    grid.sweep(first)

    def second(t, col):
        hn, hp = grid.both_cols(work, 0, col)
        pn, pp = grid.both_cols(work, 1, col)
        qn, qp = grid.both_cols(work, 2, col)
        gn, gp = grid.both_cols(work, 3, col)
        fn, fp = grid.both_cols(work, 4, col)
        for k, (n, p) in enumerate(((hn, hp), (pn, pp), (qn, qp))):
            grid.put(xy, k, col, grid.get(xy, k, col) + 0.1 * (n + p))
        for k, (n, p) in enumerate(((qn, qp), (gn, gp), (fn, fp))):
            grid.put(xy, 3 + k, col, grid.get(xy, 3 + k, col) - 0.5 * (n - p))

    grid.sweep(second)


CU, CV, CZ, CW, CE, CB = range(6)
MU, MV, MZ, MW, ME, MB, MM, MH, MY = range(9)


def middle(top_rows, kept, xy, count_row, at_one, mid, row, work):
    grid = Grid(kept.shape[1], kept.shape[2])
    dt = step_length(top_rows, grid.lane.shape)
    half = 0.5 * dt

    def first(t, col):
        keep = grid.inside(t)
        height, down, across = (
            jnp.where(keep, grid.get(xy, k, col) + dt * grid.get(xy, 3 + k, col), 0.0) for k in range(3)
        )
        inv, u, v = velocities(height, down, across)
        turb_of = grid.get(kept, FB, col)
        inv_speed, dry, turb = friction(height, u, v, grid.get(kept, FA, col), turb_of)
        drag = dry + turb
        grid.put(at_one, CU, col, u)
        grid.put(at_one, CV, col, v)
        grid.put(at_one, CZ, col, (turb_of - dry * inv_speed) * inv_speed * inv)
        grid.put(at_one, CW, col, drag * inv)
        grid.put(at_one, CE, col, dry)
        grid.put(at_one, CB, col, turb)
        pressure = 0.5 * COS_SLOPE * height * height
        mixed = down * v
        for k, value in enumerate((height, down, across, mixed, across * v + pressure)):
            grid.spare_put(work, k, col, value)
        sources = (0.0, dt * (SIN_SLOPE * height - drag * u), -dt * drag * v)
        for k, (value, flux) in enumerate(((height, down), (down, down * u + pressure), (across, mixed))):
            tenth, moved = 0.1 * value, half * flux
            total = grid.get(kept, k, col) + 0.6 * value + sources[k]
            total += grid.rows_next(tenth - moved) + grid.rows_prev(tenth + moved)
            grid.put(mid, k, col, total)

    grid.sweep(first)

    def second(t, col, most):
        keep = grid.inside(t)
        found = []
        for k, (value, flux) in enumerate(((0, 2), (1, 3), (2, 4))):
            vn, vp = grid.both_cols(work, value, col)
            fn, fp = grid.both_cols(work, flux, col)
            total = grid.get(mid, k, col) + 0.1 * (vn + vp) - half * (fn - fp)
            found.append(jnp.where(keep, 0.5 * total, 0.0))
            grid.put(mid, k, col, found[k])
        own = (t > 0) & (t < grid.tiles - 1)
        return jnp.maximum(most, jnp.where(own, speed_of(*found), 0.0))

    fastest = grid.sweep(second, carry=jnp.zeros(grid.lane.shape, jnp.float32))
    lane = lax.broadcasted_iota(jnp.int32, row.shape, 1)
    count = jnp.broadcast_to(count_row[...], row.shape)
    row[...] = jnp.where(lane < LANES // 2, jnp.full(row.shape, jnp.max(fastest), jnp.float32), count)


def between(top_rows, kept, weights, change, at_one, smooth, tan, work, bent):
    grid = Grid(kept.shape[1], kept.shape[2])
    dt = step_length(top_rows, grid.lane.shape)
    half = 0.5 * dt

    def first(t, col):
        tp, tq = dt * grid.get(change, 0, col), dt * grid.get(change, 1, col)
        u, v = grid.get(at_one, CU, col), grid.get(at_one, CV, col)
        w = grid.get(at_one, CW, col)
        moved = grid.get(at_one, CE, col) * grid.get(kept, DM, col) - grid.get(at_one, CB, col) * grid.get(kept, DX, col)
        along = grid.get(at_one, CZ, col) * (u * tp + v * tq) + moved
        mixed = v * tp + u * tq
        for k, value in enumerate((tp, tq, mixed, 2.0 * v * tq)):
            grid.spare_put(work, k, col, value)
        for k, field in enumerate((DM, DX)):
            grid.spare_put(bent, k, col, grid.get(kept, field, col))
        moved = half * tp
        grid.put(tan, 0, col, grid.rows_prev(moved) - grid.rows_next(moved))
        sources = (-dt * (u * along + w * tp), -dt * (v * along + w * tq))
        for k, (value, flux) in enumerate(((tp, 2.0 * u * tp), (tq, mixed))):
            tenth, moved = 0.1 * value, half * flux
            total = 0.6 * value + sources[k]
            total += grid.rows_next(tenth - moved) + grid.rows_prev(tenth + moved)
            grid.put(tan, 1 + k, col, total)

    grid.sweep(first)

    def laplace(k, col):
        value = grid.spare_get(bent, k, col)
        rn, rp = grid.both_rows(value)
        cn, cp = grid.both_cols(bent, k, col)
        return 4.0 * value - rn - rp - cn - cp

    def second(t, col):
        keep = grid.inside(t)
        qn, qp = grid.both_cols(work, 1, col)
        pn, pp = grid.both_cols(work, 0, col)
        gn, gp = grid.both_cols(work, 2, col)
        fn, fp = grid.both_cols(work, 3, col)
        th = grid.get(tan, 0, col) - half * (qn - qp)
        tp = grid.get(tan, 1, col) + 0.1 * (pn + pp) - half * (gn - gp)
        tq = grid.get(tan, 2, col) + 0.1 * (qn + qp) - half * (fn - fp)
        for k, value in enumerate((th, tp, tq)):
            grid.put(tan, k, col, jnp.where(keep, 0.5 * value, 0.0))
        weight = grid.get(weights, 0, col)
        for k in range(2):
            grid.spare_put(bent, 2 + k, col, weight * laplace(k, col))

    grid.sweep(second)

    def third(t, col):
        for k in range(2):
            grid.put(smooth, k, col - TILE, laplace(2 + k, col))

    grid.sweep_own(third)


def finish(cells, top_rows, next_rows, kept, at_one, mid, tan, smooth, out_mu, out_xi, at_mid, end, work, total):
    grid = Grid(kept.shape[1], kept.shape[2])
    shape = grid.lane.shape
    dt0 = step_length(top_rows, shape)
    rows = next_rows[...]
    lane = lax.broadcasted_iota(jnp.int32, (1, LANES), 1)
    most = jnp.max(rows, axis=0, keepdims=True)
    added = jnp.sum(rows, axis=0, keepdims=True)
    dt1 = COURANT / jnp.broadcast_to(jnp.where(lane < LANES // 2, most, pltpu.roll(most, LANES // 2, 1)), shape)
    count = jnp.where(lane < LANES // 2, pltpu.roll(added, LANES // 2, 1), added)
    weight = jnp.broadcast_to((DATA_WEIGHT * cells) / count, shape)
    half1 = 0.5 * dt1
    half0 = 0.5 * dt0

    def open_end(t, col):
        th, tp, tq = (grid.get(tan, k, col) for k in range(3))
        height, down, across = (grid.get(mid, k, col) for k in range(3))
        inv, u, v = velocities(height, down, across)
        above = jnp.where(height > DEPTH_FLOOR, 1.0, jnp.where(height == DEPTH_FLOOR, 0.5, 0.0))
        turb_of = grid.get(kept, FB, col)
        dry_of = grid.get(kept, FA, col)
        inv_speed, dry, turb = friction(height, u, v, dry_of, turb_of)
        z = (turb_of - dry * inv_speed) * inv_speed * inv
        w = (dry + turb) * inv
        y = dry_of * inv_speed - above * (z * (u * u + v * v) + w)
        eight = COS_SLOPE * height
        for k, value in ((MU, u), (MV, v), (MZ, z), (MW, w), (ME, dry), (MB, turb), (MM, above), (MH, eight), (MY, y)):
            grid.put(at_mid, k, col, value)
        along = z * (u * tp + v * tq) + y * th
        along += dry * grid.get(kept, DM, col) - turb * grid.get(kept, DX, col)
        lift = above * th
        flux_down = 2.0 * u * tp + eight * th - u * u * lift
        mixed = v * tp + u * tq - u * v * lift
        for k, value in enumerate((th, tp, tq, mixed, 2.0 * v * tq + eight * th - v * v * lift)):
            grid.spare_put(work, k, col, value)
        tenths = (0.1 * th, 0.1 * tp, 0.1 * tq)
        moves = (half1 * tp, half1 * flux_down, half1 * mixed)
        sources = (0.0, dt1 * (SIN_SLOPE * th - u * along - w * tp), -dt1 * (v * along + w * tq))
        for k, value in enumerate((th, tp, tq)):
            total_k = 0.6 * value + sources[k]
            total_k += grid.rows_next(tenths[k] - moves[k]) + grid.rows_prev(tenths[k] + moves[k])
            grid.spare_put(end, k, col, total_k)

    grid.sweep(open_end)

    def close_end(t, col):
        keep = grid.inside(t)
        for k, (value, flux) in enumerate(((0, 2), (1, 3), (2, 4))):
            vn, vp = grid.both_cols(work, value, col)
            fn, fp = grid.both_cols(work, flux, col)
            found = grid.spare_get(end, k, col) + 0.1 * (vn + vp) - half1 * (fn - fp)
            grid.spare_put(end, k, col, jnp.where(keep, found, 0.0))

    grid.sweep(close_end)

    def seed_end(t, col):
        th, tp = grid.spare_get(end, 0, col), grid.spare_get(end, 1, col)
        tenth, moved = 0.1 * th, half1 * tp
        hn, hp = grid.both_cols(end, 0, col)
        qn, qp = grid.both_cols(end, 2, col)
        value = grid.get(tan, 0, col) + 0.6 * th + grid.rows_next(tenth - moved) + grid.rows_prev(tenth + moved)
        value += 0.1 * (hn + hp) - half1 * (qn - qp)
        grid.spare_put(work, 0, col, weight * grid.get(kept, OB, col) * (0.5 * value))

    grid.sweep(seed_end)

    def back_second(t, col):
        keep = grid.inside(t)
        seed = grid.spare_get(work, 0, col)
        rn, rp = grid.both_rows(seed)
        cn, cp = grid.both_cols(work, 0, col)
        grid.spare_put(work, 1, col, jnp.where(keep, 0.3 * seed + 0.05 * (rn + rp + cn + cp), 0.0))
        grid.spare_put(work, 2, col, jnp.where(keep, 0.5 * half1 * (rn - rp), 0.0))
        grid.spare_put(work, 3, col, jnp.where(keep, 0.5 * half1 * (cn - cp), 0.0))

    grid.sweep(back_second)

    def back_first(t, col):
        keep = grid.inside(t)
        g0, g1, g2 = (grid.spare_get(work, 1 + k, col) for k in range(3))
        r0n, r0p = grid.both_rows(g0)
        r1n, r1p = grid.both_rows(g1)
        r2n, r2p = grid.both_rows(g2)
        c0n, c0p = grid.both_cols(work, 1, col)
        c1n, c1p = grid.both_cols(work, 2, col)
        c2n, c2p = grid.both_cols(work, 3, col)
        u, v = grid.get(at_mid, MU, col), grid.get(at_mid, MV, col)
        z, w = grid.get(at_mid, MZ, col), grid.get(at_mid, MW, col)
        down = half1 * (r1n - r1p)
        cross = half1 * ((r2n - r2p) + (c1n - c1p))
        side = half1 * (c2n - c2p)
        h1, h2 = dt1 * g1, dt1 * g2
        along = u * h1 + v * h2
        grid.put(total, 0, col, -grid.get(at_mid, ME, col) * along)
        grid.put(total, 1, col, grid.get(at_mid, MB, col) * along)
        pull = z * along
        part_u = u * down + v * cross
        part_v = v * side
        m0 = 0.5 * grid.spare_get(work, 0, col) + 0.6 * g0 + 0.1 * (r0n + r0p + c0n + c0p)
        m0 += SIN_SLOPE * h1 - grid.get(at_mid, MY, col) * along + grid.get(at_mid, MH, col) * (down + side)
        m0 -= grid.get(at_mid, MM, col) * (u * part_u + v * part_v)
        m1 = 0.6 * g1 + 0.1 * (r1n + r1p + c1n + c1p)
        m1 += half1 * (r0n - r0p) + u * (down - pull) + part_u - w * h1
        m2 = 0.6 * g2 + 0.1 * (r2n + r2p + c2n + c2p)
        m2 += half1 * (c0n - c0p) + u * cross + 2.0 * part_v - v * pull - w * h2
        for k, value in enumerate((m0, m1, m2)):
            grid.spare_put(work, 4 + k, col, jnp.where(keep, value, 0.0))

    grid.sweep(back_first)

    def early(t, col):
        m0, m1, m2 = (grid.spare_get(work, 4 + k, col) for k in range(3))
        r0n, r0p = grid.both_rows(m0)
        r1n, r1p = grid.both_rows(m1)
        r2n, r2p = grid.both_rows(m2)
        c0n, c0p = grid.both_cols(work, 4, col)
        c1n, c1p = grid.both_cols(work, 5, col)
        c2n, c2p = grid.both_cols(work, 6, col)
        u, v = grid.get(at_one, CU, col), grid.get(at_one, CV, col)
        z, w = grid.get(at_one, CZ, col), grid.get(at_one, CW, col)
        quarter = 0.5 * half0
        down = quarter * (r1n - r1p)
        cross = quarter * ((r2n - r2p) + (c1n - c1p))
        side = quarter * (c2n - c2p)
        p1, p2 = half0 * m1, half0 * m2
        along = u * p1 + v * p2
        pull = z * along
        f1 = 0.3 * m1 + 0.05 * (r1n + r1p + c1n + c1p)
        f1 += quarter * (r0n - r0p) + 2.0 * u * down + v * cross - u * pull - w * p1
        f2 = 0.3 * m2 + 0.05 * (r2n + r2p + c2n + c2p)
        f2 += quarter * (c0n - c0p) + u * cross + 2.0 * v * side - v * pull - w * p2
        height, down, across = (grid.get(kept, k, col) for k in (H, Q1, Q2))
        _, u, v = velocities(height, down, across)
        _, dry, turb = friction(height, u, v, grid.get(kept, FA, col), grid.get(kept, FB, col))
        start = dt0 * (u * f1 + v * f2)
        mu = grid.get(total, 0, col) + grid.get(smooth, 0, col - TILE)
        xi = grid.get(total, 1, col) + grid.get(smooth, 1, col - TILE)
        grid.put(total, 0, col, mu - grid.get(at_one, CE, col) * along - dry * start)
        grid.put(total, 1, col, xi + grid.get(at_one, CB, col) * along + turb * start)

    grid.sweep_own(early)

    cols = out_mu.shape[1]
    for g in range(grid.groups):
        at = pl.ds(g * LANES, LANES)
        out_mu[at, :] = total[0, g, TILE : TILE + cols, :].T
        out_xi[at, :] = total[1, g, TILE : TILE + cols, :].T


VMEM = pl.BlockSpec(memory_space=pltpu.VMEM)
ANY = pl.BlockSpec(memory_space=pltpu.HBM)


def call(body, name, operands, outs, scratch, flops, spaces=None, aliases=None):
    outs = [jax.ShapeDtypeStruct(shape, jnp.float32) for shape in outs]
    moved = 4 * sum(x.size for x in operands) + 4 * sum(x.size for x in outs)
    return pl.pallas_call(
        body,
        name=name,
        out_shape=outs,
        in_specs=spaces or [VMEM] * len(operands),
        out_specs=[VMEM] * len(outs),
        scratch_shapes=[pltpu.VMEM(x, jnp.float32) if isinstance(x, tuple) else x for x in scratch],
        input_output_aliases=aliases or {},
        compiler_params=pltpu.CompilerParams(vmem_limit_bytes=24 * 1024 * 1024),
        cost_estimate=pl.CostEstimate(flops=flops, bytes_accessed=moved, transcendentals=0),
    )(*operands)


def swap_edges(edge_a, edge_b, count):
    pairs_a = [(i, i ^ 1) for i in range(count)]
    pairs_b = [(i, i - 1 if i % 2 == 0 else i + 1) for i in range(1, count - 1)]
    return lax.ppermute(edge_a, "cross", pairs_a), lax.ppermute(edge_b, "cross", pairs_b)


def share(row):
    return lax.all_to_all(row, "cross", 0, 0, tiled=True)


def local(state, log_mu, log_xi, dir_mu, dir_xi, wet, observed, terrain, class_weight):
    rows, cols = log_mu.shape
    groups = rows // LANES
    count = lax.axis_size("cross")
    own = (groups, cols, LANES)
    wide = (groups, cols + 2 * TILE, LANES)
    spare = (groups, cols + 4 * TILE, LANES)
    edge = (SHARED, groups, TILE, LANES)
    work = rows * cols

    inputs = (state, log_mu, log_xi, dir_mu, dir_xi, wet, observed, terrain, class_weight)
    inputs = tuple(pltpu.with_memory_space_constraint(x, pltpu.HBM) for x in inputs)
    kept, weights, edge_a, edge_b, row, count_row = call(
        prepare,
        "prepare",
        inputs,
        [(KEPT,) + wide, (1,) + wide, edge, edge, (count, LANES), (1, LANES)],
        [(rows, cols), (3,) + own]
        + [pltpu.VMEM(x.shape, x.dtype) for x in inputs[:-1]]
        + [pltpu.SMEM(class_weight.shape, jnp.float32), pltpu.SemaphoreType.DMA((len(inputs),))],
        100 * work,
        spaces=[ANY] * len(inputs),
    )
    edge_a, edge_b = swap_edges(edge_a, edge_b, count)
    top_rows = share(row)
    kept, weights, xy, change = call(
        open_step,
        "open_step",
        (kept, weights, edge_a, edge_b),
        [(KEPT,) + wide, (1,) + wide, (6,) + wide, (3,) + wide],
        [(5,) + spare],
        100 * work,
        aliases={0: 0, 1: 1},
    )
    at_one, mid, next_row = call(
        middle,
        "middle",
        (top_rows, kept, xy, count_row),
        [(6,) + wide, (3,) + wide, (count, LANES)],
        [(5,) + spare],
        120 * work,
    )
    next_rows = share(next_row)
    smooth, tan = call(
        between,
        "between",
        (top_rows, kept, weights, change, at_one),
        [(2,) + own, (3,) + wide],
        [(4,) + spare, (4,) + spare],
        100 * work,
        aliases={3: 1},
    )
    return call(
        functools.partial(finish, float(rows * cols * count)),
        "finish",
        (top_rows, next_rows, kept, at_one, mid, tan, smooth),
        [(rows, cols), (rows, cols)],
        [(9,) + wide, (3,) + spare, (7,) + spare, (2,) + wide],
        300 * work,
    )


def solution(mesh):
    return jax.shard_map(
        local,
        mesh=mesh,
        in_specs=(
            P(None, "grp", "cross"),
            P("grp", "cross"),
            P("grp", "cross"),
            P("grp", "cross"),
            P("grp", "cross"),
            P("grp", "cross"),
            P("grp", "cross"),
            P("grp", "cross"),
            P(),
        ),
        out_specs=(P("grp", "cross"), P("grp", "cross")),
        check_vma=False,
    )
```

```python
import functools

import jax
import jax.numpy as jnp
from jax import lax
from jax.experimental import pallas as pl
from jax.experimental.pallas import tpu as pltpu
from jax.sharding import PartitionSpec as P

COS_SLOPE = 0.8
SIN_SLOPE = 0.6
DEPTH_FLOOR = 0.05
SPEED_EPS = 0.01
COURANT = 0.2
DATA_WEIGHT = 100000.0

LANES = 128
TILE = 8
H, Q1, Q2, FA, FB, DM, DX, OB, WR = range(9)
KEPT = 8
SHARED = 9
UNROLL = 6


class Grid:
    def __init__(self, groups, wide):
        self.groups = groups
        self.tiles = wide // TILE
        self.lane = lax.broadcasted_iota(jnp.int32, (groups * TILE, LANES), 1)
        self.blank = jnp.zeros((TILE, LANES), jnp.float32)
        me = lax.axis_index("cross")
        self.ends = (me == 0, me == lax.axis_size("cross") - 1)

    def rows_next(self, v):
        turned = pltpu.roll(v, LANES - 1, 1)
        after = jnp.concatenate([turned[TILE:], self.blank], axis=0)
        return jnp.where(self.lane == LANES - 1, after, turned)

    def rows_prev(self, v):
        turned = pltpu.roll(v, 1, 1)
        before = jnp.concatenate([self.blank, turned[:-TILE]], axis=0)
        return jnp.where(self.lane == 0, before, turned)

    def both_rows(self, v):
        return self.rows_next(v), self.rows_prev(v)

    def get(self, ref, k, col):
        return jnp.concatenate([ref[k, g, pl.ds(col, TILE), :] for g in range(self.groups)], axis=0)

    def put(self, ref, k, col, value):
        for g in range(self.groups):
            ref[k, g, pl.ds(col, TILE), :] = value[g * TILE : (g + 1) * TILE]

    def spare_get(self, ref, k, col, off=0):
        return self.get(ref, k, col + TILE + off)

    def spare_put(self, ref, k, col, value):
        self.put(ref, k, col + TILE, value)

    def both_cols(self, ref, k, col):
        return self.spare_get(ref, k, col, 1), self.spare_get(ref, k, col, -1)

    def sweep(self, body, first=0, last=None, carry=None):
        last = self.tiles if last is None else last
        steps, rest = divmod(last - first, UNROLL)

        def visit(t, col, carry):
            return body(t, col) if carry is None else body(t, col, carry)

        def step(i, carry):
            for u in range(UNROLL):
                t = first + i * UNROLL + u
                carry = visit(t, pl.multiple_of(t * TILE, TILE), carry)
            return carry

        carry = lax.fori_loop(0, steps, step, carry)
        for t in range(last - rest, last):
            carry = visit(t, t * TILE, carry)
        return carry

    def sweep_own(self, body):
        self.sweep(body, 1, self.tiles - 1)

    def inside(self, t):
        return jnp.logical_not(((t == 0) & self.ends[0]) | ((t == self.tiles - 1) & self.ends[1]))


def speed_of(height, down, across):
    inv = 1.0 / jnp.maximum(height, DEPTH_FLOOR)
    vel_down = down * inv
    vel_across = across * inv
    return jnp.sqrt(vel_down * vel_down + vel_across * vel_across) + jnp.sqrt(COS_SLOPE * jnp.maximum(height, 0.0))


def velocities(height, down, across):
    inv = 1.0 / jnp.maximum(height, DEPTH_FLOOR)
    return inv, down * inv, across * inv


def friction(height, vel_down, vel_across, dry, turbulent):
    squared = vel_down * vel_down + vel_across * vel_across + SPEED_EPS
    inv_speed = lax.rsqrt(squared)
    return inv_speed, dry * height * inv_speed, turbulent * (squared * inv_speed)


def step_length(rows, shape):
    return COURANT / jnp.broadcast_to(jnp.max(rows[...], axis=0, keepdims=True), shape)


def prepare(*refs):
    sources = refs[:9]
    kept, weights, edge_a, edge_b, row, count_row, code, turned = refs[9:17]
    held, arrived = refs[17:26], refs[26]
    copies = [pltpu.make_async_copy(src, dst, arrived.at[i]) for i, (src, dst) in enumerate(zip(sources, held))]
    for i in (0, 6, 5, 7, 3, 4, 1, 2, 8):
        copies[i].start()
    state, log_mu, log_xi, dir_mu, dir_xi, wet, observed, terrain, class_weight = held
    rows, cols = log_mu.shape
    groups = rows // LANES
    own = pl.ds(TILE, cols)

    copies[0].wait()
    top = jnp.zeros((16, cols), jnp.float32)
    for i in range(0, rows, 16):
        top = jnp.maximum(top, speed_of(*(state[k, i : i + 16, :] for k in range(3))))
    row[...] = jnp.full(row.shape, jnp.max(top), jnp.float32)
    for g in range(groups):
        for k in range(3):
            kept[k, g, own, :] = state[k, pl.ds(g * LANES, LANES), :].T

    for i in (6, 5, 7):
        copies[i].wait()
    seen = jnp.zeros((16, cols), jnp.float32)
    for i in range(0, rows, 16):
        seen_here = observed[i : i + 16, :]
        code[i : i + 16, :] = (wet[i : i + 16, :] + 2 * seen_here + 4 * terrain[i : i + 16, :]).astype(jnp.float32)
        seen += seen_here.astype(jnp.float32)
    count_row[...] = jnp.full(count_row.shape, jnp.sum(seen), jnp.float32)

    for i in (3, 4, 1, 2, 8):
        copies[i].wait()
    for g in range(groups):
        at = pl.ds(g * LANES, LANES)
        turned[2, g] = code[at, :].T
        kept[DM, g, own, :] = dir_mu[at, :].T
        kept[DX, g, own, :] = dir_xi[at, :].T
        turned[0, g] = log_mu[at, :].T
        turned[1, g] = log_xi[at, :].T

    def derive(i, carry):
        for g, half in ((g, half) for g in range(groups) for half in range(2)):
            at = pl.ds(pl.multiple_of((2 * i + half) * TILE, TILE), TILE)
            to = pl.ds(pl.multiple_of((2 * i + half + 1) * TILE, TILE), TILE)
            bits = turned[2, g, at, :].astype(jnp.int32)
            wet_here = (bits & 1).astype(jnp.float32)
            kind = bits >> 2
            kept[FA, g, to, :] = wet_here * jnp.exp(turned[0, g, at, :]) * COS_SLOPE
            kept[FB, g, to, :] = wet_here * jnp.exp(-turned[1, g, at, :])
            kept[OB, g, to, :] = ((bits >> 1) & 1).astype(jnp.float32)
            weight = jnp.zeros((TILE, LANES), jnp.float32)
            for c in range(class_weight.shape[0]):
                weight = jnp.where(kind == c, class_weight[c], weight)
            weights[0, g, to, :] = weight
        return carry

    lax.fori_loop(0, cols // (2 * TILE), derive, 0)
    even = lax.rem(lax.axis_index("cross"), 2) == 0
    for k in range(SHARED):
        ref, j = (kept, k) if k < KEPT else (weights, 0)
        for g in range(groups):
            left = ref[j, g, TILE : 2 * TILE, :]
            right = ref[j, g, cols : cols + TILE, :]
            edge_a[k, g] = jnp.where(even, right, left)
            edge_b[k, g] = jnp.where(even, left, right)


def fill_halo(source, ref, j, k, edge_a, edge_b):
    even = lax.rem(lax.axis_index("cross"), 2) == 0
    wide = ref.shape[2]
    for g in range(ref.shape[1]):
        ref[j, g, TILE : wide - TILE, :] = source[j, g, TILE : wide - TILE, :]
        ref[j, g, :TILE, :] = jnp.where(even, edge_b[k, g], edge_a[k, g])
        ref[j, g, wide - TILE :, :] = jnp.where(even, edge_a[k, g], edge_b[k, g])


def open_step(kept_in, weights_in, edge_a, edge_b, kept, weights, xy, change, work):
    grid = Grid(kept.shape[1], kept.shape[2])
    for k in range(KEPT):
        fill_halo(kept_in, kept, k, k, edge_a, edge_b)
    fill_halo(weights_in, weights, 0, WR, edge_a, edge_b)

    def first(t, col):
        height, down, across = (grid.get(kept, k, col) for k in (H, Q1, Q2))
        _, u, v = velocities(height, down, across)
        _, dry, turb = friction(height, u, v, grid.get(kept, FA, col), grid.get(kept, FB, col))
        moved = dry * grid.get(kept, DM, col) - turb * grid.get(kept, DX, col)
        grid.put(change, 0, col, -u * moved)
        grid.put(change, 1, col, -v * moved)
        drag = dry + turb
        pressure = 0.5 * COS_SLOPE * height * height
        mixed = down * v
        for k, value in enumerate((height, down, across, mixed, across * v + pressure)):
            grid.spare_put(work, k, col, value)
        hn, hp = grid.both_rows(height)
        pn, pp = grid.both_rows(down)
        qn, qp = grid.both_rows(across)
        fn, fp = grid.both_rows(down * u + pressure)
        gn, gp = grid.both_rows(mixed)
        grid.put(xy, 0, col, 0.6 * height + 0.1 * (hn + hp))
        grid.put(xy, 1, col, 0.6 * down + 0.1 * (pn + pp))
        grid.put(xy, 2, col, 0.6 * across + 0.1 * (qn + qp))
        grid.put(xy, 3, col, -0.5 * (pn - pp))
        grid.put(xy, 4, col, SIN_SLOPE * height - drag * u - 0.5 * (fn - fp))
        grid.put(xy, 5, col, -drag * v - 0.5 * (gn - gp))

    grid.sweep(first)

    def second(t, col):
        hn, hp = grid.both_cols(work, 0, col)
        pn, pp = grid.both_cols(work, 1, col)
        qn, qp = grid.both_cols(work, 2, col)
        gn, gp = grid.both_cols(work, 3, col)
        fn, fp = grid.both_cols(work, 4, col)
        for k, (n, p) in enumerate(((hn, hp), (pn, pp), (qn, qp))):
            grid.put(xy, k, col, grid.get(xy, k, col) + 0.1 * (n + p))
        for k, (n, p) in enumerate(((qn, qp), (gn, gp), (fn, fp))):
            grid.put(xy, 3 + k, col, grid.get(xy, 3 + k, col) - 0.5 * (n - p))

    grid.sweep(second)


CU, CV, CZ, CW, CE, CB = range(6)
MU, MV, MZ, MW, ME, MB, MM, MH, MY = range(9)


def middle(top_rows, kept, xy, count_row, at_one, mid, row, work):
    grid = Grid(kept.shape[1], kept.shape[2])
    dt = step_length(top_rows, grid.lane.shape)
    half = 0.5 * dt

    def first(t, col):
        keep = grid.inside(t)
        height, down, across = (
            jnp.where(keep, grid.get(xy, k, col) + dt * grid.get(xy, 3 + k, col), 0.0) for k in range(3)
        )
        inv, u, v = velocities(height, down, across)
        turb_of = grid.get(kept, FB, col)
        inv_speed, dry, turb = friction(height, u, v, grid.get(kept, FA, col), turb_of)
        drag = dry + turb
        grid.put(at_one, CU, col, u)
        grid.put(at_one, CV, col, v)
        grid.put(at_one, CZ, col, (turb_of - dry * inv_speed) * inv_speed * inv)
        grid.put(at_one, CW, col, drag * inv)
        grid.put(at_one, CE, col, dry)
        grid.put(at_one, CB, col, turb)
        pressure = 0.5 * COS_SLOPE * height * height
        mixed = down * v
        for k, value in enumerate((height, down, across, mixed, across * v + pressure)):
            grid.spare_put(work, k, col, value)
        sources = (0.0, dt * (SIN_SLOPE * height - drag * u), -dt * drag * v)
        for k, (value, flux) in enumerate(((height, down), (down, down * u + pressure), (across, mixed))):
            tenth, moved = 0.1 * value, half * flux
            total = grid.get(kept, k, col) + 0.6 * value + sources[k]
            total += grid.rows_next(tenth - moved) + grid.rows_prev(tenth + moved)
            grid.put(mid, k, col, total)

    grid.sweep(first)

    def second(t, col, most):
        keep = grid.inside(t)
        found = []
        for k, (value, flux) in enumerate(((0, 2), (1, 3), (2, 4))):
            vn, vp = grid.both_cols(work, value, col)
            fn, fp = grid.both_cols(work, flux, col)
            total = grid.get(mid, k, col) + 0.1 * (vn + vp) - half * (fn - fp)
            found.append(jnp.where(keep, 0.5 * total, 0.0))
            grid.put(mid, k, col, found[k])
        own = (t > 0) & (t < grid.tiles - 1)
        return jnp.maximum(most, jnp.where(own, speed_of(*found), 0.0))

    fastest = grid.sweep(second, carry=jnp.zeros(grid.lane.shape, jnp.float32))
    lane = lax.broadcasted_iota(jnp.int32, row.shape, 1)
    count = jnp.broadcast_to(count_row[...], row.shape)
    row[...] = jnp.where(lane < LANES // 2, jnp.full(row.shape, jnp.max(fastest), jnp.float32), count)


def between(top_rows, kept, weights, change, at_one, smooth, tan, work, bent):
    grid = Grid(kept.shape[1], kept.shape[2])
    dt = step_length(top_rows, grid.lane.shape)
    half = 0.5 * dt

    def first(t, col):
        tp, tq = dt * grid.get(change, 0, col), dt * grid.get(change, 1, col)
        u, v = grid.get(at_one, CU, col), grid.get(at_one, CV, col)
        w = grid.get(at_one, CW, col)
        moved = grid.get(at_one, CE, col) * grid.get(kept, DM, col) - grid.get(at_one, CB, col) * grid.get(kept, DX, col)
        along = grid.get(at_one, CZ, col) * (u * tp + v * tq) + moved
        mixed = v * tp + u * tq
        for k, value in enumerate((tp, tq, mixed, 2.0 * v * tq)):
            grid.spare_put(work, k, col, value)
        for k, field in enumerate((DM, DX)):
            grid.spare_put(bent, k, col, grid.get(kept, field, col))
        moved = half * tp
        grid.put(tan, 0, col, grid.rows_prev(moved) - grid.rows_next(moved))
        sources = (-dt * (u * along + w * tp), -dt * (v * along + w * tq))
        for k, (value, flux) in enumerate(((tp, 2.0 * u * tp), (tq, mixed))):
            tenth, moved = 0.1 * value, half * flux
            total = 0.6 * value + sources[k]
            total += grid.rows_next(tenth - moved) + grid.rows_prev(tenth + moved)
            grid.put(tan, 1 + k, col, total)

    grid.sweep(first)

    def laplace(k, col):
        value = grid.spare_get(bent, k, col)
        rn, rp = grid.both_rows(value)
        cn, cp = grid.both_cols(bent, k, col)
        return 4.0 * value - rn - rp - cn - cp

    def second(t, col):
        keep = grid.inside(t)
        qn, qp = grid.both_cols(work, 1, col)
        pn, pp = grid.both_cols(work, 0, col)
        gn, gp = grid.both_cols(work, 2, col)
        fn, fp = grid.both_cols(work, 3, col)
        th = grid.get(tan, 0, col) - half * (qn - qp)
        tp = grid.get(tan, 1, col) + 0.1 * (pn + pp) - half * (gn - gp)
        tq = grid.get(tan, 2, col) + 0.1 * (qn + qp) - half * (fn - fp)
        for k, value in enumerate((th, tp, tq)):
            grid.put(tan, k, col, jnp.where(keep, 0.5 * value, 0.0))
        weight = grid.get(weights, 0, col)
        for k in range(2):
            grid.spare_put(bent, 2 + k, col, weight * laplace(k, col))

    grid.sweep(second)

    def third(t, col):
        for k in range(2):
            grid.put(smooth, k, col - TILE, laplace(2 + k, col))

    grid.sweep_own(third)


def finish(cells, top_rows, next_rows, kept, at_one, mid, tan, smooth, out_mu, out_xi, at_mid, end, work, total):
    grid = Grid(kept.shape[1], kept.shape[2])
    shape = grid.lane.shape
    dt0 = step_length(top_rows, shape)
    rows = next_rows[...]
    lane = lax.broadcasted_iota(jnp.int32, (1, LANES), 1)
    most = jnp.max(rows, axis=0, keepdims=True)
    added = jnp.sum(rows, axis=0, keepdims=True)
    dt1 = COURANT / jnp.broadcast_to(jnp.where(lane < LANES // 2, most, pltpu.roll(most, LANES // 2, 1)), shape)
    count = jnp.where(lane < LANES // 2, pltpu.roll(added, LANES // 2, 1), added)
    weight = jnp.broadcast_to((DATA_WEIGHT * cells) / count, shape)
    half1 = 0.5 * dt1
    half0 = 0.5 * dt0

    def open_end(t, col):
        th, tp, tq = (grid.get(tan, k, col) for k in range(3))
        height, down, across = (grid.get(mid, k, col) for k in range(3))
        inv, u, v = velocities(height, down, across)
        above = jnp.where(height > DEPTH_FLOOR, 1.0, jnp.where(height == DEPTH_FLOOR, 0.5, 0.0))
        turb_of = grid.get(kept, FB, col)
        dry_of = grid.get(kept, FA, col)
        inv_speed, dry, turb = friction(height, u, v, dry_of, turb_of)
        z = (turb_of - dry * inv_speed) * inv_speed * inv
        w = (dry + turb) * inv
        y = dry_of * inv_speed - above * (z * (u * u + v * v) + w)
        eight = COS_SLOPE * height
        for k, value in ((MU, u), (MV, v), (MZ, z), (MW, w), (ME, dry), (MB, turb), (MM, above), (MH, eight), (MY, y)):
            grid.put(at_mid, k, col, value)
        along = z * (u * tp + v * tq) + y * th
        along += dry * grid.get(kept, DM, col) - turb * grid.get(kept, DX, col)
        lift = above * th
        flux_down = 2.0 * u * tp + eight * th - u * u * lift
        mixed = v * tp + u * tq - u * v * lift
        for k, value in enumerate((th, tp, tq, mixed, 2.0 * v * tq + eight * th - v * v * lift)):
            grid.spare_put(work, k, col, value)
        tenths = (0.1 * th, 0.1 * tp, 0.1 * tq)
        moves = (half1 * tp, half1 * flux_down, half1 * mixed)
        sources = (0.0, dt1 * (SIN_SLOPE * th - u * along - w * tp), -dt1 * (v * along + w * tq))
        for k, value in enumerate((th, tp, tq)):
            total_k = 0.6 * value + sources[k]
            total_k += grid.rows_next(tenths[k] - moves[k]) + grid.rows_prev(tenths[k] + moves[k])
            grid.spare_put(end, k, col, total_k)

    grid.sweep(open_end)

    def close_end(t, col):
        keep = grid.inside(t)
        for k, (value, flux) in enumerate(((0, 2), (1, 3), (2, 4))):
            vn, vp = grid.both_cols(work, value, col)
            fn, fp = grid.both_cols(work, flux, col)
            found = grid.spare_get(end, k, col) + 0.1 * (vn + vp) - half1 * (fn - fp)
            grid.spare_put(end, k, col, jnp.where(keep, found, 0.0))

    grid.sweep(close_end)

    def seed_end(t, col):
        th, tp = grid.spare_get(end, 0, col), grid.spare_get(end, 1, col)
        tenth, moved = 0.1 * th, half1 * tp
        hn, hp = grid.both_cols(end, 0, col)
        qn, qp = grid.both_cols(end, 2, col)
        value = grid.get(tan, 0, col) + 0.6 * th + grid.rows_next(tenth - moved) + grid.rows_prev(tenth + moved)
        value += 0.1 * (hn + hp) - half1 * (qn - qp)
        grid.spare_put(work, 0, col, weight * grid.get(kept, OB, col) * (0.5 * value))

    grid.sweep(seed_end)

    def back_second(t, col):
        keep = grid.inside(t)
        seed = grid.spare_get(work, 0, col)
        rn, rp = grid.both_rows(seed)
        cn, cp = grid.both_cols(work, 0, col)
        grid.spare_put(work, 1, col, jnp.where(keep, 0.3 * seed + 0.05 * (rn + rp + cn + cp), 0.0))
        grid.spare_put(work, 2, col, jnp.where(keep, 0.5 * half1 * (rn - rp), 0.0))
        grid.spare_put(work, 3, col, jnp.where(keep, 0.5 * half1 * (cn - cp), 0.0))

    grid.sweep(back_second)

    def back_first(t, col):
        keep = grid.inside(t)
        g0, g1, g2 = (grid.spare_get(work, 1 + k, col) for k in range(3))
        r0n, r0p = grid.both_rows(g0)
        r1n, r1p = grid.both_rows(g1)
        r2n, r2p = grid.both_rows(g2)
        c0n, c0p = grid.both_cols(work, 1, col)
        c1n, c1p = grid.both_cols(work, 2, col)
        c2n, c2p = grid.both_cols(work, 3, col)
        u, v = grid.get(at_mid, MU, col), grid.get(at_mid, MV, col)
        z, w = grid.get(at_mid, MZ, col), grid.get(at_mid, MW, col)
        down = half1 * (r1n - r1p)
        cross = half1 * ((r2n - r2p) + (c1n - c1p))
        side = half1 * (c2n - c2p)
        h1, h2 = dt1 * g1, dt1 * g2
        along = u * h1 + v * h2
        grid.put(total, 0, col, -grid.get(at_mid, ME, col) * along)
        grid.put(total, 1, col, grid.get(at_mid, MB, col) * along)
        pull = z * along
        part_u = u * down + v * cross
        part_v = v * side
        m0 = 0.5 * grid.spare_get(work, 0, col) + 0.6 * g0 + 0.1 * (r0n + r0p + c0n + c0p)
        m0 += SIN_SLOPE * h1 - grid.get(at_mid, MY, col) * along + grid.get(at_mid, MH, col) * (down + side)
        m0 -= grid.get(at_mid, MM, col) * (u * part_u + v * part_v)
        m1 = 0.6 * g1 + 0.1 * (r1n + r1p + c1n + c1p)
        m1 += half1 * (r0n - r0p) + u * (down - pull) + part_u - w * h1
        m2 = 0.6 * g2 + 0.1 * (r2n + r2p + c2n + c2p)
        m2 += half1 * (c0n - c0p) + u * cross + 2.0 * part_v - v * pull - w * h2
        for k, value in enumerate((m0, m1, m2)):
            grid.spare_put(work, 4 + k, col, jnp.where(keep, value, 0.0))

    grid.sweep(back_first)

    def early(t, col):
        m0, m1, m2 = (grid.spare_get(work, 4 + k, col) for k in range(3))
        r0n, r0p = grid.both_rows(m0)
        r1n, r1p = grid.both_rows(m1)
        r2n, r2p = grid.both_rows(m2)
        c0n, c0p = grid.both_cols(work, 4, col)
        c1n, c1p = grid.both_cols(work, 5, col)
        c2n, c2p = grid.both_cols(work, 6, col)
        u, v = grid.get(at_one, CU, col), grid.get(at_one, CV, col)
        z, w = grid.get(at_one, CZ, col), grid.get(at_one, CW, col)
        quarter = 0.5 * half0
        down = quarter * (r1n - r1p)
        cross = quarter * ((r2n - r2p) + (c1n - c1p))
        side = quarter * (c2n - c2p)
        p1, p2 = half0 * m1, half0 * m2
        along = u * p1 + v * p2
        pull = z * along
        f1 = 0.3 * m1 + 0.05 * (r1n + r1p + c1n + c1p)
        f1 += quarter * (r0n - r0p) + 2.0 * u * down + v * cross - u * pull - w * p1
        f2 = 0.3 * m2 + 0.05 * (r2n + r2p + c2n + c2p)
        f2 += quarter * (c0n - c0p) + u * cross + 2.0 * v * side - v * pull - w * p2
        height, down, across = (grid.get(kept, k, col) for k in (H, Q1, Q2))
        _, u, v = velocities(height, down, across)
        _, dry, turb = friction(height, u, v, grid.get(kept, FA, col), grid.get(kept, FB, col))
        start = dt0 * (u * f1 + v * f2)
        mu = grid.get(total, 0, col) + grid.get(smooth, 0, col - TILE)
        xi = grid.get(total, 1, col) + grid.get(smooth, 1, col - TILE)
        grid.put(total, 0, col, mu - grid.get(at_one, CE, col) * along - dry * start)
        grid.put(total, 1, col, xi + grid.get(at_one, CB, col) * along + turb * start)

    grid.sweep_own(early)

    cols = out_mu.shape[1]
    for g in range(grid.groups):
        at = pl.ds(g * LANES, LANES)
        out_mu[at, :] = total[0, g, TILE : TILE + cols, :].T
        out_xi[at, :] = total[1, g, TILE : TILE + cols, :].T


VMEM = pl.BlockSpec(memory_space=pltpu.VMEM)
ANY = pl.BlockSpec(memory_space=pltpu.HBM)


def call(body, name, operands, outs, scratch, flops, spaces=None, aliases=None):
    outs = [jax.ShapeDtypeStruct(shape, jnp.float32) for shape in outs]
    moved = 4 * sum(x.size for x in operands) + 4 * sum(x.size for x in outs)
    return pl.pallas_call(
        body,
        name=name,
        out_shape=outs,
        in_specs=spaces or [VMEM] * len(operands),
        out_specs=[VMEM] * len(outs),
        scratch_shapes=[pltpu.VMEM(x, jnp.float32) if isinstance(x, tuple) else x for x in scratch],
        input_output_aliases=aliases or {},
        compiler_params=pltpu.CompilerParams(vmem_limit_bytes=24 * 1024 * 1024),
        cost_estimate=pl.CostEstimate(flops=flops, bytes_accessed=moved, transcendentals=0),
    )(*operands)


def swap_edges(edge_a, edge_b, count):
    pairs_a = [(i, i ^ 1) for i in range(count)]
    pairs_b = [(i, i - 1 if i % 2 == 0 else i + 1) for i in range(1, count - 1)]
    return lax.ppermute(edge_a, "cross", pairs_a), lax.ppermute(edge_b, "cross", pairs_b)


def share(row, combine):
    count = lax.axis_size("cross")
    row = combine(row, lax.ppermute(row, "cross", [(i, i ^ 1) for i in range(count)]))
    parity = [list(range(first, count, 2)) for first in (0, 1)]
    return lax.all_to_all(row, "cross", 0, 0, axis_index_groups=parity, tiled=True)


def max_and_sum(a, b):
    return jnp.where(lax.broadcasted_iota(jnp.int32, a.shape, 1) < LANES // 2, jnp.maximum(a, b), a + b)


def local(state, log_mu, log_xi, dir_mu, dir_xi, wet, observed, terrain, class_weight):
    rows, cols = log_mu.shape
    groups = rows // LANES
    count = lax.axis_size("cross")
    own = (groups, cols, LANES)
    wide = (groups, cols + 2 * TILE, LANES)
    spare = (groups, cols + 4 * TILE, LANES)
    edge = (SHARED, groups, TILE, LANES)
    work = rows * cols

    inputs = (state, log_mu, log_xi, dir_mu, dir_xi, wet, observed, terrain, class_weight)
    inputs = tuple(pltpu.with_memory_space_constraint(x, pltpu.HBM) for x in inputs)
    kept, weights, edge_a, edge_b, row, count_row = call(
        prepare,
        "prepare",
        inputs,
        [(KEPT,) + wide, (1,) + wide, edge, edge, (count // 2, LANES), (1, LANES)],
        [(rows, cols), (3,) + own]
        + [pltpu.VMEM(x.shape, x.dtype) for x in inputs[:-1]]
        + [pltpu.SMEM(class_weight.shape, jnp.float32), pltpu.SemaphoreType.DMA((len(inputs),))],
        100 * work,
        spaces=[ANY] * len(inputs),
    )
    edge_a, edge_b = swap_edges(edge_a, edge_b, count)
    top_rows = share(row, jnp.maximum)
    kept, weights, xy, change = call(
        open_step,
        "open_step",
        (kept, weights, edge_a, edge_b),
        [(KEPT,) + wide, (1,) + wide, (6,) + wide, (3,) + wide],
        [(5,) + spare],
        100 * work,
        aliases={0: 0, 1: 1},
    )
    at_one, mid, next_row = call(
        middle,
        "middle",
        (top_rows, kept, xy, count_row),
        [(6,) + wide, (3,) + wide, (count // 2, LANES)],
        [(5,) + spare],
        120 * work,
    )
    next_rows = share(next_row, max_and_sum)
    smooth, tan = call(
        between,
        "between",
        (top_rows, kept, weights, change, at_one),
        [(2,) + own, (3,) + wide],
        [(4,) + spare, (4,) + spare],
        100 * work,
        aliases={3: 1},
    )
    return call(
        functools.partial(finish, float(rows * cols * count)),
        "finish",
        (top_rows, next_rows, kept, at_one, mid, tan, smooth),
        [(rows, cols), (rows, cols)],
        [(9,) + wide, (3,) + spare, (7,) + spare, (2,) + wide],
        300 * work,
    )


def solution(mesh):
    return jax.shard_map(
        local,
        mesh=mesh,
        in_specs=(
            P(None, "grp", "cross"),
            P("grp", "cross"),
            P("grp", "cross"),
            P("grp", "cross"),
            P("grp", "cross"),
            P("grp", "cross"),
            P("grp", "cross"),
            P("grp", "cross"),
            P(),
        ),
        out_specs=(P("grp", "cross"), P("grp", "cross")),
        check_vma=False,
    )
```

```python
import functools

import jax
import jax.numpy as jnp
from jax import lax
from jax.experimental import pallas as pl
from jax.experimental.pallas import tpu as pltpu
from jax.sharding import PartitionSpec as P

COS_SLOPE = 0.8
SIN_SLOPE = 0.6
DEPTH_FLOOR = 0.05
SPEED_EPS = 0.01
COURANT = 0.2
DATA_WEIGHT = 100000.0

LANES = 128
TILE = 8
H, Q1, Q2, FA, FB, DM, DX, OB, WR = range(9)
KEPT = 8
SHARED = 9
UNROLL = 6


class Grid:
    def __init__(self, groups, wide):
        self.groups = groups
        self.tiles = wide // TILE
        self.lane = lax.broadcasted_iota(jnp.int32, (groups * TILE, LANES), 1)
        self.blank = jnp.zeros((TILE, LANES), jnp.float32)
        me = lax.axis_index("cross")
        self.ends = (me == 0, me == lax.axis_size("cross") - 1)

    def rows_next(self, v):
        turned = pltpu.roll(v, LANES - 1, 1)
        after = jnp.concatenate([turned[TILE:], self.blank], axis=0)
        return jnp.where(self.lane == LANES - 1, after, turned)

    def rows_prev(self, v):
        turned = pltpu.roll(v, 1, 1)
        before = jnp.concatenate([self.blank, turned[:-TILE]], axis=0)
        return jnp.where(self.lane == 0, before, turned)

    def both_rows(self, v):
        return self.rows_next(v), self.rows_prev(v)

    def get(self, ref, k, col):
        return jnp.concatenate([ref[k, g, pl.ds(col, TILE), :] for g in range(self.groups)], axis=0)

    def put(self, ref, k, col, value):
        for g in range(self.groups):
            ref[k, g, pl.ds(col, TILE), :] = value[g * TILE : (g + 1) * TILE]

    def spare_get(self, ref, k, col, off=0):
        return self.get(ref, k, col + TILE + off)

    def spare_put(self, ref, k, col, value):
        self.put(ref, k, col + TILE, value)

    def both_cols(self, ref, k, col):
        return self.spare_get(ref, k, col, 1), self.spare_get(ref, k, col, -1)

    def sweep(self, body, first=0, last=None, carry=None):
        last = self.tiles if last is None else last
        steps, rest = divmod(last - first, UNROLL)

        def visit(t, col, carry):
            return body(t, col) if carry is None else body(t, col, carry)

        def step(i, carry):
            for u in range(UNROLL):
                t = first + i * UNROLL + u
                carry = visit(t, pl.multiple_of(t * TILE, TILE), carry)
            return carry

        carry = lax.fori_loop(0, steps, step, carry)
        for t in range(last - rest, last):
            carry = visit(t, t * TILE, carry)
        return carry

    def sweep_own(self, body):
        self.sweep(body, 1, self.tiles - 1)

    def inside(self, t):
        return jnp.logical_not(((t == 0) & self.ends[0]) | ((t == self.tiles - 1) & self.ends[1]))


def speed_of(height, down, across):
    inv = 1.0 / jnp.maximum(height, DEPTH_FLOOR)
    vel_down = down * inv
    vel_across = across * inv
    return jnp.sqrt(vel_down * vel_down + vel_across * vel_across) + jnp.sqrt(COS_SLOPE * jnp.maximum(height, 0.0))


def velocities(height, down, across):
    inv = 1.0 / jnp.maximum(height, DEPTH_FLOOR)
    return inv, down * inv, across * inv


def friction(height, vel_down, vel_across, dry, turbulent):
    squared = vel_down * vel_down + vel_across * vel_across + SPEED_EPS
    inv_speed = lax.rsqrt(squared)
    return inv_speed, dry * height * inv_speed, turbulent * (squared * inv_speed)


def step_length(row, last, shape):
    return COURANT / jnp.broadcast_to(jnp.maximum(row[:1, :], last[:1, :]), shape)


def prepare(*refs):
    sources = refs[:9]
    kept, weights, edge_a, edge_b, row, count_row, code, turned = refs[9:17]
    held, arrived = refs[17:26], refs[26]
    copies = [pltpu.make_async_copy(src, dst, arrived.at[i]) for i, (src, dst) in enumerate(zip(sources, held))]
    for i in (0, 6, 5, 7, 3, 4, 1, 2, 8):
        copies[i].start()
    state, log_mu, log_xi, dir_mu, dir_xi, wet, observed, terrain, class_weight = held
    rows, cols = log_mu.shape
    groups = rows // LANES
    own = pl.ds(TILE, cols)

    copies[0].wait()
    top = jnp.zeros((16, cols), jnp.float32)
    for i in range(0, rows, 16):
        top = jnp.maximum(top, speed_of(*(state[k, i : i + 16, :] for k in range(3))))
    row[...] = jnp.full(row.shape, jnp.max(top), jnp.float32)
    for g in range(groups):
        for k in range(3):
            kept[k, g, own, :] = state[k, pl.ds(g * LANES, LANES), :].T

    for i in (6, 5, 7):
        copies[i].wait()
    seen = jnp.zeros((16, cols), jnp.float32)
    for i in range(0, rows, 16):
        seen_here = observed[i : i + 16, :]
        code[i : i + 16, :] = (wet[i : i + 16, :] + 2 * seen_here + 4 * terrain[i : i + 16, :]).astype(jnp.float32)
        seen += seen_here.astype(jnp.float32)
    count_row[...] = jnp.full(count_row.shape, jnp.sum(seen), jnp.float32)

    for i in (3, 4, 1, 2, 8):
        copies[i].wait()
    for g in range(groups):
        at = pl.ds(g * LANES, LANES)
        turned[2, g] = code[at, :].T
        kept[DM, g, own, :] = dir_mu[at, :].T
        kept[DX, g, own, :] = dir_xi[at, :].T
        turned[0, g] = log_mu[at, :].T
        turned[1, g] = log_xi[at, :].T

    def derive(i, carry):
        for g, half in ((g, half) for g in range(groups) for half in range(2)):
            at = pl.ds(pl.multiple_of((2 * i + half) * TILE, TILE), TILE)
            to = pl.ds(pl.multiple_of((2 * i + half + 1) * TILE, TILE), TILE)
            bits = turned[2, g, at, :].astype(jnp.int32)
            wet_here = (bits & 1).astype(jnp.float32)
            kind = bits >> 2
            kept[FA, g, to, :] = wet_here * jnp.exp(turned[0, g, at, :]) * COS_SLOPE
            kept[FB, g, to, :] = wet_here * jnp.exp(-turned[1, g, at, :])
            kept[OB, g, to, :] = ((bits >> 1) & 1).astype(jnp.float32)
            weight = jnp.zeros((TILE, LANES), jnp.float32)
            for c in range(class_weight.shape[0]):
                weight = jnp.where(kind == c, class_weight[c], weight)
            weights[0, g, to, :] = weight
        return carry

    lax.fori_loop(0, cols // (2 * TILE), derive, 0)
    even = lax.rem(lax.axis_index("cross"), 2) == 0
    for k in range(SHARED):
        ref, j = (kept, k) if k < KEPT else (weights, 0)
        for g in range(groups):
            left = ref[j, g, TILE : 2 * TILE, :]
            right = ref[j, g, cols : cols + TILE, :]
            edge_a[k, g] = jnp.where(even, right, left)
            edge_b[k, g] = jnp.where(even, left, right)


def fill_halo(source, ref, j, k, edge_a, edge_b):
    even = lax.rem(lax.axis_index("cross"), 2) == 0
    wide = ref.shape[2]
    for g in range(ref.shape[1]):
        ref[j, g, TILE : wide - TILE, :] = source[j, g, TILE : wide - TILE, :]
        ref[j, g, :TILE, :] = jnp.where(even, edge_b[k, g], edge_a[k, g])
        ref[j, g, wide - TILE :, :] = jnp.where(even, edge_a[k, g], edge_b[k, g])


def open_step(kept_in, weights_in, edge_a, edge_b, kept, weights, xy, change, work):
    grid = Grid(kept.shape[1], kept.shape[2])
    for k in range(KEPT):
        fill_halo(kept_in, kept, k, k, edge_a, edge_b)
    fill_halo(weights_in, weights, 0, WR, edge_a, edge_b)

    def first(t, col):
        height, down, across = (grid.get(kept, k, col) for k in (H, Q1, Q2))
        _, u, v = velocities(height, down, across)
        _, dry, turb = friction(height, u, v, grid.get(kept, FA, col), grid.get(kept, FB, col))
        moved = dry * grid.get(kept, DM, col) - turb * grid.get(kept, DX, col)
        grid.put(change, 0, col, -u * moved)
        grid.put(change, 1, col, -v * moved)
        drag = dry + turb
        pressure = 0.5 * COS_SLOPE * height * height
        mixed = down * v
        for k, value in enumerate((height, down, across, mixed, across * v + pressure)):
            grid.spare_put(work, k, col, value)
        hn, hp = grid.both_rows(height)
        pn, pp = grid.both_rows(down)
        qn, qp = grid.both_rows(across)
        fn, fp = grid.both_rows(down * u + pressure)
        gn, gp = grid.both_rows(mixed)
        grid.put(xy, 0, col, 0.6 * height + 0.1 * (hn + hp))
        grid.put(xy, 1, col, 0.6 * down + 0.1 * (pn + pp))
        grid.put(xy, 2, col, 0.6 * across + 0.1 * (qn + qp))
        grid.put(xy, 3, col, -0.5 * (pn - pp))
        grid.put(xy, 4, col, SIN_SLOPE * height - drag * u - 0.5 * (fn - fp))
        grid.put(xy, 5, col, -drag * v - 0.5 * (gn - gp))

    grid.sweep(first)

    def second(t, col):
        hn, hp = grid.both_cols(work, 0, col)
        pn, pp = grid.both_cols(work, 1, col)
        qn, qp = grid.both_cols(work, 2, col)
        gn, gp = grid.both_cols(work, 3, col)
        fn, fp = grid.both_cols(work, 4, col)
        for k, (n, p) in enumerate(((hn, hp), (pn, pp), (qn, qp))):
            grid.put(xy, k, col, grid.get(xy, k, col) + 0.1 * (n + p))
        for k, (n, p) in enumerate(((qn, qp), (gn, gp), (fn, fp))):
            grid.put(xy, 3 + k, col, grid.get(xy, 3 + k, col) - 0.5 * (n - p))

    grid.sweep(second)


CU, CV, CZ, CW, CE, CB = range(6)
MU, MV, MZ, MW, ME, MB, MM, MH, MY = range(9)


def middle(top, last, kept, xy, count_row, at_one, mid, row, work):
    grid = Grid(kept.shape[1], kept.shape[2])
    dt = step_length(top, last, grid.lane.shape)
    half = 0.5 * dt

    def first(t, col):
        keep = grid.inside(t)
        height, down, across = (
            jnp.where(keep, grid.get(xy, k, col) + dt * grid.get(xy, 3 + k, col), 0.0) for k in range(3)
        )
        inv, u, v = velocities(height, down, across)
        turb_of = grid.get(kept, FB, col)
        inv_speed, dry, turb = friction(height, u, v, grid.get(kept, FA, col), turb_of)
        drag = dry + turb
        grid.put(at_one, CU, col, u)
        grid.put(at_one, CV, col, v)
        grid.put(at_one, CZ, col, (turb_of - dry * inv_speed) * inv_speed * inv)
        grid.put(at_one, CW, col, drag * inv)
        grid.put(at_one, CE, col, dry)
        grid.put(at_one, CB, col, turb)
        pressure = 0.5 * COS_SLOPE * height * height
        mixed = down * v
        for k, value in enumerate((height, down, across, mixed, across * v + pressure)):
            grid.spare_put(work, k, col, value)
        sources = (0.0, dt * (SIN_SLOPE * height - drag * u), -dt * drag * v)
        for k, (value, flux) in enumerate(((height, down), (down, down * u + pressure), (across, mixed))):
            tenth, moved = 0.1 * value, half * flux
            total = grid.get(kept, k, col) + 0.6 * value + sources[k]
            total += grid.rows_next(tenth - moved) + grid.rows_prev(tenth + moved)
            grid.put(mid, k, col, total)

    grid.sweep(first)

    def second(t, col, most):
        keep = grid.inside(t)
        found = []
        for k, (value, flux) in enumerate(((0, 2), (1, 3), (2, 4))):
            vn, vp = grid.both_cols(work, value, col)
            fn, fp = grid.both_cols(work, flux, col)
            total = grid.get(mid, k, col) + 0.1 * (vn + vp) - half * (fn - fp)
            found.append(jnp.where(keep, 0.5 * total, 0.0))
            grid.put(mid, k, col, found[k])
        own = (t > 0) & (t < grid.tiles - 1)
        return jnp.maximum(most, jnp.where(own, speed_of(*found), 0.0))

    fastest = grid.sweep(second, carry=jnp.zeros(grid.lane.shape, jnp.float32))
    row[0:1, :] = jnp.full((1, LANES), jnp.max(fastest), jnp.float32)
    row[1:2, :] = count_row[...]


def regularize(kept, weights, smooth, bent):
    grid = Grid(kept.shape[1], kept.shape[2])

    def spread(t, col):
        for k, field in enumerate((DM, DX)):
            grid.spare_put(bent, k, col, grid.get(kept, field, col))

    grid.sweep(spread)

    def laplace(k, col):
        value = grid.spare_get(bent, k, col)
        rn, rp = grid.both_rows(value)
        cn, cp = grid.both_cols(bent, k, col)
        return 4.0 * value - rn - rp - cn - cp

    def bend(t, col):
        weight = grid.get(weights, 0, col)
        for k in range(2):
            grid.spare_put(bent, 2 + k, col, weight * laplace(k, col))

    grid.sweep(bend)

    def bend_again(t, col):
        for k in range(2):
            grid.put(smooth, k, col - TILE, laplace(2 + k, col))

    grid.sweep_own(bend_again)


def tangent_one(top, last, kept, change, at_one, one, part):
    grid = Grid(kept.shape[1], kept.shape[2])
    dt = step_length(top, last, grid.lane.shape)
    half = 0.5 * dt

    def first(t, col):
        tp, tq = dt * grid.get(change, 0, col), dt * grid.get(change, 1, col)
        u, v = grid.get(at_one, CU, col), grid.get(at_one, CV, col)
        w = grid.get(at_one, CW, col)
        moved = grid.get(at_one, CE, col) * grid.get(kept, DM, col) - grid.get(at_one, CB, col) * grid.get(kept, DX, col)
        along = grid.get(at_one, CZ, col) * (u * tp + v * tq) + moved
        mixed = v * tp + u * tq
        for k, value in enumerate((tp, tq, mixed, 2.0 * v * tq)):
            grid.spare_put(one, k, col, value)
        moved = half * tp
        grid.put(part, 0, col, grid.rows_prev(moved) - grid.rows_next(moved))
        sources = (-dt * (u * along + w * tp), -dt * (v * along + w * tq))
        for k, (value, flux) in enumerate(((tp, 2.0 * u * tp), (tq, mixed))):
            tenth, moved = 0.1 * value, half * flux
            total = 0.6 * value + sources[k]
            total += grid.rows_next(tenth - moved) + grid.rows_prev(tenth + moved)
            grid.put(part, 1 + k, col, total)

    grid.sweep(first)


def tangent_mid(top, last, kept, mid, one, part_one, part, at_mid, work):
    grid = Grid(kept.shape[1], kept.shape[2])
    dt = step_length(top, last, grid.lane.shape)
    half = 0.5 * dt

    def second(t, col):
        keep = grid.inside(t)
        qn, qp = grid.both_cols(one, 1, col)
        pn, pp = grid.both_cols(one, 0, col)
        gn, gp = grid.both_cols(one, 2, col)
        fn, fp = grid.both_cols(one, 3, col)
        th = grid.get(part_one, 0, col) - half * (qn - qp)
        tp = grid.get(part_one, 1, col) + 0.1 * (pn + pp) - half * (gn - gp)
        tq = grid.get(part_one, 2, col) + 0.1 * (qn + qp) - half * (fn - fp)
        th, tp, tq = (jnp.where(keep, 0.5 * x, 0.0) for x in (th, tp, tq))
        height, down, across = (grid.get(mid, k, col) for k in range(3))
        inv, u, v = velocities(height, down, across)
        above = jnp.where(height > DEPTH_FLOOR, 1.0, jnp.where(height == DEPTH_FLOOR, 0.5, 0.0))
        turb_of = grid.get(kept, FB, col)
        dry_of = grid.get(kept, FA, col)
        inv_speed, dry, turb = friction(height, u, v, dry_of, turb_of)
        z = (turb_of - dry * inv_speed) * inv_speed * inv
        w = (dry + turb) * inv
        y = dry_of * inv_speed - above * (z * (u * u + v * v) + w)
        eight = COS_SLOPE * height
        for k, value in ((MU, u), (MV, v), (MZ, z), (MW, w), (ME, dry), (MB, turb), (MM, above), (MH, eight), (MY, y)):
            grid.put(at_mid, k, col, value)
        along = z * (u * tp + v * tq) + y * th
        along += dry * grid.get(kept, DM, col) - turb * grid.get(kept, DX, col)
        lift = above * th
        flux_down = 2.0 * u * tp + eight * th - u * u * lift
        mixed = v * tp + u * tq - u * v * lift
        for k, value in enumerate((th, tp, tq, mixed, 2.0 * v * tq + eight * th - v * v * lift)):
            grid.spare_put(work, k, col, value)
        hn, hp = grid.both_rows(th)
        pn, pp = grid.both_rows(tp)
        qn, qp = grid.both_rows(tq)
        fn, fp = grid.both_rows(flux_down)
        gn, gp = grid.both_rows(mixed)
        grid.put(part, 0, col, 0.6 * th + 0.1 * (hn + hp))
        grid.put(part, 1, col, 0.6 * tp + 0.1 * (pn + pp))
        grid.put(part, 2, col, 0.6 * tq + 0.1 * (qn + qp))
        grid.put(part, 3, col, -0.5 * (pn - pp))
        grid.put(part, 4, col, SIN_SLOPE * th - u * along - w * tp - 0.5 * (fn - fp))
        grid.put(part, 5, col, -v * along - w * tq - 0.5 * (gn - gp))

    grid.sweep(second)


def tangent_end(part, work, tan):
    grid = Grid(part.shape[1], part.shape[2])

    def third(t, col):
        keep = grid.inside(t)
        hn, hp = grid.both_cols(work, 0, col)
        pn, pp = grid.both_cols(work, 1, col)
        qn, qp = grid.both_cols(work, 2, col)
        gn, gp = grid.both_cols(work, 3, col)
        fn, fp = grid.both_cols(work, 4, col)
        for k, (n, p) in enumerate(((hn, hp), (pn, pp), (qn, qp))):
            grid.spare_put(tan, k, col, jnp.where(keep, grid.get(part, k, col) + 0.1 * (n + p), 0.0))
        for k, (n, p) in enumerate(((qn, qp), (gn, gp), (fn, fp))):
            grid.spare_put(tan, 3 + k, col, jnp.where(keep, grid.get(part, 3 + k, col) - 0.5 * (n - p), 0.0))

    grid.sweep(third)


def finish(cells, top, last, fast, fast_last, kept, at_one, at_mid, between, tan, smooth, out_mu, out_xi, work, total):
    grid = Grid(kept.shape[1], kept.shape[2])
    shape = grid.lane.shape
    dt0 = step_length(top, last, shape)
    dt1 = step_length(fast, fast_last, shape)
    weight = jnp.broadcast_to((DATA_WEIGHT * cells) / jnp.maximum(fast[1:2, :], fast_last[1:2, :]), shape)
    half1 = 0.5 * dt1
    half0 = 0.5 * dt0

    def seed_end(t, col):
        def section(k, off):
            return grid.spare_get(tan, k, col, off) + dt1 * grid.spare_get(tan, 3 + k, col, off)

        th, tp = section(0, 0), section(1, 0)
        tenth, moved = 0.1 * th, half1 * tp
        value = grid.spare_get(between, 0, col) + 0.6 * th
        value += grid.rows_next(tenth - moved) + grid.rows_prev(tenth + moved)
        value += 0.1 * (section(0, 1) + section(0, -1)) - half1 * (section(2, 1) - section(2, -1))
        grid.spare_put(work, 0, col, weight * grid.get(kept, OB, col) * (0.5 * value))

    grid.sweep(seed_end)

    def back_second(t, col):
        keep = grid.inside(t)
        seed = grid.spare_get(work, 0, col)
        rn, rp = grid.both_rows(seed)
        cn, cp = grid.both_cols(work, 0, col)
        grid.spare_put(work, 1, col, jnp.where(keep, 0.3 * seed + 0.05 * (rn + rp + cn + cp), 0.0))
        grid.spare_put(work, 2, col, jnp.where(keep, 0.5 * half1 * (rn - rp), 0.0))
        grid.spare_put(work, 3, col, jnp.where(keep, 0.5 * half1 * (cn - cp), 0.0))

    grid.sweep(back_second)

    def back_first(t, col):
        keep = grid.inside(t)
        g0, g1, g2 = (grid.spare_get(work, 1 + k, col) for k in range(3))
        r0n, r0p = grid.both_rows(g0)
        r1n, r1p = grid.both_rows(g1)
        r2n, r2p = grid.both_rows(g2)
        c0n, c0p = grid.both_cols(work, 1, col)
        c1n, c1p = grid.both_cols(work, 2, col)
        c2n, c2p = grid.both_cols(work, 3, col)
        u, v = grid.get(at_mid, MU, col), grid.get(at_mid, MV, col)
        z, w = grid.get(at_mid, MZ, col), grid.get(at_mid, MW, col)
        down = half1 * (r1n - r1p)
        cross = half1 * ((r2n - r2p) + (c1n - c1p))
        side = half1 * (c2n - c2p)
        h1, h2 = dt1 * g1, dt1 * g2
        along = u * h1 + v * h2
        grid.put(total, 0, col, -grid.get(at_mid, ME, col) * along)
        grid.put(total, 1, col, grid.get(at_mid, MB, col) * along)
        pull = z * along
        part_u = u * down + v * cross
        part_v = v * side
        m0 = 0.5 * grid.spare_get(work, 0, col) + 0.6 * g0 + 0.1 * (r0n + r0p + c0n + c0p)
        m0 += SIN_SLOPE * h1 - grid.get(at_mid, MY, col) * along + grid.get(at_mid, MH, col) * (down + side)
        m0 -= grid.get(at_mid, MM, col) * (u * part_u + v * part_v)
        m1 = 0.6 * g1 + 0.1 * (r1n + r1p + c1n + c1p)
        m1 += half1 * (r0n - r0p) + u * (down - pull) + part_u - w * h1
        m2 = 0.6 * g2 + 0.1 * (r2n + r2p + c2n + c2p)
        m2 += half1 * (c0n - c0p) + u * cross + 2.0 * part_v - v * pull - w * h2
        for k, value in enumerate((m0, m1, m2)):
            grid.spare_put(work, 4 + k, col, jnp.where(keep, value, 0.0))

    grid.sweep(back_first)

    def early(t, col):
        m0, m1, m2 = (grid.spare_get(work, 4 + k, col) for k in range(3))
        r0n, r0p = grid.both_rows(m0)
        r1n, r1p = grid.both_rows(m1)
        r2n, r2p = grid.both_rows(m2)
        c0n, c0p = grid.both_cols(work, 4, col)
        c1n, c1p = grid.both_cols(work, 5, col)
        c2n, c2p = grid.both_cols(work, 6, col)
        u, v = grid.get(at_one, CU, col), grid.get(at_one, CV, col)
        z, w = grid.get(at_one, CZ, col), grid.get(at_one, CW, col)
        quarter = 0.5 * half0
        down = quarter * (r1n - r1p)
        cross = quarter * ((r2n - r2p) + (c1n - c1p))
        side = quarter * (c2n - c2p)
        p1, p2 = half0 * m1, half0 * m2
        along = u * p1 + v * p2
        pull = z * along
        f1 = 0.3 * m1 + 0.05 * (r1n + r1p + c1n + c1p)
        f1 += quarter * (r0n - r0p) + 2.0 * u * down + v * cross - u * pull - w * p1
        f2 = 0.3 * m2 + 0.05 * (r2n + r2p + c2n + c2p)
        f2 += quarter * (c0n - c0p) + u * cross + 2.0 * v * side - v * pull - w * p2
        height, down, across = (grid.get(kept, k, col) for k in (H, Q1, Q2))
        _, u, v = velocities(height, down, across)
        _, dry, turb = friction(height, u, v, grid.get(kept, FA, col), grid.get(kept, FB, col))
        start = dt0 * (u * f1 + v * f2)
        mu = grid.get(total, 0, col) + grid.get(smooth, 0, col - TILE)
        xi = grid.get(total, 1, col) + grid.get(smooth, 1, col - TILE)
        grid.put(total, 0, col, mu - grid.get(at_one, CE, col) * along - dry * start)
        grid.put(total, 1, col, xi + grid.get(at_one, CB, col) * along + turb * start)

    grid.sweep_own(early)

    cols = out_mu.shape[1]
    for g in range(grid.groups):
        at = pl.ds(g * LANES, LANES)
        out_mu[at, :] = total[0, g, TILE : TILE + cols, :].T
        out_xi[at, :] = total[1, g, TILE : TILE + cols, :].T


VMEM = pl.BlockSpec(memory_space=pltpu.VMEM)
ANY = pl.BlockSpec(memory_space=pltpu.HBM)


def call(body, name, operands, outs, scratch, flops, spaces=None, aliases=None):
    outs = [jax.ShapeDtypeStruct(shape, jnp.float32) for shape in outs]
    moved = 4 * sum(x.size for x in operands) + 4 * sum(x.size for x in outs)
    return pl.pallas_call(
        body,
        name=name,
        out_shape=outs,
        in_specs=spaces or [VMEM] * len(operands),
        out_specs=[VMEM] * len(outs),
        scratch_shapes=[pltpu.VMEM(x, jnp.float32) if isinstance(x, tuple) else x for x in scratch],
        input_output_aliases=aliases or {},
        compiler_params=pltpu.CompilerParams(vmem_limit_bytes=24 * 1024 * 1024),
        cost_estimate=pl.CostEstimate(flops=flops, bytes_accessed=moved, transcendentals=0),
    )(*operands)


def swap(value, other):
    count = lax.axis_size("cross")
    pairs = [(i, other(i)) for i in range(count) if other(i) is not None and 0 <= other(i) < count]
    return lax.ppermute(value, "cross", pairs)


def other_core(i):
    return i ^ 1


def next_chip(i):
    return i - 1 if i % 2 == 0 else i + 1


def odd_far(step):
    return lambda i: i ^ step if i % 2 == 1 else None


def to_even(i):
    return i - 1 if i % 2 == 1 else None


def max_and_sum(a, b):
    return jnp.where(lax.broadcasted_iota(jnp.int32, a.shape, 0) == 0, jnp.maximum(a, b), a + b)


def round_beside(row, other, result=None):
    arrived = swap(row, other)
    if result is not None:
        arrived, result = lax.optimization_barrier((arrived, result))
    return max_and_sum(row, arrived), result


def local(state, log_mu, log_xi, dir_mu, dir_xi, wet, observed, terrain, class_weight):
    rows, cols = log_mu.shape
    groups = rows // LANES
    count = lax.axis_size("cross")
    own = (groups, cols, LANES)
    wide = (groups, cols + 2 * TILE, LANES)
    spare = (groups, cols + 4 * TILE, LANES)
    edge = (SHARED, groups, TILE, LANES)
    work = rows * cols

    inputs = (state, log_mu, log_xi, dir_mu, dir_xi, wet, observed, terrain, class_weight)
    inputs = tuple(pltpu.with_memory_space_constraint(x, pltpu.HBM) for x in inputs)
    kept, weights, edge_a, edge_b, row, count_row = call(
        prepare,
        "prepare",
        inputs,
        [(KEPT,) + wide, (1,) + wide, edge, edge, (1, LANES), (1, LANES)],
        [(rows, cols), (3,) + own]
        + [pltpu.VMEM(x.shape, x.dtype) for x in inputs[:-1]]
        + [pltpu.SMEM(class_weight.shape, jnp.float32), pltpu.SemaphoreType.DMA((len(inputs),))],
        100 * work,
        spaces=[ANY] * len(inputs),
    )
    steps = [2**k for k in range(1, count.bit_length() - 1)]
    edge_a = swap(edge_a, other_core)
    row = jnp.maximum(row, swap(row, other_core))
    for step in steps[:-1]:
        row = jnp.maximum(row, swap(row, odd_far(step)))
        if step == 2:
            row, edge_b = lax.optimization_barrier((row, edge_b))
            edge_b = swap(edge_b, next_chip)
    kept, weights, xy, change = call(
        open_step,
        "open_step",
        (kept, weights, edge_a, edge_b),
        [(KEPT,) + wide, (1,) + wide, (6,) + wide, (2,) + wide],
        [(5,) + spare],
        100 * work,
        aliases={0: 0, 1: 1},
    )
    arrived, xy = lax.optimization_barrier((swap(row, odd_far(steps[-1])), xy))
    top = jnp.maximum(row, arrived)
    last = swap(top, to_even)
    at_one, mid, row = call(
        middle,
        "middle",
        (top, last, kept, xy, count_row),
        [(6,) + wide, (3,) + wide, (2, LANES)],
        [(5,) + spare],
        120 * work,
    )
    (smooth,) = call(regularize, "regularize", (kept, weights), [(2,) + own], [(4,) + spare], 30 * work)
    row, smooth = round_beside(row, other_core, smooth)
    one, part = call(
        tangent_one, "tangent_one", (top, last, kept, change, at_one), [(4,) + spare, (3,) + wide], [], 60 * work
    )
    row, one = round_beside(row, odd_far(steps[0]), one)
    part, at_mid, between = call(
        tangent_mid,
        "tangent_mid",
        (top, last, kept, mid, one, part),
        [(6,) + wide, (9,) + wide, (5,) + spare],
        [],
        120 * work,
    )
    row, part = round_beside(row, odd_far(steps[1]), part)
    (tan,) = call(tangent_end, "tangent_end", (part, between), [(6,) + spare], [], 30 * work)
    row, tan = round_beside(row, odd_far(steps[2]), tan)
    for step in steps[3:]:
        row, _ = round_beside(row, odd_far(step))
    return call(
        functools.partial(finish, float(rows * cols * count)),
        "finish",
        (top, last, row, swap(row, to_even), kept, at_one, at_mid, between, tan, smooth),
        [(rows, cols), (rows, cols)],
        [(7,) + spare, (2,) + wide],
        300 * work,
    )


def solution(mesh):
    return jax.shard_map(
        local,
        mesh=mesh,
        in_specs=(
            P(None, "grp", "cross"),
            P("grp", "cross"),
            P("grp", "cross"),
            P("grp", "cross"),
            P("grp", "cross"),
            P("grp", "cross"),
            P("grp", "cross"),
            P("grp", "cross"),
            P(),
        ),
        out_specs=(P("grp", "cross"), P("grp", "cross")),
        check_vma=False,
    )
```

```python
import functools

import jax
import jax.numpy as jnp
from jax import lax
from jax.experimental import pallas as pl
from jax.experimental.pallas import tpu as pltpu
from jax.sharding import PartitionSpec as P

COS_SLOPE = 0.8
SIN_SLOPE = 0.6
DEPTH_FLOOR = 0.05
SPEED_EPS = 0.01
COURANT = 0.2
DATA_WEIGHT = 100000.0

LANES = 128
TILE = 8
H, Q1, Q2, FA, FB, DM, DX, OB, WR = range(9)
KEPT = 8
SHARED = 9
UNROLL = 6


class Grid:
    def __init__(self, groups, wide):
        self.groups = groups
        self.tiles = wide // TILE
        self.lane = lax.broadcasted_iota(jnp.int32, (groups * TILE, LANES), 1)
        self.blank = jnp.zeros((TILE, LANES), jnp.float32)
        me = lax.axis_index("cross")
        self.ends = (me == 0, me == lax.axis_size("cross") - 1)

    def rows_next(self, v):
        turned = pltpu.roll(v, LANES - 1, 1)
        after = jnp.concatenate([turned[TILE:], self.blank], axis=0)
        return jnp.where(self.lane == LANES - 1, after, turned)

    def rows_prev(self, v):
        turned = pltpu.roll(v, 1, 1)
        before = jnp.concatenate([self.blank, turned[:-TILE]], axis=0)
        return jnp.where(self.lane == 0, before, turned)

    def both_rows(self, v):
        return self.rows_next(v), self.rows_prev(v)

    def get(self, ref, k, col):
        return jnp.concatenate([ref[k, g, pl.ds(col, TILE), :] for g in range(self.groups)], axis=0)

    def put(self, ref, k, col, value):
        for g in range(self.groups):
            ref[k, g, pl.ds(col, TILE), :] = value[g * TILE : (g + 1) * TILE]

    def spare_get(self, ref, k, col, off=0):
        return self.get(ref, k, col + TILE + off)

    def spare_put(self, ref, k, col, value):
        self.put(ref, k, col + TILE, value)

    def both_cols(self, ref, k, col):
        return self.spare_get(ref, k, col, 1), self.spare_get(ref, k, col, -1)

    def sweep(self, body, first=0, last=None, carry=None):
        last = self.tiles if last is None else last
        steps, rest = divmod(last - first, UNROLL)

        def visit(t, col, carry):
            return body(t, col) if carry is None else body(t, col, carry)

        def step(i, carry):
            for u in range(UNROLL):
                t = first + i * UNROLL + u
                carry = visit(t, pl.multiple_of(t * TILE, TILE), carry)
            return carry

        carry = lax.fori_loop(0, steps, step, carry)
        for t in range(last - rest, last):
            carry = visit(t, t * TILE, carry)
        return carry

    def sweep_own(self, body):
        self.sweep(body, 1, self.tiles - 1)

    def inside(self, t):
        return jnp.logical_not(((t == 0) & self.ends[0]) | ((t == self.tiles - 1) & self.ends[1]))


def speed_of(height, down, across):
    inv = 1.0 / jnp.maximum(height, DEPTH_FLOOR)
    vel_down = down * inv
    vel_across = across * inv
    return jnp.sqrt(vel_down * vel_down + vel_across * vel_across) + jnp.sqrt(COS_SLOPE * jnp.maximum(height, 0.0))


def velocities(height, down, across):
    inv = 1.0 / jnp.maximum(height, DEPTH_FLOOR)
    return inv, down * inv, across * inv


def friction(height, vel_down, vel_across, dry, turbulent):
    squared = vel_down * vel_down + vel_across * vel_across + SPEED_EPS
    inv_speed = lax.rsqrt(squared)
    return inv_speed, dry * height * inv_speed, turbulent * (squared * inv_speed)


def known(row, last, k):
    return jnp.where(lax.rem(lax.axis_index("cross"), 2) == 0, last[k : k + 1, :], row[k : k + 1, :])


def step_length(row, last, shape):
    return COURANT / jnp.broadcast_to(known(row, last, 0), shape)


def prepare(*refs):
    sources = refs[:9]
    kept, weights, edge_a, edge_b, row, count_row, code, turned = refs[9:17]
    held, arrived = refs[17:26], refs[26]
    copies = [pltpu.make_async_copy(src, dst, arrived.at[i]) for i, (src, dst) in enumerate(zip(sources, held))]
    for i in (0, 6, 5, 7, 3, 4, 1, 2, 8):
        copies[i].start()
    state, log_mu, log_xi, dir_mu, dir_xi, wet, observed, terrain, class_weight = held
    rows, cols = log_mu.shape
    groups = rows // LANES
    own = pl.ds(TILE, cols)

    copies[0].wait()
    top = jnp.zeros((16, cols), jnp.float32)
    for i in range(0, rows, 16):
        top = jnp.maximum(top, speed_of(*(state[k, i : i + 16, :] for k in range(3))))
    row[...] = jnp.full(row.shape, jnp.max(top), jnp.float32)
    for g in range(groups):
        for k in range(3):
            kept[k, g, own, :] = state[k, pl.ds(g * LANES, LANES), :].T

    for i in (6, 5, 7):
        copies[i].wait()
    seen = jnp.zeros((16, cols), jnp.float32)
    for i in range(0, rows, 16):
        seen_here = observed[i : i + 16, :]
        code[i : i + 16, :] = (wet[i : i + 16, :] + 2 * seen_here + 4 * terrain[i : i + 16, :]).astype(jnp.float32)
        seen += seen_here.astype(jnp.float32)
    count_row[...] = jnp.full(count_row.shape, jnp.sum(seen), jnp.float32)

    for i in (3, 4, 1, 2, 8):
        copies[i].wait()
    for g in range(groups):
        at = pl.ds(g * LANES, LANES)
        turned[2, g] = code[at, :].T
        kept[DM, g, own, :] = dir_mu[at, :].T
        kept[DX, g, own, :] = dir_xi[at, :].T
        turned[0, g] = log_mu[at, :].T
        turned[1, g] = log_xi[at, :].T

    def derive(i, carry):
        for g, half in ((g, half) for g in range(groups) for half in range(2)):
            at = pl.ds(pl.multiple_of((2 * i + half) * TILE, TILE), TILE)
            to = pl.ds(pl.multiple_of((2 * i + half + 1) * TILE, TILE), TILE)
            bits = turned[2, g, at, :].astype(jnp.int32)
            wet_here = (bits & 1).astype(jnp.float32)
            kind = bits >> 2
            kept[FA, g, to, :] = wet_here * jnp.exp(turned[0, g, at, :]) * COS_SLOPE
            kept[FB, g, to, :] = wet_here * jnp.exp(-turned[1, g, at, :])
            kept[OB, g, to, :] = ((bits >> 1) & 1).astype(jnp.float32)
            weight = jnp.zeros((TILE, LANES), jnp.float32)
            for c in range(class_weight.shape[0]):
                weight = jnp.where(kind == c, class_weight[c], weight)
            weights[0, g, to, :] = weight
        return carry

    lax.fori_loop(0, cols // (2 * TILE), derive, 0)
    even = lax.rem(lax.axis_index("cross"), 2) == 0
    for k in range(SHARED):
        ref, j = (kept, k) if k < KEPT else (weights, 0)
        for g in range(groups):
            left = ref[j, g, TILE : 2 * TILE, :]
            right = ref[j, g, cols : cols + TILE, :]
            edge_a[k, g] = jnp.where(even, right, left)
            edge_b[k, g] = jnp.where(even, left, right)


def fill_halo(source, ref, j, k, edge_a, edge_b):
    me = lax.axis_index("cross")
    even = lax.rem(me, 2) == 0
    first, last = me == 0, me == lax.axis_size("cross") - 1
    wide = ref.shape[2]
    for g in range(ref.shape[1]):
        ref[j, g, TILE : wide - TILE, :] = source[j, g, TILE : wide - TILE, :]
        ref[j, g, :TILE, :] = jnp.where(first, 0.0, jnp.where(even, edge_b[k, g], edge_a[k, g]))
        ref[j, g, wide - TILE :, :] = jnp.where(last, 0.0, jnp.where(even, edge_a[k, g], edge_b[k, g]))


def open_step(kept_in, weights_in, edge_a, edge_b, kept, weights, xy, change, work):
    grid = Grid(kept.shape[1], kept.shape[2])
    for k in range(KEPT):
        fill_halo(kept_in, kept, k, k, edge_a, edge_b)
    fill_halo(weights_in, weights, 0, WR, edge_a, edge_b)

    def first(t, col):
        height, down, across = (grid.get(kept, k, col) for k in (H, Q1, Q2))
        _, u, v = velocities(height, down, across)
        _, dry, turb = friction(height, u, v, grid.get(kept, FA, col), grid.get(kept, FB, col))
        moved = dry * grid.get(kept, DM, col) - turb * grid.get(kept, DX, col)
        grid.put(change, 0, col, -u * moved)
        grid.put(change, 1, col, -v * moved)
        drag = dry + turb
        pressure = 0.5 * COS_SLOPE * height * height
        mixed = down * v
        for k, value in enumerate((height, down, across, mixed, across * v + pressure)):
            grid.spare_put(work, k, col, value)
        hn, hp = grid.both_rows(height)
        pn, pp = grid.both_rows(down)
        qn, qp = grid.both_rows(across)
        fn, fp = grid.both_rows(down * u + pressure)
        gn, gp = grid.both_rows(mixed)
        grid.put(xy, 0, col, 0.6 * height + 0.1 * (hn + hp))
        grid.put(xy, 1, col, 0.6 * down + 0.1 * (pn + pp))
        grid.put(xy, 2, col, 0.6 * across + 0.1 * (qn + qp))
        grid.put(xy, 3, col, -0.5 * (pn - pp))
        grid.put(xy, 4, col, SIN_SLOPE * height - drag * u - 0.5 * (fn - fp))
        grid.put(xy, 5, col, -drag * v - 0.5 * (gn - gp))

    grid.sweep(first)

    def second(t, col):
        hn, hp = grid.both_cols(work, 0, col)
        pn, pp = grid.both_cols(work, 1, col)
        qn, qp = grid.both_cols(work, 2, col)
        gn, gp = grid.both_cols(work, 3, col)
        fn, fp = grid.both_cols(work, 4, col)
        for k, (n, p) in enumerate(((hn, hp), (pn, pp), (qn, qp))):
            grid.put(xy, k, col, grid.get(xy, k, col) + 0.1 * (n + p))
        for k, (n, p) in enumerate(((qn, qp), (gn, gp), (fn, fp))):
            grid.put(xy, 3 + k, col, grid.get(xy, 3 + k, col) - 0.5 * (n - p))

    grid.sweep(second)


CU, CV, CZ, CW, CE, CB = range(6)
MU, MV, MZ, MW, ME, MB, MM, MH, MY = range(9)


def middle(top, last, kept, xy, count_row, at_one, mid, row, work):
    grid = Grid(kept.shape[1], kept.shape[2])
    dt = step_length(top, last, grid.lane.shape)
    half = 0.5 * dt

    def first(t, col):
        keep = grid.inside(t)
        height, down, across = (
            jnp.where(keep, grid.get(xy, k, col) + dt * grid.get(xy, 3 + k, col), 0.0) for k in range(3)
        )
        inv, u, v = velocities(height, down, across)
        turb_of = grid.get(kept, FB, col)
        inv_speed, dry, turb = friction(height, u, v, grid.get(kept, FA, col), turb_of)
        drag = dry + turb
        grid.put(at_one, CU, col, u)
        grid.put(at_one, CV, col, v)
        grid.put(at_one, CZ, col, (turb_of - dry * inv_speed) * inv_speed * inv)
        grid.put(at_one, CW, col, drag * inv)
        grid.put(at_one, CE, col, dry)
        grid.put(at_one, CB, col, turb)
        pressure = 0.5 * COS_SLOPE * height * height
        mixed = down * v
        for k, value in enumerate((height, down, across, mixed, across * v + pressure)):
            grid.spare_put(work, k, col, value)
        sources = (0.0, dt * (SIN_SLOPE * height - drag * u), -dt * drag * v)
        for k, (value, flux) in enumerate(((height, down), (down, down * u + pressure), (across, mixed))):
            tenth, moved = 0.1 * value, half * flux
            total = grid.get(kept, k, col) + 0.6 * value + sources[k]
            total += grid.rows_next(tenth - moved) + grid.rows_prev(tenth + moved)
            grid.put(mid, k, col, total)

    grid.sweep(first)

    def second(t, col, most):
        keep = grid.inside(t)
        found = []
        for k, (value, flux) in enumerate(((0, 2), (1, 3), (2, 4))):
            vn, vp = grid.both_cols(work, value, col)
            fn, fp = grid.both_cols(work, flux, col)
            total = grid.get(mid, k, col) + 0.1 * (vn + vp) - half * (fn - fp)
            found.append(jnp.where(keep, 0.5 * total, 0.0))
            grid.put(mid, k, col, found[k])
        own = (t > 0) & (t < grid.tiles - 1)
        return jnp.maximum(most, jnp.where(own, speed_of(*found), 0.0))

    fastest = grid.sweep(second, carry=jnp.zeros(grid.lane.shape, jnp.float32))
    row[0:1, :] = jnp.full((1, LANES), jnp.max(fastest), jnp.float32)
    row[1:2, :] = count_row[...]


def regularize(kept, weights, smooth, bent):
    grid = Grid(kept.shape[1], kept.shape[2])

    def spread(t, col):
        for k, field in enumerate((DM, DX)):
            grid.spare_put(bent, k, col, grid.get(kept, field, col))

    grid.sweep(spread)

    def laplace(k, col):
        value = grid.spare_get(bent, k, col)
        rn, rp = grid.both_rows(value)
        cn, cp = grid.both_cols(bent, k, col)
        return 4.0 * value - rn - rp - cn - cp

    def bend(t, col):
        weight = grid.get(weights, 0, col)
        for k in range(2):
            grid.spare_put(bent, 2 + k, col, weight * laplace(k, col))

    grid.sweep(bend)

    def bend_again(t, col):
        for k in range(2):
            grid.put(smooth, k, col - TILE, laplace(2 + k, col))

    grid.sweep_own(bend_again)


def tangent_one(top, last, kept, change, at_one, one, part):
    grid = Grid(kept.shape[1], kept.shape[2])
    dt = step_length(top, last, grid.lane.shape)
    half = 0.5 * dt

    def first(t, col):
        tp, tq = dt * grid.get(change, 0, col), dt * grid.get(change, 1, col)
        u, v = grid.get(at_one, CU, col), grid.get(at_one, CV, col)
        w = grid.get(at_one, CW, col)
        moved = grid.get(at_one, CE, col) * grid.get(kept, DM, col) - grid.get(at_one, CB, col) * grid.get(kept, DX, col)
        along = grid.get(at_one, CZ, col) * (u * tp + v * tq) + moved
        mixed = v * tp + u * tq
        for k, value in enumerate((tp, tq, mixed, 2.0 * v * tq)):
            grid.spare_put(one, k, col, value)
        moved = half * tp
        grid.put(part, 0, col, grid.rows_prev(moved) - grid.rows_next(moved))
        sources = (-dt * (u * along + w * tp), -dt * (v * along + w * tq))
        for k, (value, flux) in enumerate(((tp, 2.0 * u * tp), (tq, mixed))):
            tenth, moved = 0.1 * value, half * flux
            total = 0.6 * value + sources[k]
            total += grid.rows_next(tenth - moved) + grid.rows_prev(tenth + moved)
            grid.put(part, 1 + k, col, total)

    grid.sweep(first)


def tangent_mid(top, last, kept, mid, one, part_one, part, at_mid, work):
    grid = Grid(kept.shape[1], kept.shape[2])
    dt = step_length(top, last, grid.lane.shape)
    half = 0.5 * dt

    def second(t, col):
        keep = grid.inside(t)
        qn, qp = grid.both_cols(one, 1, col)
        pn, pp = grid.both_cols(one, 0, col)
        gn, gp = grid.both_cols(one, 2, col)
        fn, fp = grid.both_cols(one, 3, col)
        th = grid.get(part_one, 0, col) - half * (qn - qp)
        tp = grid.get(part_one, 1, col) + 0.1 * (pn + pp) - half * (gn - gp)
        tq = grid.get(part_one, 2, col) + 0.1 * (qn + qp) - half * (fn - fp)
        th, tp, tq = (jnp.where(keep, 0.5 * x, 0.0) for x in (th, tp, tq))
        height, down, across = (grid.get(mid, k, col) for k in range(3))
        inv, u, v = velocities(height, down, across)
        above = jnp.where(height > DEPTH_FLOOR, 1.0, jnp.where(height == DEPTH_FLOOR, 0.5, 0.0))
        turb_of = grid.get(kept, FB, col)
        dry_of = grid.get(kept, FA, col)
        inv_speed, dry, turb = friction(height, u, v, dry_of, turb_of)
        z = (turb_of - dry * inv_speed) * inv_speed * inv
        w = (dry + turb) * inv
        y = dry_of * inv_speed - above * (z * (u * u + v * v) + w)
        eight = COS_SLOPE * height
        for k, value in ((MU, u), (MV, v), (MZ, z), (MW, w), (ME, dry), (MB, turb), (MM, above), (MH, eight), (MY, y)):
            grid.put(at_mid, k, col, value)
        along = z * (u * tp + v * tq) + y * th
        along += dry * grid.get(kept, DM, col) - turb * grid.get(kept, DX, col)
        lift = above * th
        flux_down = 2.0 * u * tp + eight * th - u * u * lift
        mixed = v * tp + u * tq - u * v * lift
        for k, value in enumerate((th, tp, tq, mixed, 2.0 * v * tq + eight * th - v * v * lift)):
            grid.spare_put(work, k, col, value)
        hn, hp = grid.both_rows(th)
        pn, pp = grid.both_rows(tp)
        qn, qp = grid.both_rows(tq)
        fn, fp = grid.both_rows(flux_down)
        gn, gp = grid.both_rows(mixed)
        grid.put(part, 0, col, 0.6 * th + 0.1 * (hn + hp))
        grid.put(part, 1, col, 0.6 * tp + 0.1 * (pn + pp))
        grid.put(part, 2, col, 0.6 * tq + 0.1 * (qn + qp))
        grid.put(part, 3, col, -0.5 * (pn - pp))
        grid.put(part, 4, col, SIN_SLOPE * th - u * along - w * tp - 0.5 * (fn - fp))
        grid.put(part, 5, col, -v * along - w * tq - 0.5 * (gn - gp))

    grid.sweep(second)


def tangent_end(part, work, tan):
    grid = Grid(part.shape[1], part.shape[2])

    def third(t, col):
        keep = grid.inside(t)
        hn, hp = grid.both_cols(work, 0, col)
        pn, pp = grid.both_cols(work, 1, col)
        qn, qp = grid.both_cols(work, 2, col)
        gn, gp = grid.both_cols(work, 3, col)
        fn, fp = grid.both_cols(work, 4, col)
        for k, (n, p) in enumerate(((hn, hp), (pn, pp), (qn, qp))):
            grid.spare_put(tan, k, col, jnp.where(keep, grid.get(part, k, col) + 0.1 * (n + p), 0.0))
        for k, (n, p) in enumerate(((qn, qp), (gn, gp), (fn, fp))):
            grid.spare_put(tan, 3 + k, col, jnp.where(keep, grid.get(part, 3 + k, col) - 0.5 * (n - p), 0.0))

    grid.sweep(third)


def finish(cells, top, last, fast, fast_last, kept, at_one, at_mid, between, tan, smooth, out_mu, out_xi, work, total):
    grid = Grid(kept.shape[1], kept.shape[2])
    shape = grid.lane.shape
    dt0 = step_length(top, last, shape)
    dt1 = step_length(fast, fast_last, shape)
    weight = jnp.broadcast_to((DATA_WEIGHT * cells) / known(fast, fast_last, 1), shape)
    half1 = 0.5 * dt1
    half0 = 0.5 * dt0

    def seed_end(t, col):
        def section(k, off):
            return grid.spare_get(tan, k, col, off) + dt1 * grid.spare_get(tan, 3 + k, col, off)

        th, tp = section(0, 0), section(1, 0)
        tenth, moved = 0.1 * th, half1 * tp
        value = grid.spare_get(between, 0, col) + 0.6 * th
        value += grid.rows_next(tenth - moved) + grid.rows_prev(tenth + moved)
        value += 0.1 * (section(0, 1) + section(0, -1)) - half1 * (section(2, 1) - section(2, -1))
        grid.spare_put(work, 0, col, weight * grid.get(kept, OB, col) * (0.5 * value))

    grid.sweep(seed_end)

    def back_second(t, col):
        keep = grid.inside(t)
        seed = grid.spare_get(work, 0, col)
        rn, rp = grid.both_rows(seed)
        cn, cp = grid.both_cols(work, 0, col)
        grid.spare_put(work, 1, col, jnp.where(keep, 0.3 * seed + 0.05 * (rn + rp + cn + cp), 0.0))
        grid.spare_put(work, 2, col, jnp.where(keep, 0.5 * half1 * (rn - rp), 0.0))
        grid.spare_put(work, 3, col, jnp.where(keep, 0.5 * half1 * (cn - cp), 0.0))

    grid.sweep(back_second)

    def back_first(t, col):
        keep = grid.inside(t)
        g0, g1, g2 = (grid.spare_get(work, 1 + k, col) for k in range(3))
        r0n, r0p = grid.both_rows(g0)
        r1n, r1p = grid.both_rows(g1)
        r2n, r2p = grid.both_rows(g2)
        c0n, c0p = grid.both_cols(work, 1, col)
        c1n, c1p = grid.both_cols(work, 2, col)
        c2n, c2p = grid.both_cols(work, 3, col)
        u, v = grid.get(at_mid, MU, col), grid.get(at_mid, MV, col)
        z, w = grid.get(at_mid, MZ, col), grid.get(at_mid, MW, col)
        down = half1 * (r1n - r1p)
        cross = half1 * ((r2n - r2p) + (c1n - c1p))
        side = half1 * (c2n - c2p)
        h1, h2 = dt1 * g1, dt1 * g2
        along = u * h1 + v * h2
        grid.put(total, 0, col, -grid.get(at_mid, ME, col) * along)
        grid.put(total, 1, col, grid.get(at_mid, MB, col) * along)
        pull = z * along
        part_u = u * down + v * cross
        part_v = v * side
        m0 = 0.5 * grid.spare_get(work, 0, col) + 0.6 * g0 + 0.1 * (r0n + r0p + c0n + c0p)
        m0 += SIN_SLOPE * h1 - grid.get(at_mid, MY, col) * along + grid.get(at_mid, MH, col) * (down + side)
        m0 -= grid.get(at_mid, MM, col) * (u * part_u + v * part_v)
        m1 = 0.6 * g1 + 0.1 * (r1n + r1p + c1n + c1p)
        m1 += half1 * (r0n - r0p) + u * (down - pull) + part_u - w * h1
        m2 = 0.6 * g2 + 0.1 * (r2n + r2p + c2n + c2p)
        m2 += half1 * (c0n - c0p) + u * cross + 2.0 * part_v - v * pull - w * h2
        for k, value in enumerate((m0, m1, m2)):
            grid.spare_put(work, 4 + k, col, jnp.where(keep, value, 0.0))

    grid.sweep(back_first)

    def early(t, col):
        m0, m1, m2 = (grid.spare_get(work, 4 + k, col) for k in range(3))
        r0n, r0p = grid.both_rows(m0)
        r1n, r1p = grid.both_rows(m1)
        r2n, r2p = grid.both_rows(m2)
        c0n, c0p = grid.both_cols(work, 4, col)
        c1n, c1p = grid.both_cols(work, 5, col)
        c2n, c2p = grid.both_cols(work, 6, col)
        u, v = grid.get(at_one, CU, col), grid.get(at_one, CV, col)
        z, w = grid.get(at_one, CZ, col), grid.get(at_one, CW, col)
        quarter = 0.5 * half0
        down = quarter * (r1n - r1p)
        cross = quarter * ((r2n - r2p) + (c1n - c1p))
        side = quarter * (c2n - c2p)
        p1, p2 = half0 * m1, half0 * m2
        along = u * p1 + v * p2
        pull = z * along
        f1 = 0.3 * m1 + 0.05 * (r1n + r1p + c1n + c1p)
        f1 += quarter * (r0n - r0p) + 2.0 * u * down + v * cross - u * pull - w * p1
        f2 = 0.3 * m2 + 0.05 * (r2n + r2p + c2n + c2p)
        f2 += quarter * (c0n - c0p) + u * cross + 2.0 * v * side - v * pull - w * p2
        height, down, across = (grid.get(kept, k, col) for k in (H, Q1, Q2))
        _, u, v = velocities(height, down, across)
        _, dry, turb = friction(height, u, v, grid.get(kept, FA, col), grid.get(kept, FB, col))
        start = dt0 * (u * f1 + v * f2)
        mu = grid.get(total, 0, col) + grid.get(smooth, 0, col - TILE)
        xi = grid.get(total, 1, col) + grid.get(smooth, 1, col - TILE)
        grid.put(total, 0, col, mu - grid.get(at_one, CE, col) * along - dry * start)
        grid.put(total, 1, col, xi + grid.get(at_one, CB, col) * along + turb * start)

    grid.sweep_own(early)

    cols = out_mu.shape[1]
    for g in range(grid.groups):
        at = pl.ds(g * LANES, LANES)
        out_mu[at, :] = total[0, g, TILE : TILE + cols, :].T
        out_xi[at, :] = total[1, g, TILE : TILE + cols, :].T


VMEM = pl.BlockSpec(memory_space=pltpu.VMEM)
ANY = pl.BlockSpec(memory_space=pltpu.HBM)


def call(body, name, operands, outs, scratch, flops, spaces=None, aliases=None):
    outs = [jax.ShapeDtypeStruct(shape, jnp.float32) for shape in outs]
    moved = 4 * sum(x.size for x in operands) + 4 * sum(x.size for x in outs)
    return pl.pallas_call(
        body,
        name=name,
        out_shape=outs,
        in_specs=spaces or [VMEM] * len(operands),
        out_specs=[VMEM] * len(outs),
        scratch_shapes=[pltpu.VMEM(x, jnp.float32) if isinstance(x, tuple) else x for x in scratch],
        input_output_aliases=aliases or {},
        compiler_params=pltpu.CompilerParams(vmem_limit_bytes=24 * 1024 * 1024),
        cost_estimate=pl.CostEstimate(flops=flops, bytes_accessed=moved, transcendentals=0),
    )(*operands)


def swap(value, other):
    count = lax.axis_size("cross")
    return lax.ppermute(value, "cross", [(i, other(i) if 0 <= other(i) < count else i) for i in range(count)])


def other_core(i):
    return i ^ 1


def next_chip(i):
    return i - 1 if i % 2 == 0 else i + 1


def odd_far(step):
    return lambda i: i ^ step if i % 2 == 1 else i


def max_and_sum(a, b):
    return jnp.where(lax.broadcasted_iota(jnp.int32, a.shape, 0) == 0, jnp.maximum(a, b), a + b)


def round_beside(row, other, result=None):
    arrived = swap(row, other)
    if result is not None:
        arrived, result = lax.optimization_barrier((arrived, result))
    return max_and_sum(row, arrived), result


def local(state, log_mu, log_xi, dir_mu, dir_xi, wet, observed, terrain, class_weight):
    rows, cols = log_mu.shape
    groups = rows // LANES
    count = lax.axis_size("cross")
    own = (groups, cols, LANES)
    wide = (groups, cols + 2 * TILE, LANES)
    spare = (groups, cols + 4 * TILE, LANES)
    edge = (SHARED, groups, TILE, LANES)
    work = rows * cols

    inputs = (state, log_mu, log_xi, dir_mu, dir_xi, wet, observed, terrain, class_weight)
    inputs = tuple(pltpu.with_memory_space_constraint(x, pltpu.HBM) for x in inputs)
    kept, weights, edge_a, edge_b, row, count_row = call(
        prepare,
        "prepare",
        inputs,
        [(KEPT,) + wide, (1,) + wide, edge, edge, (1, LANES), (1, LANES)],
        [(rows, cols), (3,) + own]
        + [pltpu.VMEM(x.shape, x.dtype) for x in inputs[:-1]]
        + [pltpu.SMEM(class_weight.shape, jnp.float32), pltpu.SemaphoreType.DMA((len(inputs),))],
        100 * work,
        spaces=[ANY] * len(inputs),
    )
    steps = [2**k for k in range(1, count.bit_length() - 1)]
    edge_a = swap(edge_a, other_core)
    row = jnp.maximum(row, swap(row, other_core))
    for step in steps[:-1]:
        row = jnp.maximum(row, swap(row, odd_far(step)))
        if step == 2:
            row, edge_b = lax.optimization_barrier((row, edge_b))
            edge_b = swap(edge_b, next_chip)
    kept, weights, xy, change = call(
        open_step,
        "open_step",
        (kept, weights, edge_a, edge_b),
        [(KEPT,) + wide, (1,) + wide, (6,) + wide, (2,) + wide],
        [(5,) + spare],
        100 * work,
        aliases={0: 0, 1: 1},
    )
    arrived, xy = lax.optimization_barrier((swap(row, odd_far(steps[-1])), xy))
    top = jnp.maximum(row, arrived)
    last = swap(top, other_core)
    at_one, mid, row = call(
        middle,
        "middle",
        (top, last, kept, xy, count_row),
        [(6,) + wide, (3,) + wide, (2, LANES)],
        [(5,) + spare],
        120 * work,
    )
    (smooth,) = call(regularize, "regularize", (kept, weights), [(2,) + own], [(4,) + spare], 30 * work)
    row, smooth = round_beside(row, other_core, smooth)
    one, part = call(
        tangent_one, "tangent_one", (top, last, kept, change, at_one), [(4,) + spare, (3,) + wide], [], 60 * work
    )
    row, one = round_beside(row, odd_far(steps[0]), one)
    part, at_mid, between = call(
        tangent_mid,
        "tangent_mid",
        (top, last, kept, mid, one, part),
        [(6,) + wide, (9,) + wide, (5,) + spare],
        [],
        120 * work,
    )
    row, part = round_beside(row, odd_far(steps[1]), part)
    (tan,) = call(tangent_end, "tangent_end", (part, between), [(6,) + spare], [], 30 * work)
    row, tan = round_beside(row, odd_far(steps[2]), tan)
    for step in steps[3:]:
        row, _ = round_beside(row, odd_far(step))
    return call(
        functools.partial(finish, float(rows * cols * count)),
        "finish",
        (top, last, row, swap(row, other_core), kept, at_one, at_mid, between, tan, smooth),
        [(rows, cols), (rows, cols)],
        [(7,) + spare, (2,) + wide],
        300 * work,
    )


def solution(mesh):
    return jax.shard_map(
        local,
        mesh=mesh,
        in_specs=(
            P(None, "grp", "cross"),
            P("grp", "cross"),
            P("grp", "cross"),
            P("grp", "cross"),
            P("grp", "cross"),
            P("grp", "cross"),
            P("grp", "cross"),
            P("grp", "cross"),
            P(),
        ),
        out_specs=(P("grp", "cross"), P("grp", "cross")),
        check_vma=False,
    )
```

```python
import functools

import jax
import jax.numpy as jnp
from jax import lax
from jax.experimental import pallas as pl
from jax.experimental.pallas import tpu as pltpu
from jax.sharding import PartitionSpec as P

COS_SLOPE = 0.8
SIN_SLOPE = 0.6
DEPTH_FLOOR = 0.05
SPEED_EPS = 0.01
COURANT = 0.2
DATA_WEIGHT = 100000.0

LANES = 128
TILE = 8
H, Q1, Q2, FA, FB, DM, DX, OB, WR = range(9)
KEPT = 8
SHARED = 9
UNROLL = 6


class Grid:
    def __init__(self, groups, wide):
        self.groups = groups
        self.tiles = wide // TILE
        self.lane = lax.broadcasted_iota(jnp.int32, (groups * TILE, LANES), 1)
        self.blank = jnp.zeros((TILE, LANES), jnp.float32)
        me = lax.axis_index("cross")
        self.ends = (me == 0, me == lax.axis_size("cross") - 1)

    def rows_next(self, v):
        turned = pltpu.roll(v, LANES - 1, 1)
        after = jnp.concatenate([turned[TILE:], self.blank], axis=0)
        return jnp.where(self.lane == LANES - 1, after, turned)

    def rows_prev(self, v):
        turned = pltpu.roll(v, 1, 1)
        before = jnp.concatenate([self.blank, turned[:-TILE]], axis=0)
        return jnp.where(self.lane == 0, before, turned)

    def both_rows(self, v):
        return self.rows_next(v), self.rows_prev(v)

    def get(self, ref, k, col):
        return jnp.concatenate([ref[k, g, pl.ds(col, TILE), :] for g in range(self.groups)], axis=0)

    def put(self, ref, k, col, value):
        for g in range(self.groups):
            ref[k, g, pl.ds(col, TILE), :] = value[g * TILE : (g + 1) * TILE]

    def spare_get(self, ref, k, col, off=0):
        return self.get(ref, k, col + TILE + off)

    def spare_put(self, ref, k, col, value):
        self.put(ref, k, col + TILE, value)

    def both_cols(self, ref, k, col):
        return self.spare_get(ref, k, col, 1), self.spare_get(ref, k, col, -1)

    def sweep(self, body, first=0, last=None, carry=None):
        last = self.tiles if last is None else last
        steps, rest = divmod(last - first, UNROLL)

        def visit(t, col, carry):
            return body(t, col) if carry is None else body(t, col, carry)

        def step(i, carry):
            for u in range(UNROLL):
                t = first + i * UNROLL + u
                carry = visit(t, pl.multiple_of(t * TILE, TILE), carry)
            return carry

        carry = lax.fori_loop(0, steps, step, carry)
        for t in range(last - rest, last):
            carry = visit(t, t * TILE, carry)
        return carry

    def sweep_own(self, body):
        self.sweep(body, 1, self.tiles - 1)

    def inside(self, t):
        return jnp.logical_not(((t == 0) & self.ends[0]) | ((t == self.tiles - 1) & self.ends[1]))


def speed_of(height, down, across):
    inv = 1.0 / jnp.maximum(height, DEPTH_FLOOR)
    vel_down = down * inv
    vel_across = across * inv
    return jnp.sqrt(vel_down * vel_down + vel_across * vel_across) + jnp.sqrt(COS_SLOPE * jnp.maximum(height, 0.0))


def velocities(height, down, across):
    inv = 1.0 / jnp.maximum(height, DEPTH_FLOOR)
    return inv, down * inv, across * inv


def friction(height, vel_down, vel_across, dry, turbulent):
    squared = vel_down * vel_down + vel_across * vel_across + SPEED_EPS
    inv_speed = lax.rsqrt(squared)
    return inv_speed, dry * height * inv_speed, turbulent * (squared * inv_speed)


def step_length(row, last, shape):
    return COURANT / jnp.broadcast_to(jnp.maximum(row[:1, :], last[:1, :]), shape)


def first_speed(state, row, held, arrived):
    rows, cols = state.shape[1:]
    parts = held.shape[0]
    size = rows // parts
    copies = []
    for i in range(parts):
        copies.append(pltpu.make_async_copy(state.at[:, pl.ds(i * size, size), :], held.at[i], arrived.at[i]))
        copies[i].start()
    top = jnp.zeros((16, cols), jnp.float32)
    for i in range(parts):
        copies[i].wait()
        for j in range(0, size, 16):
            top = jnp.maximum(top, speed_of(*(held[i, k, j : j + 16, :] for k in range(3))))
    row[...] = jnp.full(row.shape, jnp.max(top), jnp.float32)


def prepare(*refs):
    sources = refs[:9]
    kept, weights, edge_a, edge_b, count_row, code, turned = refs[10:17]
    held, arrived = refs[17:26], refs[26]
    copies = [pltpu.make_async_copy(src, dst, arrived.at[i]) for i, (src, dst) in enumerate(zip(sources, held))]
    for i in (0, 6, 5, 7, 3, 4, 1, 2, 8):
        copies[i].start()
    state, log_mu, log_xi, dir_mu, dir_xi, wet, observed, terrain, class_weight = held
    rows, cols = log_mu.shape
    groups = rows // LANES
    own = pl.ds(TILE, cols)

    copies[0].wait()
    for g in range(groups):
        for k in range(3):
            kept[k, g, own, :] = state[k, pl.ds(g * LANES, LANES), :].T

    for i in (6, 5, 7):
        copies[i].wait()
    seen = jnp.zeros((16, cols), jnp.float32)
    for i in range(0, rows, 16):
        seen_here = observed[i : i + 16, :]
        code[i : i + 16, :] = (wet[i : i + 16, :] + 2 * seen_here + 4 * terrain[i : i + 16, :]).astype(jnp.float32)
        seen += seen_here.astype(jnp.float32)
    count_row[...] = jnp.full(count_row.shape, jnp.sum(seen), jnp.float32)

    for i in (3, 4, 1, 2, 8):
        copies[i].wait()
    for g in range(groups):
        at = pl.ds(g * LANES, LANES)
        turned[2, g] = code[at, :].T
        kept[DM, g, own, :] = dir_mu[at, :].T
        kept[DX, g, own, :] = dir_xi[at, :].T
        turned[0, g] = log_mu[at, :].T
        turned[1, g] = log_xi[at, :].T

    def derive(i, carry):
        for g, half in ((g, half) for g in range(groups) for half in range(2)):
            at = pl.ds(pl.multiple_of((2 * i + half) * TILE, TILE), TILE)
            to = pl.ds(pl.multiple_of((2 * i + half + 1) * TILE, TILE), TILE)
            bits = turned[2, g, at, :].astype(jnp.int32)
            wet_here = (bits & 1).astype(jnp.float32)
            kind = bits >> 2
            kept[FA, g, to, :] = wet_here * jnp.exp(turned[0, g, at, :]) * COS_SLOPE
            kept[FB, g, to, :] = wet_here * jnp.exp(-turned[1, g, at, :])
            kept[OB, g, to, :] = ((bits >> 1) & 1).astype(jnp.float32)
            weight = jnp.zeros((TILE, LANES), jnp.float32)
            for c in range(class_weight.shape[0]):
                weight = jnp.where(kind == c, class_weight[c], weight)
            weights[0, g, to, :] = weight
        return carry

    lax.fori_loop(0, cols // (2 * TILE), derive, 0)
    even = lax.rem(lax.axis_index("cross"), 2) == 0
    for k in range(SHARED):
        ref, j = (kept, k) if k < KEPT else (weights, 0)
        for g in range(groups):
            left = ref[j, g, TILE : 2 * TILE, :]
            right = ref[j, g, cols : cols + TILE, :]
            edge_a[k, g] = jnp.where(even, right, left)
            edge_b[k, g] = jnp.where(even, left, right)


def fill_halo(source, ref, j, k, edge_a, edge_b):
    me = lax.axis_index("cross")
    even = lax.rem(me, 2) == 0
    first, last = me == 0, me == lax.axis_size("cross") - 1
    wide = ref.shape[2]
    for g in range(ref.shape[1]):
        ref[j, g, TILE : wide - TILE, :] = source[j, g, TILE : wide - TILE, :]
        ref[j, g, :TILE, :] = jnp.where(first, 0.0, jnp.where(even, edge_b[k, g], edge_a[k, g]))
        ref[j, g, wide - TILE :, :] = jnp.where(last, 0.0, jnp.where(even, edge_a[k, g], edge_b[k, g]))


def open_step(kept_in, weights_in, edge_a, edge_b, kept, weights, xy, change, work):
    grid = Grid(kept.shape[1], kept.shape[2])
    for k in range(KEPT):
        fill_halo(kept_in, kept, k, k, edge_a, edge_b)
    fill_halo(weights_in, weights, 0, WR, edge_a, edge_b)

    def first(t, col):
        height, down, across = (grid.get(kept, k, col) for k in (H, Q1, Q2))
        _, u, v = velocities(height, down, across)
        _, dry, turb = friction(height, u, v, grid.get(kept, FA, col), grid.get(kept, FB, col))
        moved = dry * grid.get(kept, DM, col) - turb * grid.get(kept, DX, col)
        grid.put(change, 0, col, -u * moved)
        grid.put(change, 1, col, -v * moved)
        drag = dry + turb
        pressure = 0.5 * COS_SLOPE * height * height
        mixed = down * v
        for k, value in enumerate((height, down, across, mixed, across * v + pressure)):
            grid.spare_put(work, k, col, value)
        hn, hp = grid.both_rows(height)
        pn, pp = grid.both_rows(down)
        qn, qp = grid.both_rows(across)
        fn, fp = grid.both_rows(down * u + pressure)
        gn, gp = grid.both_rows(mixed)
        grid.put(xy, 0, col, 0.6 * height + 0.1 * (hn + hp))
        grid.put(xy, 1, col, 0.6 * down + 0.1 * (pn + pp))
        grid.put(xy, 2, col, 0.6 * across + 0.1 * (qn + qp))
        grid.put(xy, 3, col, -0.5 * (pn - pp))
        grid.put(xy, 4, col, SIN_SLOPE * height - drag * u - 0.5 * (fn - fp))
        grid.put(xy, 5, col, -drag * v - 0.5 * (gn - gp))

    grid.sweep(first)

    def second(t, col):
        hn, hp = grid.both_cols(work, 0, col)
        pn, pp = grid.both_cols(work, 1, col)
        qn, qp = grid.both_cols(work, 2, col)
        gn, gp = grid.both_cols(work, 3, col)
        fn, fp = grid.both_cols(work, 4, col)
        for k, (n, p) in enumerate(((hn, hp), (pn, pp), (qn, qp))):
            grid.put(xy, k, col, grid.get(xy, k, col) + 0.1 * (n + p))
        for k, (n, p) in enumerate(((qn, qp), (gn, gp), (fn, fp))):
            grid.put(xy, 3 + k, col, grid.get(xy, 3 + k, col) - 0.5 * (n - p))

    grid.sweep(second)


CU, CV, CZ, CW, CE, CB = range(6)
MU, MV, MZ, MW, ME, MB, MM, MH, MY = range(9)


def middle(top, last, kept, xy, count_row, at_one, mid, row, work):
    grid = Grid(kept.shape[1], kept.shape[2])
    dt = step_length(top, last, grid.lane.shape)
    half = 0.5 * dt

    def first(t, col):
        keep = grid.inside(t)
        height, down, across = (
            jnp.where(keep, grid.get(xy, k, col) + dt * grid.get(xy, 3 + k, col), 0.0) for k in range(3)
        )
        inv, u, v = velocities(height, down, across)
        turb_of = grid.get(kept, FB, col)
        inv_speed, dry, turb = friction(height, u, v, grid.get(kept, FA, col), turb_of)
        drag = dry + turb
        grid.put(at_one, CU, col, u)
        grid.put(at_one, CV, col, v)
        grid.put(at_one, CZ, col, (turb_of - dry * inv_speed) * inv_speed * inv)
        grid.put(at_one, CW, col, drag * inv)
        grid.put(at_one, CE, col, dry)
        grid.put(at_one, CB, col, turb)
        pressure = 0.5 * COS_SLOPE * height * height
        mixed = down * v
        for k, value in enumerate((height, down, across, mixed, across * v + pressure)):
            grid.spare_put(work, k, col, value)
        sources = (0.0, dt * (SIN_SLOPE * height - drag * u), -dt * drag * v)
        for k, (value, flux) in enumerate(((height, down), (down, down * u + pressure), (across, mixed))):
            tenth, moved = 0.1 * value, half * flux
            total = grid.get(kept, k, col) + 0.6 * value + sources[k]
            total += grid.rows_next(tenth - moved) + grid.rows_prev(tenth + moved)
            grid.put(mid, k, col, total)

    grid.sweep(first)

    def second(t, col, most):
        keep = grid.inside(t)
        found = []
        for k, (value, flux) in enumerate(((0, 2), (1, 3), (2, 4))):
            vn, vp = grid.both_cols(work, value, col)
            fn, fp = grid.both_cols(work, flux, col)
            total = grid.get(mid, k, col) + 0.1 * (vn + vp) - half * (fn - fp)
            found.append(jnp.where(keep, 0.5 * total, 0.0))
            grid.put(mid, k, col, found[k])
        own = (t > 0) & (t < grid.tiles - 1)
        return jnp.maximum(most, jnp.where(own, speed_of(*found), 0.0))

    fastest = grid.sweep(second, carry=jnp.zeros(grid.lane.shape, jnp.float32))
    row[0:1, :] = jnp.full((1, LANES), jnp.max(fastest), jnp.float32)
    row[1:2, :] = count_row[...]


def regularize(kept, weights, smooth, bent):
    grid = Grid(kept.shape[1], kept.shape[2])

    def spread(t, col):
        for k, field in enumerate((DM, DX)):
            grid.spare_put(bent, k, col, grid.get(kept, field, col))

    grid.sweep(spread)

    def laplace(k, col):
        value = grid.spare_get(bent, k, col)
        rn, rp = grid.both_rows(value)
        cn, cp = grid.both_cols(bent, k, col)
        return 4.0 * value - rn - rp - cn - cp

    def bend(t, col):
        weight = grid.get(weights, 0, col)
        for k in range(2):
            grid.spare_put(bent, 2 + k, col, weight * laplace(k, col))

    grid.sweep(bend)

    def bend_again(t, col):
        for k in range(2):
            grid.put(smooth, k, col - TILE, laplace(2 + k, col))

    grid.sweep_own(bend_again)


def tangent_one(top, last, kept, change, at_one, one, part):
    grid = Grid(kept.shape[1], kept.shape[2])
    dt = step_length(top, last, grid.lane.shape)
    half = 0.5 * dt

    def first(t, col):
        tp, tq = dt * grid.get(change, 0, col), dt * grid.get(change, 1, col)
        u, v = grid.get(at_one, CU, col), grid.get(at_one, CV, col)
        w = grid.get(at_one, CW, col)
        moved = grid.get(at_one, CE, col) * grid.get(kept, DM, col) - grid.get(at_one, CB, col) * grid.get(kept, DX, col)
        along = grid.get(at_one, CZ, col) * (u * tp + v * tq) + moved
        mixed = v * tp + u * tq
        for k, value in enumerate((tp, tq, mixed, 2.0 * v * tq)):
            grid.spare_put(one, k, col, value)
        moved = half * tp
        grid.put(part, 0, col, grid.rows_prev(moved) - grid.rows_next(moved))
        sources = (-dt * (u * along + w * tp), -dt * (v * along + w * tq))
        for k, (value, flux) in enumerate(((tp, 2.0 * u * tp), (tq, mixed))):
            tenth, moved = 0.1 * value, half * flux
            total = 0.6 * value + sources[k]
            total += grid.rows_next(tenth - moved) + grid.rows_prev(tenth + moved)
            grid.put(part, 1 + k, col, total)

    grid.sweep(first)


def tangent_mid(top, last, kept, mid, one, part_one, part, at_mid, work):
    grid = Grid(kept.shape[1], kept.shape[2])
    dt = step_length(top, last, grid.lane.shape)
    half = 0.5 * dt

    def second(t, col):
        keep = grid.inside(t)
        qn, qp = grid.both_cols(one, 1, col)
        pn, pp = grid.both_cols(one, 0, col)
        gn, gp = grid.both_cols(one, 2, col)
        fn, fp = grid.both_cols(one, 3, col)
        th = grid.get(part_one, 0, col) - half * (qn - qp)
        tp = grid.get(part_one, 1, col) + 0.1 * (pn + pp) - half * (gn - gp)
        tq = grid.get(part_one, 2, col) + 0.1 * (qn + qp) - half * (fn - fp)
        th, tp, tq = (jnp.where(keep, 0.5 * x, 0.0) for x in (th, tp, tq))
        height, down, across = (grid.get(mid, k, col) for k in range(3))
        inv, u, v = velocities(height, down, across)
        above = jnp.where(height > DEPTH_FLOOR, 1.0, jnp.where(height == DEPTH_FLOOR, 0.5, 0.0))
        turb_of = grid.get(kept, FB, col)
        dry_of = grid.get(kept, FA, col)
        inv_speed, dry, turb = friction(height, u, v, dry_of, turb_of)
        z = (turb_of - dry * inv_speed) * inv_speed * inv
        w = (dry + turb) * inv
        y = dry_of * inv_speed - above * (z * (u * u + v * v) + w)
        eight = COS_SLOPE * height
        for k, value in ((MU, u), (MV, v), (MZ, z), (MW, w), (ME, dry), (MB, turb), (MM, above), (MH, eight), (MY, y)):
            grid.put(at_mid, k, col, value)
        along = z * (u * tp + v * tq) + y * th
        along += dry * grid.get(kept, DM, col) - turb * grid.get(kept, DX, col)
        lift = above * th
        flux_down = 2.0 * u * tp + eight * th - u * u * lift
        mixed = v * tp + u * tq - u * v * lift
        for k, value in enumerate((th, tp, tq, mixed, 2.0 * v * tq + eight * th - v * v * lift)):
            grid.spare_put(work, k, col, value)
        hn, hp = grid.both_rows(th)
        pn, pp = grid.both_rows(tp)
        qn, qp = grid.both_rows(tq)
        fn, fp = grid.both_rows(flux_down)
        gn, gp = grid.both_rows(mixed)
        grid.put(part, 0, col, 0.6 * th + 0.1 * (hn + hp))
        grid.put(part, 1, col, 0.6 * tp + 0.1 * (pn + pp))
        grid.put(part, 2, col, 0.6 * tq + 0.1 * (qn + qp))
        grid.put(part, 3, col, -0.5 * (pn - pp))
        grid.put(part, 4, col, SIN_SLOPE * th - u * along - w * tp - 0.5 * (fn - fp))
        grid.put(part, 5, col, -v * along - w * tq - 0.5 * (gn - gp))

    grid.sweep(second)


def tangent_end(part, work, tan):
    grid = Grid(part.shape[1], part.shape[2])

    def third(t, col):
        keep = grid.inside(t)
        hn, hp = grid.both_cols(work, 0, col)
        pn, pp = grid.both_cols(work, 1, col)
        qn, qp = grid.both_cols(work, 2, col)
        gn, gp = grid.both_cols(work, 3, col)
        fn, fp = grid.both_cols(work, 4, col)
        for k, (n, p) in enumerate(((hn, hp), (pn, pp), (qn, qp))):
            grid.spare_put(tan, k, col, jnp.where(keep, grid.get(part, k, col) + 0.1 * (n + p), 0.0))
        for k, (n, p) in enumerate(((qn, qp), (gn, gp), (fn, fp))):
            grid.spare_put(tan, 3 + k, col, jnp.where(keep, grid.get(part, 3 + k, col) - 0.5 * (n - p), 0.0))

    grid.sweep(third)


def finish(cells, top, last, fast, fast_last, kept, at_one, at_mid, between, tan, smooth, out_mu, out_xi, work, total):
    grid = Grid(kept.shape[1], kept.shape[2])
    shape = grid.lane.shape
    dt0 = step_length(top, last, shape)
    dt1 = step_length(fast, fast_last, shape)
    weight = jnp.broadcast_to((DATA_WEIGHT * cells) / (fast[1:2, :] + fast_last[1:2, :]), shape)
    half1 = 0.5 * dt1
    half0 = 0.5 * dt0

    def seed_end(t, col):
        def section(k, off):
            return grid.spare_get(tan, k, col, off) + dt1 * grid.spare_get(tan, 3 + k, col, off)

        th, tp = section(0, 0), section(1, 0)
        tenth, moved = 0.1 * th, half1 * tp
        value = grid.spare_get(between, 0, col) + 0.6 * th
        value += grid.rows_next(tenth - moved) + grid.rows_prev(tenth + moved)
        value += 0.1 * (section(0, 1) + section(0, -1)) - half1 * (section(2, 1) - section(2, -1))
        grid.spare_put(work, 0, col, weight * grid.get(kept, OB, col) * (0.5 * value))

    grid.sweep(seed_end)

    def back_second(t, col):
        keep = grid.inside(t)
        seed = grid.spare_get(work, 0, col)
        rn, rp = grid.both_rows(seed)
        cn, cp = grid.both_cols(work, 0, col)
        grid.spare_put(work, 1, col, jnp.where(keep, 0.3 * seed + 0.05 * (rn + rp + cn + cp), 0.0))
        grid.spare_put(work, 2, col, jnp.where(keep, 0.5 * half1 * (rn - rp), 0.0))
        grid.spare_put(work, 3, col, jnp.where(keep, 0.5 * half1 * (cn - cp), 0.0))

    grid.sweep(back_second)

    def back_first(t, col):
        keep = grid.inside(t)
        g0, g1, g2 = (grid.spare_get(work, 1 + k, col) for k in range(3))
        r0n, r0p = grid.both_rows(g0)
        r1n, r1p = grid.both_rows(g1)
        r2n, r2p = grid.both_rows(g2)
        c0n, c0p = grid.both_cols(work, 1, col)
        c1n, c1p = grid.both_cols(work, 2, col)
        c2n, c2p = grid.both_cols(work, 3, col)
        u, v = grid.get(at_mid, MU, col), grid.get(at_mid, MV, col)
        z, w = grid.get(at_mid, MZ, col), grid.get(at_mid, MW, col)
        down = half1 * (r1n - r1p)
        cross = half1 * ((r2n - r2p) + (c1n - c1p))
        side = half1 * (c2n - c2p)
        h1, h2 = dt1 * g1, dt1 * g2
        along = u * h1 + v * h2
        grid.put(total, 0, col, -grid.get(at_mid, ME, col) * along)
        grid.put(total, 1, col, grid.get(at_mid, MB, col) * along)
        pull = z * along
        part_u = u * down + v * cross
        part_v = v * side
        m0 = 0.5 * grid.spare_get(work, 0, col) + 0.6 * g0 + 0.1 * (r0n + r0p + c0n + c0p)
        m0 += SIN_SLOPE * h1 - grid.get(at_mid, MY, col) * along + grid.get(at_mid, MH, col) * (down + side)
        m0 -= grid.get(at_mid, MM, col) * (u * part_u + v * part_v)
        m1 = 0.6 * g1 + 0.1 * (r1n + r1p + c1n + c1p)
        m1 += half1 * (r0n - r0p) + u * (down - pull) + part_u - w * h1
        m2 = 0.6 * g2 + 0.1 * (r2n + r2p + c2n + c2p)
        m2 += half1 * (c0n - c0p) + u * cross + 2.0 * part_v - v * pull - w * h2
        for k, value in enumerate((m0, m1, m2)):
            grid.spare_put(work, 4 + k, col, jnp.where(keep, value, 0.0))

    grid.sweep(back_first)

    def early(t, col):
        m0, m1, m2 = (grid.spare_get(work, 4 + k, col) for k in range(3))
        r0n, r0p = grid.both_rows(m0)
        r1n, r1p = grid.both_rows(m1)
        r2n, r2p = grid.both_rows(m2)
        c0n, c0p = grid.both_cols(work, 4, col)
        c1n, c1p = grid.both_cols(work, 5, col)
        c2n, c2p = grid.both_cols(work, 6, col)
        u, v = grid.get(at_one, CU, col), grid.get(at_one, CV, col)
        z, w = grid.get(at_one, CZ, col), grid.get(at_one, CW, col)
        quarter = 0.5 * half0
        down = quarter * (r1n - r1p)
        cross = quarter * ((r2n - r2p) + (c1n - c1p))
        side = quarter * (c2n - c2p)
        p1, p2 = half0 * m1, half0 * m2
        along = u * p1 + v * p2
        pull = z * along
        f1 = 0.3 * m1 + 0.05 * (r1n + r1p + c1n + c1p)
        f1 += quarter * (r0n - r0p) + 2.0 * u * down + v * cross - u * pull - w * p1
        f2 = 0.3 * m2 + 0.05 * (r2n + r2p + c2n + c2p)
        f2 += quarter * (c0n - c0p) + u * cross + 2.0 * v * side - v * pull - w * p2
        height, down, across = (grid.get(kept, k, col) for k in (H, Q1, Q2))
        _, u, v = velocities(height, down, across)
        _, dry, turb = friction(height, u, v, grid.get(kept, FA, col), grid.get(kept, FB, col))
        start = dt0 * (u * f1 + v * f2)
        mu = grid.get(total, 0, col) + grid.get(smooth, 0, col - TILE)
        xi = grid.get(total, 1, col) + grid.get(smooth, 1, col - TILE)
        grid.put(total, 0, col, mu - grid.get(at_one, CE, col) * along - dry * start)
        grid.put(total, 1, col, xi + grid.get(at_one, CB, col) * along + turb * start)

    grid.sweep_own(early)

    cols = out_mu.shape[1]
    for g in range(grid.groups):
        at = pl.ds(g * LANES, LANES)
        out_mu[at, :] = total[0, g, TILE : TILE + cols, :].T
        out_xi[at, :] = total[1, g, TILE : TILE + cols, :].T


VMEM = pl.BlockSpec(memory_space=pltpu.VMEM)
ANY = pl.BlockSpec(memory_space=pltpu.HBM)


def call(body, name, operands, outs, scratch, flops, spaces=None, aliases=None):
    outs = [jax.ShapeDtypeStruct(shape, jnp.float32) for shape in outs]
    moved = 4 * sum(x.size for x in operands) + 4 * sum(x.size for x in outs)
    return pl.pallas_call(
        body,
        name=name,
        out_shape=outs,
        in_specs=spaces or [VMEM] * len(operands),
        out_specs=[VMEM] * len(outs),
        scratch_shapes=[pltpu.VMEM(x, jnp.float32) if isinstance(x, tuple) else x for x in scratch],
        input_output_aliases=aliases or {},
        compiler_params=pltpu.CompilerParams(vmem_limit_bytes=24 * 1024 * 1024),
        cost_estimate=pl.CostEstimate(flops=flops, bytes_accessed=moved, transcendentals=0),
    )(*operands)


def swap(value, other):
    count = lax.axis_size("cross")
    return lax.ppermute(value, "cross", [(i, other(i) % count) for i in range(count)])


def other_core(i):
    return i ^ 1


def next_chip(i):
    return i - 1 if i % 2 == 0 else i + 1


def other_chip(step):
    return lambda i: i ^ (step + 1)


def max_and_sum(a, b):
    return jnp.where(lax.broadcasted_iota(jnp.int32, a.shape, 0) == 0, jnp.maximum(a, b), a + b)


def round_beside(row, other, result=None):
    arrived = swap(row, other)
    if result is not None:
        arrived, result = lax.optimization_barrier((arrived, result))
    return max_and_sum(row, arrived), result


def local(state, log_mu, log_xi, dir_mu, dir_xi, wet, observed, terrain, class_weight):
    rows, cols = log_mu.shape
    groups = rows // LANES
    count = lax.axis_size("cross")
    own = (groups, cols, LANES)
    wide = (groups, cols + 2 * TILE, LANES)
    spare = (groups, cols + 4 * TILE, LANES)
    edge = (SHARED, groups, TILE, LANES)
    work = rows * cols

    inputs = (state, log_mu, log_xi, dir_mu, dir_xi, wet, observed, terrain, class_weight)
    inputs = tuple(pltpu.with_memory_space_constraint(x, pltpu.HBM) for x in inputs)
    (row,) = call(
        first_speed,
        "first_speed",
        inputs[:1],
        [(1, LANES)],
        [pltpu.VMEM((4, 3, rows // 4, cols), jnp.float32), pltpu.SemaphoreType.DMA((4,))],
        20 * work,
        spaces=[ANY],
    )
    row = jnp.maximum(row, swap(row, other_core))
    kept, weights, edge_a, edge_b, count_row = call(
        prepare,
        "prepare",
        inputs + (row,),
        [(KEPT,) + wide, (1,) + wide, edge, edge, (1, LANES)],
        [(rows, cols), (3,) + own]
        + [pltpu.VMEM(x.shape, x.dtype) for x in inputs[:-1]]
        + [pltpu.SMEM(class_weight.shape, jnp.float32), pltpu.SemaphoreType.DMA((len(inputs),))],
        100 * work,
        spaces=[ANY] * len(inputs) + [VMEM],
    )
    steps = [2**k for k in range(1, count.bit_length() - 1)]
    edge_a = swap(edge_a, other_core)
    row = jnp.maximum(row, swap(row, other_chip(steps[0])))
    row, edge_b = lax.optimization_barrier((row, edge_b))
    edge_b = swap(edge_b, next_chip)
    for step in steps[1:-1]:
        row = jnp.maximum(row, swap(row, other_chip(step)))
    kept, weights, xy, change = call(
        open_step,
        "open_step",
        (kept, weights, edge_a, edge_b),
        [(KEPT,) + wide, (1,) + wide, (6,) + wide, (2,) + wide],
        [(5,) + spare],
        100 * work,
        aliases={0: 0, 1: 1},
    )
    top, last = row, swap(row, other_chip(steps[-1]))
    at_one, mid, row = call(
        middle,
        "middle",
        (top, last, kept, xy, count_row),
        [(6,) + wide, (3,) + wide, (2, LANES)],
        [(5,) + spare],
        120 * work,
    )
    (smooth,) = call(regularize, "regularize", (kept, weights), [(2,) + own], [(4,) + spare], 30 * work)
    row, smooth = round_beside(row, other_core, smooth)
    one, part = call(
        tangent_one, "tangent_one", (top, last, kept, change, at_one), [(4,) + spare, (3,) + wide], [], 60 * work
    )
    row, one = round_beside(row, other_chip(steps[0]), one)
    part, at_mid, between = call(
        tangent_mid,
        "tangent_mid",
        (top, last, kept, mid, one, part),
        [(6,) + wide, (9,) + wide, (5,) + spare],
        [],
        120 * work,
    )
    row, part = round_beside(row, other_chip(steps[1]), part)
    for step in steps[2:-1]:
        row, _ = round_beside(row, other_chip(step))
    (tan,) = call(tangent_end, "tangent_end", (part, between), [(6,) + spare], [], 30 * work)
    return call(
        functools.partial(finish, float(rows * cols * count)),
        "finish",
        (top, last, row, swap(row, other_chip(steps[-1])), kept, at_one, at_mid, between, tan, smooth),
        [(rows, cols), (rows, cols)],
        [(7,) + spare, (2,) + wide],
        300 * work,
    )


def solution(mesh):
    return jax.shard_map(
        local,
        mesh=mesh,
        in_specs=(
            P(None, "grp", "cross"),
            P("grp", "cross"),
            P("grp", "cross"),
            P("grp", "cross"),
            P("grp", "cross"),
            P("grp", "cross"),
            P("grp", "cross"),
            P("grp", "cross"),
            P(),
        ),
        out_specs=(P("grp", "cross"), P("grp", "cross")),
        check_vma=False,
    )
```
